128 devices in a mesh: dp: 16 (over z, x_lo, core), ctx: 8 (over y, x_hi).
Axes of the slice: x: 4 (x_hi: 2, x_lo: 2; x = x_hi * 2 + x_lo), y: 4, z: 4, core: 2. Of those that a mesh axis runs over, the one named last changes fastest.
Arguments:
- loader_rows: bfloat16 [32768, 512], P(('dp', 'ctx')), may hold values from -60 to 60
- send_slot: int32 [32768], P(('dp', 'ctx')), may hold values from 0 to 383, as said below
- arrive_slot: int32 [32768], P(('dp', 'ctx')), may hold values from 0 to 383, as said below
- user_lengths: int32 [16, 4], P('dp'), may hold values from 1 to 1280, 2048 in all within a row
- proj_weight: bfloat16 [512, 2048], replicated, may hold values from -0.25 to 0.25
- out_weight: bfloat16 [512, 512], replicated, may hold values from -0.25 to 0.25
- cotangent: bfloat16 [32768, 512], P(('dp', 'ctx')), may hold values from -6 to 6
Outputs:
- layer_out: bfloat16 [32768, 512], P(('dp', 'ctx'))
- row_grads: bfloat16 [32768, 512], P(('dp', 'ctx'))
- proj_grad: float32 [512, 2048], replicated
- out_grad: float32 [512, 512], replicated
The draws below stay inside these ranges and needn't reach their ends.
Inputs may be any that keep to these rules, and one draw needn't show every extreme that they name: `send_slot`: on each loader device its 256 entries are distinct slots d * 3 + k, d the owner device and k counting that owner's rows from this loader from 0; no loader sends more than 3 rows to one owner and some pairs send exactly 3; the number of rows from loader s to owner d depends only on (d - s) mod (16 * 8). `arrive_slot`: on each owner device its 256 entries are distinct slots s * 3 + k, the k-th row that loader s sends to it; every owner receives exactly 256 rows.
All inputs are finite; a program needn't handle non-finite values.
Results may differ from the reference program's by a relative error of at most 0.009.
Values may be sent and summed in bfloat16 or wider, within the bound.
A program may use at most 128 MiB of HBM per device.

```python
import math
import jax
import jax.numpy as jnp
import numpy as np
from jax import lax

D = 512
HEADS = 8
TOK_DEV = 256
USERS = 4
GROUP_ROWS = 2048
LONGEST = 1280
GROUPS = 16
ALL_ROWS = 32768
CAP = 3
N_DP = 16
N_CTX = 8


def packing_tables(key):
    device_count = N_DP * N_CTX
    per_pair = TOK_DEV // device_count
    spread = max(1, per_pair // 2)
    capacity = per_pair + spread
    base = jax.random.fold_in(key, 71)
    shuffled = jax.random.permutation(jax.random.fold_in(base, 1), device_count).astype(jnp.int32) + 3
    distance = jnp.arange(device_count, dtype=jnp.int32)
    priority = jnp.where(distance == 1, 0, jnp.where(distance == device_count // 2, 1, jnp.where(distance == device_count - 1, 2, shuffled)))
    order = jnp.argsort(jnp.argsort(priority, stable=True), stable=True)
    offset_of = jnp.where(order < device_count // 2, spread, -spread).astype(jnp.int32)
    source_ids = jnp.arange(device_count, dtype=jnp.int32)[:, None]
    target_ids = jnp.arange(device_count, dtype=jnp.int32)[None, :]
    counts = per_pair + offset_of[(target_ids - source_ids) % device_count]
    send_start = jnp.cumsum(counts, axis=1) - counts
    send_keys = jax.random.split(jax.random.fold_in(base, 2), device_count)
    send_order = jax.vmap(lambda each: jax.random.permutation(each, TOK_DEV))(send_keys).astype(jnp.int32)
    send_ends = send_start + counts
    target = jnp.sum((send_ends[:, None, :] <= send_order[:, :, None]).astype(jnp.int32), axis=2)
    send_within = send_order - jnp.take_along_axis(send_start, target, axis=1)
    send_slot = (target * capacity + send_within).reshape(-1).astype(jnp.int32)
    arrive_start = (jnp.cumsum(counts, axis=0) - counts).T
    arrive_keys = jax.random.split(jax.random.fold_in(base, 3), device_count)
    arrive_order = jax.vmap(lambda each: jax.random.permutation(each, TOK_DEV))(arrive_keys).astype(jnp.int32)
    arrive_ends = arrive_start + counts.T
    source = jnp.sum((arrive_ends[:, None, :] <= arrive_order[:, :, None]).astype(jnp.int32), axis=2)
    arrive_within = arrive_order - jnp.take_along_axis(arrive_start, source, axis=1)
    arrive_slot = (source * capacity + arrive_within).reshape(-1).astype(jnp.int32)
    return (send_slot, arrive_slot)


def draw_send_slot(key, part):
    return packing_tables(key)[0]


def draw_arrive_slot(key, part):
    return packing_tables(key)[1]


def draw_loader_rows(key, part):
    row_total = N_DP * N_CTX * TOK_DEV
    first, second, third = jax.random.split(jax.random.fold_in(key, 5), 3)
    values = jnp.clip(jax.random.normal(first, (row_total, D), jnp.float32), -4.0, 4.0)
    row_scale = 0.5 * jnp.exp(jax.random.uniform(second, (row_total, 1), jnp.float32, 0.0, math.log(10.0)))
    col_scale = 0.3 * jnp.exp(jax.random.uniform(third, (1, D), jnp.float32, 0.0, math.log(10.0)))
    result = values * row_scale * col_scale
    return result.astype(jnp.bfloat16)


def draw_cotangent(key, part):
    row_total = N_DP * N_CTX * TOK_DEV
    first = jax.random.fold_in(jax.random.fold_in(key, 9), 0)
    result = jnp.clip(jax.random.normal(first, (row_total, D), jnp.float32), -4.0, 4.0)
    return result.astype(jnp.bfloat16)


def profile(amount, total, limit, lean):
    portions = [(1 << 20) // math.isqrt(grade ** lean) + 1 for grade in range(2, amount + 1)]
    rest, given = total - limit - (amount - 1), [1] * (amount - 1)
    while rest > 0:
        candidates = [i for i in range(amount - 1) if given[i] < limit]
        mass, left = sum([portions[i] for i in candidates]), rest
        for i in candidates:
            more = min(limit - given[i], max(1, left * portions[i] // mass), rest)
            given[i] = given[i] + more
            rest = rest - more
    return np.array([limit] + given)


def ragged_sizes(own_key, number_of, total, bound, lean):
    if number_of == 2:
        one = jax.random.randint(own_key, (), max(1, total - bound), min(bound, total - 1) + 1)
        return jnp.stack([one, total - one])
    sizes = jnp.asarray(profile(number_of, total, bound, lean), jnp.int32)
    pairs = (number_of - 1) // 2
    giver, sink = sizes[1:1 + 2 * pairs:2], sizes[2:2 + 2 * pairs:2]
    margin = jnp.minimum(giver - 1, bound - sink)
    passed = jax.random.randint(jax.random.fold_in(own_key, 1), (pairs,), 0, 1 << 20) % (margin + 1)
    sizes = sizes.at[1:1 + 2 * pairs:2].set(giver - passed).at[2:2 + 2 * pairs:2].set(sink + passed)
    return sizes[jax.random.permutation(jax.random.fold_in(own_key, 2), number_of)]


def normal_values(rng, shape, scale, reach, held_as=jnp.bfloat16):
    array = jax.random.normal(rng, shape, jnp.float32) * scale
    return jnp.minimum(jnp.maximum(array, -reach), reach).astype(held_as)


def setup_inputs(seed: int = 0) -> dict:
    keys = jax.random.split(jax.random.key(seed), 8)
    loader_rows = draw_loader_rows(jax.random.fold_in(keys[7], 71), 0)
    send_slot = draw_send_slot(jax.random.fold_in(keys[7], 71), 0)
    arrive_slot = draw_arrive_slot(jax.random.fold_in(keys[7], 71), 0)
    user_lengths = jax.vmap(lambda own: ragged_sizes(own, USERS, GROUP_ROWS, LONGEST, 2))(jax.random.split(keys[3], GROUPS)).reshape((GROUPS, USERS)).astype(jnp.int32)
    proj_weight = normal_values(keys[4], (D, 4 * D), D ** -0.5, 0.25)
    out_weight = normal_values(keys[5], (D, D), D ** -0.5, 0.25)
    cotangent = draw_cotangent(jax.random.fold_in(keys[7], 71), 0)
    return dict(loader_rows=loader_rows, send_slot=send_slot, arrive_slot=arrive_slot, user_lengths=user_lengths, proj_weight=proj_weight, out_weight=out_weight, cotangent=cotangent)


norm_eps = 1e-05

def normalize(values):
    centre = values - lax.optimization_barrier(jnp.mean(values, axis=-1, keepdims=True))
    inverse = lax.rsqrt(lax.optimization_barrier(jnp.mean(centre * centre, axis=-1, keepdims=True)) + norm_eps)
    return (centre * inverse, inverse)

def normalize_back(grad_in, normed, inverse):
    mean_grad = lax.optimization_barrier(jnp.mean(grad_in, axis=-1, keepdims=True))
    mean_cross = lax.optimization_barrier(jnp.mean(grad_in * normed, axis=-1, keepdims=True))
    return (grad_in - mean_grad - normed * mean_cross) * inverse

def silu_grad(values):
    sigma = jax.nn.sigmoid(values)
    return sigma * (1.0 + values * (1.0 - sigma))

def owner_rows(loader_rows, send_slot, arrive_slot):
    device_count = N_DP * N_CTX
    row_ids = jnp.arange(device_count * TOK_DEV, dtype=jnp.int32)
    home = (row_ids // TOK_DEV).astype(jnp.int32)
    within = (row_ids % TOK_DEV).astype(jnp.int32)
    table = jnp.zeros((device_count, device_count * CAP), jnp.int32).at[home, send_slot].set(within)
    source = (arrive_slot // CAP).astype(jnp.int32)
    place = (arrive_slot % CAP).astype(jnp.int32)
    picked = table[source, home * CAP + place]
    return loader_rows[source * TOK_DEV + picked]

def reference(loader_rows, send_slot, arrive_slot, user_lengths, proj_weight, out_weight, cotangent):
    owned = owner_rows(loader_rows, send_slot, arrive_slot).reshape(N_DP, GROUP_ROWS, D)
    cot_groups = cotangent.reshape(N_DP, GROUP_ROWS, D)
    head_dim = D // HEADS
    score_scale = head_dim ** (-0.5)
    row_index = jnp.arange(GROUP_ROWS, dtype=jnp.int32)
    half_rows = TOK_DEV // 2
    device_of = (row_index // TOK_DEV).astype(jnp.int32)
    local_of = (row_index % TOK_DEV).astype(jnp.int32)
    positions = jnp.where(local_of < half_rows, device_of * half_rows + local_of, GROUP_ROWS - (device_of + 1) * half_rows + (local_of - half_rows)).astype(jnp.int32)

    def split_heads(values):
        return values.reshape(GROUP_ROWS, HEADS, head_dim).transpose(1, 0, 2)

    def merge_heads(values):
        return values.transpose(1, 0, 2).reshape(GROUP_ROWS, D)

    def one_group(carry, inputs):
        rows, cot_rows, lengths = inputs
        ends = jnp.cumsum(lengths)
        users = lax.optimization_barrier(jnp.sum((ends[None, :] <= positions[:, None]).astype(jnp.int32), axis=1))
        allowed = (positions[None, :] <= positions[:, None]) & (users[:, None] == users[None, :])
        rows_f = rows.astype(jnp.float32)
        normed, inverse_in = normalize(rows_f)
        normed_bf = normed.astype(jnp.bfloat16)
        pre = jnp.dot(normed_bf, proj_weight, preferred_element_type=jnp.float32)
        proj = (pre * jax.nn.sigmoid(pre)).astype(jnp.bfloat16)
        update_rows = proj[:, :D]
        value_rows = proj[:, D:2 * D]
        query_rows = proj[:, 2 * D:3 * D]
        key_rows = proj[:, 3 * D:]
        heads_query = split_heads(query_rows)
        heads_key = split_heads(key_rows)
        heads_value = split_heads(value_rows)

        def head_forward(items):
            query_h, key_h, value_h = items
            scores = jnp.dot(query_h, key_h.T, preferred_element_type=jnp.float32) * score_scale
            weights = jnp.where(allowed, scores * jax.nn.sigmoid(scores), 0.0).astype(jnp.bfloat16)
            return jnp.dot(weights, value_h, preferred_element_type=jnp.float32)
        attended = merge_heads(lax.map(head_forward, (heads_query, heads_key, heads_value)))
        att_normed, inverse_att = normalize(attended)
        update_f = update_rows.astype(jnp.float32)
        gated = (att_normed * update_f).astype(jnp.bfloat16)
        layer_rows = (rows_f + jnp.dot(gated, out_weight, preferred_element_type=jnp.float32)).astype(jnp.bfloat16)
        out_term = jnp.dot(gated.T, cot_rows, preferred_element_type=jnp.float32)
        grad_gated = jnp.dot(cot_rows, out_weight.T, preferred_element_type=jnp.float32)
        grad_update = grad_gated * att_normed
        grad_att = normalize_back(grad_gated * update_f, att_normed, inverse_att).astype(jnp.bfloat16)

        def head_backward(items):
            query_h, key_h, value_h, grad_h = items
            scores = jnp.dot(query_h, key_h.T, preferred_element_type=jnp.float32) * score_scale
            weights = jnp.where(allowed, scores * jax.nn.sigmoid(scores), 0.0).astype(jnp.bfloat16)
            grad_weights = jnp.dot(grad_h, value_h.T, preferred_element_type=jnp.float32)
            grad_scores = jnp.where(allowed, grad_weights * silu_grad(scores) * score_scale, 0.0).astype(jnp.bfloat16)
            grad_q = jnp.dot(grad_scores, key_h, preferred_element_type=jnp.float32)
            grad_k = jnp.dot(grad_scores.T, query_h, preferred_element_type=jnp.float32)
            grad_v = jnp.dot(weights.T, grad_h, preferred_element_type=jnp.float32)
            return (grad_q, grad_k, grad_v)
        grad_q, grad_k, grad_v = lax.map(head_backward, (heads_query, heads_key, heads_value, split_heads(grad_att)))
        grad_proj = jnp.concatenate([grad_update, merge_heads(grad_v), merge_heads(grad_q), merge_heads(grad_k)], axis=1)
        grad_pre = (grad_proj * silu_grad(pre)).astype(jnp.bfloat16)
        proj_term = jnp.dot(normed_bf.T, grad_pre, preferred_element_type=jnp.float32)
        grad_normed = jnp.dot(grad_pre, proj_weight.T, preferred_element_type=jnp.float32)
        row_grads = (cot_rows.astype(jnp.float32) + normalize_back(grad_normed, normed, inverse_in)).astype(jnp.bfloat16)
        return ((carry[0] + proj_term, carry[1] + out_term), (layer_rows, row_grads))
    start_carry = (jnp.zeros((D, 4 * D), jnp.float32), jnp.zeros((D, D), jnp.float32))
    sums, outputs = lax.scan(one_group, start_carry, (owned, cot_groups, user_lengths))
    grad_scale = ALL_ROWS ** (-0.5)
    layer_out = outputs[0].reshape(ALL_ROWS, D)
    row_grads = outputs[1].reshape(ALL_ROWS, D)
    return (layer_out, row_grads, sums[0] * grad_scale, sums[1] * grad_scale)
```

```python
import functools

import jax
import jax.numpy as jnp
from jax import lax
from jax.experimental import pallas as pl
from jax.experimental.pallas import tpu as pltpu
from jax.sharding import PartitionSpec as P

MESH = pl.DeviceIdType.MESH
F32 = jnp.float32
BF16 = jnp.bfloat16
norm_eps = 1e-05
VMEM_LIMIT = 48 * 2**20

NCTX = 8
HALF = 128
BLK = 256
NB = 8
WIDTH = 512
HD = 64
EVENTS = 2048
TILES = 640
UNITS = 5
ORDERS = ("zxy", "zxy", "xyz", "xyz", "yzx")


def normalize(values):
    centre = values - jnp.mean(values, axis=-1, keepdims=True)
    inverse = lax.rsqrt(jnp.mean(centre * centre, axis=-1, keepdims=True) + norm_eps)
    return (centre * inverse, inverse)


def normalize_back(grad_in, normed, inverse):
    mean_grad = jnp.mean(grad_in, axis=-1, keepdims=True)
    mean_cross = jnp.mean(grad_in * normed, axis=-1, keepdims=True)
    return (grad_in - mean_grad - normed * mean_cross) * inverse


def silu(z):
    h = 0.5 * z
    return h + h * jnp.tanh(h)


def silu_grad(z):
    h = 0.5 * z
    u = 1.0 + jnp.tanh(h)
    return 0.5 * (u + h * u * (2.0 - u))


def dot(a, b):
    return lax.dot_general(a, b, (((1,), (0,)), ((), ())), preferred_element_type=F32)


def dot_nt(a, b):
    return lax.dot_general(a, b, (((1,), (1,)), ((), ())), preferred_element_type=F32)


def low(a, b):
    return jnp.concatenate([a[:, :HD], b[:, :HD]], axis=1)


def high(a, b):
    return jnp.concatenate([a[:, HD:], b[:, HD:]], axis=1)


def mod(a, n):
    return lax.rem(a + n, n)


def third(a):
    return (a * 21846) >> 16


def ctx_barrier():
    cx = lax.axis_index("ctx")
    dp = lax.axis_index("dp")
    sem = pltpu.get_barrier_semaphore()
    for rel in range(1, NCTX):
        pl.semaphore_signal(
            sem, inc=1, device_id=(dp, lax.rem(cx + rel, NCTX)), device_id_type=MESH
        )
    pl.semaphore_wait(sem, NCTX - 1)


def arrive_kernel(
    rows_ref, sslot_ref, aslot_ref, w_ref,
    own_ref, normed_ref, upd_ref, qk_ref, v_ref,
    out, recv, qk_msg, v_msg, row_sems, send_sems, recv_sems, local_sems,
):
    dp, cx = lax.axis_index("dp"), lax.axis_index("ctx")
    me = dp * NCTX + cx
    ndev = 128

    rows = rows_ref[...]
    rows4 = jnp.concatenate([rows[:, q * 128 : q * 128 + 128] for q in range(4)], axis=0)
    slot = sslot_ref[...]
    to = third(slot)
    place = ((to - me) & (ndev - 1)) * 16 + (slot - 3 * to)
    target = jnp.concatenate([place + 4 * q for q in range(4)], axis=1)
    seen = lax.broadcasted_iota(jnp.int32, (BLK, 1024), 0)

    def pack(n, carry):
        hot = jnp.where(seen == target - n * BLK, 1.0, 0.0).astype(BF16)
        part = dot(hot, rows4).astype(BF16)
        out[pl.ds(n * 16, 16)] = part.reshape(16, 16, 128)

        def send(rel, carry):
            @pl.when(rel > 0)
            def _():
                d = lax.rem(me + rel, ndev)
                pltpu.make_async_remote_copy(
                    src_ref=out.at[rel],
                    dst_ref=recv.at[rel],
                    send_sem=row_sems.at[0],
                    recv_sem=row_sems.at[1],
                    device_id=(d // NCTX, lax.rem(d, NCTX)),
                    device_id_type=MESH,
                ).start()

            return carry

        return lax.fori_loop(n * 16, n * 16 + 16, send, carry)

    lax.fori_loop(0, 8, pack, 0)
    recv[0] = out[0]
    all_rows = pltpu.make_async_remote_copy(
        src_ref=out.at[pl.ds(1, ndev - 1)],
        dst_ref=recv.at[pl.ds(1, ndev - 1)],
        send_sem=row_sems.at[0],
        recv_sem=row_sems.at[1],
        device_id=(dp, cx),
        device_id_type=MESH,
    )
    aslot = jnp.transpose(jnp.broadcast_to(aslot_ref[...], (128, BLK)))[:, :1]
    come = third(aslot)
    picked = ((me - come) & (ndev - 1)) * 16 + (aslot - 3 * come)
    lanes = lax.broadcasted_iota(jnp.int32, (BLK, EVENTS), 1)
    all_rows.wait()

    got = recv[...].reshape(EVENTS, 128)
    own = jnp.concatenate(
        [
            dot(jnp.where(lanes == picked + 4 * q, 1.0, 0.0).astype(BF16), got)
            for q in range(4)
        ],
        axis=1,
    )
    own_ref[...] = own.astype(BF16)
    normed = normalize(own)[0].astype(BF16)
    normed_ref[...] = normed

    query = (silu(dot(normed, w_ref[:, 1024:1536])).astype(BF16).astype(F32) * 0.0625).astype(BF16)
    key = silu(dot(normed, w_ref[:, 1536:2048])).astype(BF16)
    for a in range(4):
        x, y = query[:, a * 128 : a * 128 + 128], key[:, a * 128 : a * 128 + 128]
        qk_msg[2 * a] = low(x, y).reshape(2, HALF, 128)
        qk_msg[2 * a + 1] = high(x, y).reshape(2, HALF, 128)

    def to_head(peer, rel, n):
        if n < 2:
            src, dst = qk_msg.at[peer, n], qk_ref.at[cx if n == 0 else 15 - cx]
        else:
            src, dst = v_msg.at[peer], v_ref.at[cx]
        if rel == 0:
            return pltpu.make_async_copy(src, dst, local_sems.at[n])
        return pltpu.make_async_remote_copy(
            src_ref=src,
            dst_ref=dst,
            send_sem=send_sems.at[rel, n],
            recv_sem=recv_sems.at[rel, n],
            device_id=(dp, peer),
            device_id_type=MESH,
        )

    copies = []
    for rel in range(NCTX):
        peer = lax.rem(cx + rel, NCTX)
        for n in range(2):
            copies.append(to_head(peer, rel, n))
            copies[-1].start()

    value = silu(dot(normed, w_ref[:, 512:1024])).astype(BF16)
    for a in range(4):
        x = value[:HALF, a * 128 : a * 128 + 128]
        y = value[HALF:, a * 128 : a * 128 + 128]
        v_msg[2 * a] = low(x, y)
        v_msg[2 * a + 1] = high(x, y)
    for rel in range(NCTX):
        copies.append(to_head(lax.rem(cx + rel, NCTX), rel, 2))
        copies[-1].start()

    upd_ref[...] = silu(dot(normed, w_ref[:, :512])).astype(BF16)
    for copy in copies:
        copy.wait()


def timeline_ends(len_ref):
    ends, total = [], 0
    for n in range(4):
        total = total + len_ref[0, n]
        ends.append(total)
    return ends


def start_of(positions, ends):
    first = jnp.zeros_like(positions)
    for n in range(3):
        first = jnp.where(positions >= ends[n], ends[n], first)
    return first


def end_of(position, ends):
    last = ends[3]
    for n in (2, 1, 0):
        last = jnp.where(position < ends[n], ends[n], last)
    return last


def in_position_order(packed, dst):
    for c in range(NCTX):
        block = packed[c]
        dst[c * HALF : (c + 1) * HALF, :] = block[:, :HD]
        dst[(15 - c) * HALF : (16 - c) * HALF, :] = block[:, HD:]


def forward_kernel(len_ref, qk_ref, v_ref, att_ref, q, kt, v, att):
    ends = timeline_ends(len_ref)
    qk = qk_ref[...].reshape(EVENTS, 128)
    q[...] = qk[:, :HD]
    kt[...] = jnp.transpose(qk)[HD:, :]
    in_position_order(v_ref, v)

    for i in range(NB):
        row = i * BLK + lax.broadcasted_iota(jnp.int32, (BLK, 1), 0)
        first = start_of(row, ends)
        q_i = q[i * BLK : (i + 1) * BLK, :]

        def block(j, acc):
            at = pl.multiple_of(j * BLK, BLK)
            h = dot(q_i, kt[:, pl.ds(at, BLK)])
            w = h + h * jnp.tanh(h)
            t = at + lax.broadcasted_iota(jnp.int32, (BLK, BLK), 1)
            w = jnp.where((t >= first) & (t <= row), w, 0.0).astype(BF16)
            return acc + dot(w, v[pl.ds(at, BLK), :])

        lowest = start_of(jnp.int32(i * BLK), ends) >> 8
        att[i * BLK : (i + 1) * BLK, :] = lax.fori_loop(
            lowest, i + 1, block, jnp.zeros((BLK, HD), F32)
        ).astype(BF16)

    for c in range(NCTX):
        att_ref[c] = jnp.concatenate(
            [att[c * HALF : (c + 1) * HALF, :], att[(15 - c) * HALF : (16 - c) * HALF, :]], axis=1
        )


def backward_kernel(
    len_ref, qk_ref, v_ref, ga_ref, g_ref, q, qt, k, kt, v, ga, gat, gqt, gk, gv
):
    ends = timeline_ends(len_ref)
    qk = qk_ref[...].reshape(EVENTS, 128)
    q[...] = qk[:, :HD]
    k[...] = qk[:, HD:]
    qkt = jnp.transpose(qk)
    qt[...] = qkt[:HD]
    kt[...] = qkt[HD:]
    in_position_order(v_ref, v)
    in_position_order(ga_ref, ga)
    gat[...] = jnp.transpose(ga[...])
    gqt[...] = jnp.zeros_like(gqt)

    for j in range(NB):
        t = j * BLK + lax.broadcasted_iota(jnp.int32, (BLK, 1), 0)
        keys = slice(j * BLK, (j + 1) * BLK)
        k_j, kt_j, v_j = k[keys, :], kt[:, keys], v[keys, :]

        def block(i, carry):
            gk_j, gv_j = carry
            at = pl.multiple_of(i * BLK, BLK)
            rows = pl.ds(at, BLK)
            h = dot(k_j, qt[:, rows])
            u = 1.0 + jnp.tanh(h)
            w = h * u
            e = dot(v_j, gat[:, rows]) * (u + w * (2.0 - u))
            p = at + lax.broadcasted_iota(jnp.int32, (1, BLK), 1)
            ok = (t >= start_of(p, ends)) & (t <= p)
            w = jnp.where(ok, w, 0.0).astype(BF16)
            e = jnp.where(ok, e, 0.0).astype(BF16)
            gqt[:, rows] += dot(kt_j, e)
            return gk_j + dot(e, q[rows, :]), gv_j + dot(w, ga[rows, :])

        zero = jnp.zeros((BLK, HD), F32)
        highest = (end_of(jnp.int32(j * BLK + BLK - 1), ends) - 1) >> 8
        gk_j, gv_j = lax.fori_loop(j, highest + 1, block, (zero, zero))
        gk[keys, :] = gk_j.astype(BF16)
        gv[keys, :] = gv_j.astype(BF16)

    gq = jnp.transpose(gqt[...] * 0.0625).astype(BF16)
    for c in range(NCTX):
        a = slice(c * HALF, (c + 1) * HALF)
        b = slice((15 - c) * HALF, (16 - c) * HALF)
        g_ref[c, 0] = jnp.concatenate([gv[a, :], gv[b, :]], axis=1)
        g_ref[c, 1] = jnp.concatenate([gq[a, :], gq[b, :]], axis=1)
        g_ref[c, 2] = jnp.concatenate([gk[a, :], gk[b, :]], axis=1)


def exchange(src, dst, sems, base=0):
    dp, cx = lax.axis_index("dp"), lax.axis_index("ctx")
    copies = []
    for rel in range(NCTX):
        peer = lax.rem(cx + rel, NCTX)
        if rel == 0:
            copy = pltpu.make_async_copy(src.at[peer], dst.at[cx], sems.at[base])
        else:
            copy = pltpu.make_async_remote_copy(
                src_ref=src.at[peer],
                dst_ref=dst.at[cx],
                send_sem=sems.at[base + rel],
                recv_sem=sems.at[base + NCTX + rel],
                device_id=(dp, peer),
                device_id_type=MESH,
            )
        copy.start()
        copies.append(copy)
    return copies


def gather_heads(parts):
    first = [low(parts[2 * a], parts[2 * a + 1]) for a in range(4)]
    second = [high(parts[2 * a], parts[2 * a + 1]) for a in range(4)]
    return jnp.concatenate(
        [jnp.concatenate(first, axis=1), jnp.concatenate(second, axis=1)], axis=0
    )


def middle_kernel(
    att_ref, own_ref, upd_ref, cot_ref, wo_ref,
    layer_ref, gu_ref, outterm_ref, ga_ref,
    att_in, ga_msg, sems,
):
    ctx_barrier()
    copies = exchange(att_ref, att_in, sems)
    cot = cot_ref[...]
    wo = wo_ref[...]
    grad_gated = dot_nt(cot, wo)
    update = upd_ref[...].astype(F32)
    for copy in copies:
        copy.wait()
    attended = gather_heads([att_in[h].astype(F32) for h in range(NCTX)])
    att_normed, inverse = normalize(attended)
    grad_att = normalize_back(grad_gated * update, att_normed, inverse).astype(BF16)
    for a in range(4):
        x = grad_att[:HALF, a * 128 : a * 128 + 128]
        y = grad_att[HALF:, a * 128 : a * 128 + 128]
        ga_msg[2 * a] = low(x, y)
        ga_msg[2 * a + 1] = high(x, y)
    copies = exchange(ga_msg, ga_ref, sems, 2 * NCTX)
    gated = (att_normed * update).astype(BF16)
    layer_ref[...] = (own_ref[...].astype(F32) + dot(gated, wo)).astype(BF16)
    outterm_ref[...] = dot(jnp.transpose(gated), cot)
    gu_ref[...] = grad_gated * att_normed
    for copy in copies:
        copy.wait()


def final_kernel(
    g_ref, own_ref, normed_ref, w_ref, cot_ref, gu_ref, outterm_ref,
    rowgrad_ref, sum_ref,
    g_in, mine, first_in, b1, in1, b2, in2, in3, sems, core_sems, axis_sems,
):
    dp, cx = lax.axis_index("dp"), lax.axis_index("ctx")
    core, xlo, z = lax.rem(dp, 2), lax.rem(dp // 2, 2), dp // 4
    xhi, y = lax.rem(cx, 2), cx // 2
    place = {"x": xhi * 2 + xlo, "y": y, "z": z}
    sibling = (dp + 1 - 2 * core, cx)

    def along(axis, r):
        c = lax.rem(place[axis] + r, 4)
        if axis == "x":
            return c, (z * 4 + lax.rem(c, 2) * 2 + core, y * 2 + c // 2)
        if axis == "y":
            return c, (dp, c * 2 + xhi)
        return c, (c * 4 + xlo * 2 + core, cx)

    barrier = pltpu.get_barrier_semaphore()
    for rel in range(1, NCTX):
        pl.semaphore_signal(
            barrier, inc=1, device_id=(dp, lax.rem(cx + rel, NCTX)), device_id_type=MESH
        )
    for device in [sibling] + [along(axis, r)[1] for axis in "xyz" for r in (1, 2, 3)]:
        pl.semaphore_signal(barrier, inc=1, device_id=device, device_id_type=MESH)
    pl.semaphore_wait(barrier, NCTX - 1 + 10)

    def remote(src, dst, send_sem, recv_sem, device):
        copy = pltpu.make_async_remote_copy(
            src_ref=src, dst_ref=dst, send_sem=send_sem, recv_sem=recv_sem,
            device_id=device, device_id_type=MESH,
        )
        copy.start()
        return copy

    copies = exchange(g_ref, g_in, sems)

    own, cot = own_ref[...].astype(F32), cot_ref[...]
    normed, inverse = normalize(own)
    normed_bf = normed_ref[...]
    normed_t = jnp.transpose(normed_bf)

    def put(block, term):
        term = term.astype(BF16)
        for n in range(4):
            mine[pl.ds((block * 4 + n) * 32, 32)] = term[:, n * 128 : n * 128 + 128].reshape(
                32, 16, 128
            )

    grad_normed = jnp.zeros((BLK, WIDTH), F32)

    def block_grads(block, grad, total):
        columns = slice(block * WIDTH, (block + 1) * WIDTH)
        w = w_ref[:, columns]
        grad_pre = (grad * silu_grad(dot(normed_bf, w))).astype(BF16)
        put(block, dot(normed_t, grad_pre))
        return total + dot_nt(grad_pre, w)

    put(4, outterm_ref[...])
    grad_normed = block_grads(0, gu_ref[...], grad_normed)
    for copy in copies:
        copy.wait()
    for n in range(3):
        grad = gather_heads([g_in[h, n].astype(F32) for h in range(NCTX)])
        grad_normed = block_grads(n + 1, grad, grad_normed)

    half = UNITS * 64
    copies = [
        remote(
            mine.at[pl.ds((1 - core) * half + u * 64, 64)], first_in.at[pl.ds(u * 64, 64)],
            core_sems.at[0, u], core_sems.at[1, u], sibling,
        )
        for u in range(UNITS)
    ]
    rowgrad_ref[...] = (
        cot.astype(F32) + normalize_back(grad_normed, normed, inverse)
    ).astype(BF16)
    for copy in copies:
        copy.wait()

    def add(own_part, parts):
        total = own_part.astype(F32)
        for part in parts:
            total = total + part.astype(F32)
        return total.astype(BF16)

    for u in range(UNITS):
        at = pl.ds(u * 64, 64)
        first_in[at] = add(first_in[at], [mine[pl.ds(core * half + u * 64, 64)]])

    stages = ((first_in, 16, in1, b1), (b1, 4, in2, b2), (b2, 1, in3, None))
    base = [0] * UNITS
    for step, (src, size, landing, dst) in enumerate(stages):
        copies = []
        for u in range(UNITS):
            axis = ORDERS[u][step]
            for r in (1, 2, 3):
                c, device = along(axis, r)
                copies.append(
                    remote(
                        src.at[pl.ds((u * 4 + c) * size, size)],
                        landing.at[r - 1, pl.ds(u * size, size)],
                        axis_sems.at[0, step, u, r], axis_sems.at[1, step, u, r], device,
                    )
                )
        for copy in copies:
            copy.wait()
        for u in range(UNITS):
            c = place[ORDERS[u][step]]
            base[u] = base[u] + c * size
            total = add(
                src[pl.ds((u * 4 + c) * size, size)],
                [landing[r, pl.ds(u * size, size)] for r in range(3)],
            )
            if dst is None:
                sum_ref[pl.ds(core * half + u * 64 + base[u], size)] = total
            else:
                dst[pl.ds(u * size, size)] = total

    for step, size in ((2, 1), (1, 4), (0, 16)):
        copies = []
        for u in range(UNITS):
            axis = ORDERS[u][step]
            held = sum_ref.at[pl.ds(core * half + u * 64 + base[u], size)]
            for r in (1, 2, 3):
                copies.append(
                    remote(
                        held, held,
                        axis_sems.at[2, step, u, r], axis_sems.at[3, step, u, r], along(axis, r)[1],
                    )
                )
            base[u] = base[u] - place[axis] * size
        for copy in copies:
            copy.wait()
    copies = []
    for u in range(UNITS):
        held = sum_ref.at[pl.ds(core * half + u * 64, 64)]
        copies.append(remote(held, held, core_sems.at[2, u], core_sems.at[3, u], sibling))
    for copy in copies:
        copy.wait()


def spread_kernel(scale, sum_ref, proj_ref, out_ref):
    n = pl.program_id(0)

    def write(dst):
        for t in range(4):
            dst[:, t * 128 : t * 128 + 128] = (
                sum_ref[t * 32 : t * 32 + 32].reshape(WIDTH, 128).astype(F32) * scale
            )

    @pl.when(n < 4)
    def _():
        write(proj_ref)

    @pl.when(n == 4)
    def _():
        write(out_ref)


VM = pl.BlockSpec(memory_space=pltpu.VMEM)
SM = pl.BlockSpec(memory_space=pltpu.SMEM)


def shape(*dims, dtype=BF16):
    return jax.ShapeDtypeStruct(dims, dtype)


def params(**kw):
    return pltpu.CompilerParams(vmem_limit_bytes=VMEM_LIMIT, **kw)


def local(loader_rows, send_slot, arrive_slot, user_lengths, proj_weight, out_weight, cotangent):
    own, normed, update, qk, v = pl.pallas_call(
        arrive_kernel,
        name="arrive",
        out_shape=(
            shape(BLK, WIDTH), shape(BLK, WIDTH), shape(BLK, WIDTH),
            shape(16, HALF, 128), shape(NCTX, HALF, 128),
        ),
        in_specs=[VM] * 4,
        out_specs=(VM,) * 5,
        scratch_shapes=[
            pltpu.VMEM((128, 16, 128), BF16),
            pltpu.VMEM((128, 16, 128), BF16),
            pltpu.VMEM((NCTX, 2, HALF, 128), BF16),
            pltpu.VMEM((NCTX, HALF, 128), BF16),
            pltpu.SemaphoreType.DMA((2,)),
            pltpu.SemaphoreType.DMA((NCTX, 3)),
            pltpu.SemaphoreType.DMA((NCTX, 3)),
            pltpu.SemaphoreType.DMA((3,)),
        ],
        compiler_params=params(has_side_effects=True),
    )(loader_rows, send_slot.reshape(1, BLK), arrive_slot.reshape(1, BLK), proj_weight)

    att = pl.pallas_call(
        forward_kernel,
        name="attend",
        out_shape=shape(NCTX, HALF, 128),
        in_specs=[SM, VM, VM],
        out_specs=VM,
        scratch_shapes=[
            pltpu.VMEM((EVENTS, HD), BF16),
            pltpu.VMEM((HD, EVENTS), BF16),
            pltpu.VMEM((EVENTS, HD), BF16),
            pltpu.VMEM((EVENTS, HD), BF16),
        ],
        compiler_params=params(),
    )(user_lengths, qk, v)

    layer_out, grad_update, out_term, grad_att = pl.pallas_call(
        middle_kernel,
        name="middle",
        out_shape=(
            shape(BLK, WIDTH), shape(BLK, WIDTH, dtype=F32), shape(WIDTH, WIDTH, dtype=F32),
            shape(NCTX, HALF, 128),
        ),
        in_specs=[VM] * 5,
        out_specs=(VM,) * 4,
        scratch_shapes=[
            pltpu.VMEM((NCTX, HALF, 128), BF16),
            pltpu.VMEM((NCTX, HALF, 128), BF16),
            pltpu.SemaphoreType.DMA((4 * NCTX,)),
        ],
        compiler_params=params(collective_id=1, has_side_effects=True),
    )(att, own, update, cotangent, out_weight)

    grads = pl.pallas_call(
        backward_kernel,
        name="attend_back",
        out_shape=shape(NCTX, 3, HALF, 128),
        in_specs=[SM, VM, VM, VM],
        out_specs=VM,
        scratch_shapes=[
            pltpu.VMEM((EVENTS, HD), BF16),
            pltpu.VMEM((HD, EVENTS), BF16),
            pltpu.VMEM((EVENTS, HD), BF16),
            pltpu.VMEM((HD, EVENTS), BF16),
            pltpu.VMEM((EVENTS, HD), BF16),
            pltpu.VMEM((EVENTS, HD), BF16),
            pltpu.VMEM((HD, EVENTS), BF16),
            pltpu.VMEM((HD, EVENTS), F32),
            pltpu.VMEM((EVENTS, HD), BF16),
            pltpu.VMEM((EVENTS, HD), BF16),
        ],
        compiler_params=params(),
    )(user_lengths, qk, v, grad_att)

    row_grads, sums = pl.pallas_call(
        final_kernel,
        name="final",
        out_shape=(shape(BLK, WIDTH), shape(TILES, 16, 128)),
        in_specs=[VM] * 7,
        out_specs=(VM,) * 2,
        scratch_shapes=[
            pltpu.VMEM((NCTX, 3, HALF, 128), BF16),
            pltpu.VMEM((TILES, 16, 128), BF16),
            pltpu.VMEM((UNITS * 64, 16, 128), BF16),
            pltpu.VMEM((UNITS * 16, 16, 128), BF16),
            pltpu.VMEM((3, UNITS * 16, 16, 128), BF16),
            pltpu.VMEM((UNITS * 4, 16, 128), BF16),
            pltpu.VMEM((3, UNITS * 4, 16, 128), BF16),
            pltpu.VMEM((3, UNITS, 16, 128), BF16),
            pltpu.SemaphoreType.DMA((2 * NCTX,)),
            pltpu.SemaphoreType.DMA((4, UNITS)),
            pltpu.SemaphoreType.DMA((4, 3, UNITS, 4)),
        ],
        compiler_params=params(collective_id=2, has_side_effects=True),
    )(grads, own, normed, proj_weight, cotangent, grad_update, out_term)

    proj_grad, out_grad = pl.pallas_call(
        functools.partial(spread_kernel, (BLK * 128) ** (-0.5)),
        name="spread",
        grid=(5,),
        out_shape=(shape(WIDTH, 4 * WIDTH, dtype=F32), shape(WIDTH, WIDTH, dtype=F32)),
        in_specs=[pl.BlockSpec((TILES // 5, 16, 128), lambda n: (n, 0, 0))],
        out_specs=(
            pl.BlockSpec((WIDTH, WIDTH), lambda n: (0, jnp.minimum(n, 3))),
            pl.BlockSpec((WIDTH, WIDTH), lambda n: (0, 0)),
        ),
        compiler_params=params(),
    )(sums)
    return (layer_out, row_grads, proj_grad, out_grad)


def solution(mesh):
    placed = (
        P(("dp", "ctx"), None),
        P(("dp", "ctx")),
        P(("dp", "ctx")),
        P("dp", None),
        P(),
        P(),
        P(("dp", "ctx"), None),
    )
    return jax.shard_map(
        local,
        mesh=mesh,
        in_specs=placed,
        out_specs=(P(("dp", "ctx"), None), P(("dp", "ctx"), None), P(), P()),
        check_vma=False,
    )
```

```python
import functools

import jax
import jax.numpy as jnp
from jax import lax
from jax.experimental import pallas as pl
from jax.experimental.pallas import tpu as pltpu
from jax.sharding import PartitionSpec as P

MESH = pl.DeviceIdType.MESH
F32 = jnp.float32
BF16 = jnp.bfloat16
norm_eps = 1e-05
VMEM_LIMIT = 32 * 2**20

NCTX = 8
HALF = 128
BLK = 256
NB = 8
WIDTH = 512
HD = 64
EVENTS = 2048
TILES = 640
UNITS = 5
ORDERS = ("zxy", "zyx", "xyz", "yzx", "zxy")


def normalize(values):
    centre = values - jnp.mean(values, axis=-1, keepdims=True)
    inverse = lax.rsqrt(jnp.mean(centre * centre, axis=-1, keepdims=True) + norm_eps)
    return (centre * inverse, inverse)


def normalize_back(grad_in, normed, inverse):
    mean_grad = jnp.mean(grad_in, axis=-1, keepdims=True)
    mean_cross = jnp.mean(grad_in * normed, axis=-1, keepdims=True)
    return (grad_in - mean_grad - normed * mean_cross) * inverse


def silu(z):
    h = 0.5 * z
    return h + h * jnp.tanh(h)


def silu_grad(z):
    h = 0.5 * z
    u = 1.0 + jnp.tanh(h)
    return 0.5 * (u + h * u * (2.0 - u))


def dot(a, b):
    return lax.dot_general(a, b, (((1,), (0,)), ((), ())), preferred_element_type=F32)


def dot_nt(a, b):
    return lax.dot_general(a, b, (((1,), (1,)), ((), ())), preferred_element_type=F32)


def low(a, b):
    return jnp.concatenate([a[:, :HD], b[:, :HD]], axis=1)


def high(a, b):
    return jnp.concatenate([a[:, HD:], b[:, HD:]], axis=1)


def mod(a, n):
    return lax.rem(a + n, n)


def third(a):
    return (a * 21846) >> 16


def greet_ctx():
    cx = lax.axis_index("ctx")
    dp = lax.axis_index("dp")
    sem = pltpu.get_barrier_semaphore()
    for rel in range(1, NCTX):
        pl.semaphore_signal(
            sem, inc=1, device_id=(dp, lax.rem(cx + rel, NCTX)), device_id_type=MESH
        )
    return sem


def arrive_kernel(
    rows_hbm, sslot_hbm, aslot_hbm, w_hbm,
    own_ref, normed_ref, upd_ref, qk_ref, v_ref,
    rows_ref, sslot_ref, aslot_ref, w_ref,
    out, recv, hot_ref, qk_msg, v_msg, row_sems, send_sems, recv_sems, local_sems, in_sems,
):
    dp, cx = lax.axis_index("dp"), lax.axis_index("ctx")
    me = dp * NCTX + cx
    ndev = 128
    loads = [
        pltpu.make_async_copy(src, dst, in_sems.at[n])
        for n, (src, dst) in enumerate(
            ((rows_hbm, rows_ref), (sslot_hbm, sslot_ref), (aslot_hbm, aslot_ref), (w_hbm, w_ref))
        )
    ]
    for load in loads:
        load.start()

    def device(rel):
        d = lax.rem(me + rel, ndev)
        return (d // NCTX, lax.rem(d, NCTX))

    barrier = pltpu.get_barrier_semaphore()

    def greet(rel, carry):
        pl.semaphore_signal(barrier, inc=1, device_id=device(rel), device_id_type=MESH)
        return carry

    lax.fori_loop(1, ndev, greet, 0)

    for load in loads[:3]:
        load.wait()
    rows = rows_ref[...]
    rows4 = jnp.concatenate([rows[:, q * 128 : q * 128 + 128] for q in range(4)], axis=0)
    slot = sslot_ref[...]
    to = third(slot)
    place = ((to - me) & (ndev - 1)) * 16 + (slot - 3 * to)
    target = jnp.concatenate([place + 4 * q for q in range(4)], axis=1)
    seen = lax.broadcasted_iota(jnp.int32, (BLK, 1024), 0)

    def pack(n, carry):
        hot = jnp.where(seen == target - n * BLK, 1.0, 0.0).astype(BF16)
        part = dot(hot, rows4).astype(BF16)
        out[pl.ds(n * 16, 16)] = part.reshape(16, 16, 128)
        return carry

    lax.fori_loop(0, 8, pack, 0)

    pl.semaphore_wait(barrier, ndev - 1)

    def send(rel, carry):
        pltpu.make_async_remote_copy(
            src_ref=out.at[rel],
            dst_ref=recv.at[rel],
            send_sem=row_sems.at[0],
            recv_sem=row_sems.at[1],
            device_id=device(rel),
            device_id_type=MESH,
        ).start()
        return carry

    lax.fori_loop(1, ndev, send, 0)
    recv[0] = out[0]
    all_rows = pltpu.make_async_remote_copy(
        src_ref=out.at[pl.ds(1, ndev - 1)],
        dst_ref=recv.at[pl.ds(1, ndev - 1)],
        send_sem=row_sems.at[0],
        recv_sem=row_sems.at[1],
        device_id=(dp, cx),
        device_id_type=MESH,
    )
    aslot = jnp.transpose(jnp.broadcast_to(aslot_ref[...], (128, BLK)))[:, :1]
    come = third(aslot)
    picked = ((me - come) & (ndev - 1)) * 16 + (aslot - 3 * come)
    lanes = lax.broadcasted_iota(jnp.int32, (BLK, EVENTS), 1)
    for q in range(4):
        hot_ref[q] = jnp.where(lanes == picked + 4 * q, 1.0, 0.0).astype(BF16)
    loads[3].wait()
    all_rows.wait()

    got = recv[...].reshape(EVENTS, 128)
    own = jnp.concatenate([dot(hot_ref[q], got) for q in range(4)], axis=1)
    own_ref[...] = own.astype(BF16)
    normed = normalize(own)[0].astype(BF16)
    normed_ref[...] = normed

    query = (silu(dot(normed, w_ref[:, 1024:1536])).astype(BF16).astype(F32) * 0.0625).astype(BF16)
    key = silu(dot(normed, w_ref[:, 1536:2048])).astype(BF16)
    for a in range(4):
        x, y = query[:, a * 128 : a * 128 + 128], key[:, a * 128 : a * 128 + 128]
        qk_msg[2 * a] = low(x, y).reshape(2, HALF, 128)
        qk_msg[2 * a + 1] = high(x, y).reshape(2, HALF, 128)

    def to_head(peer, rel, n):
        if n < 2:
            src, dst = qk_msg.at[peer, n], qk_ref.at[cx if n == 0 else 15 - cx]
        else:
            src, dst = v_msg.at[peer], v_ref.at[cx]
        if rel == 0:
            return pltpu.make_async_copy(src, dst, local_sems.at[n])
        return pltpu.make_async_remote_copy(
            src_ref=src,
            dst_ref=dst,
            send_sem=send_sems.at[rel, n],
            recv_sem=recv_sems.at[rel, n],
            device_id=(dp, peer),
            device_id_type=MESH,
        )

    copies = []
    for rel in range(NCTX):
        peer = lax.rem(cx + rel, NCTX)
        for n in range(2):
            copies.append(to_head(peer, rel, n))
            copies[-1].start()

    value = silu(dot(normed, w_ref[:, 512:1024])).astype(BF16)
    for a in range(4):
        x = value[:HALF, a * 128 : a * 128 + 128]
        y = value[HALF:, a * 128 : a * 128 + 128]
        v_msg[2 * a] = low(x, y)
        v_msg[2 * a + 1] = high(x, y)
    for rel in range(NCTX):
        copies.append(to_head(lax.rem(cx + rel, NCTX), rel, 2))
        copies[-1].start()

    upd_ref[...] = silu(dot(normed, w_ref[:, :512])).astype(BF16)
    for copy in copies:
        copy.wait()


def timeline_ends(len_ref):
    ends, total = [], 0
    for n in range(4):
        total = total + len_ref[0, n]
        ends.append(total)
    return ends


def start_of(positions, ends):
    first = jnp.zeros_like(positions)
    for n in range(3):
        first = jnp.where(positions >= ends[n], ends[n], first)
    return first


def end_of(position, ends):
    last = ends[3]
    for n in (2, 1, 0):
        last = jnp.where(position < ends[n], ends[n], last)
    return last


def in_position_order(packed, dst):
    for c in range(NCTX):
        block = packed[c]
        dst[c * HALF : (c + 1) * HALF, :] = block[:, :HD]
        dst[(15 - c) * HALF : (16 - c) * HALF, :] = block[:, HD:]


def forward_kernel(len_ref, qk_ref, v_ref, att_ref, q, kt, v, att):
    ends = timeline_ends(len_ref)
    qk = qk_ref[...].reshape(EVENTS, 128)
    q[...] = qk[:, :HD]
    kt[...] = jnp.transpose(qk)[HD:, :]
    in_position_order(v_ref, v)

    for i in range(NB):
        row = i * BLK + lax.broadcasted_iota(jnp.int32, (BLK, 1), 0)
        first = start_of(row, ends)
        q_i = q[i * BLK : (i + 1) * BLK, :]

        def block(j, acc):
            at = pl.multiple_of(j * BLK, BLK)
            h = dot(q_i, kt[:, pl.ds(at, BLK)])
            w = h + h * jnp.tanh(h)
            t = at + lax.broadcasted_iota(jnp.int32, (BLK, BLK), 1)
            w = jnp.where((t >= first) & (t <= row), w, 0.0).astype(BF16)
            return acc + dot(w, v[pl.ds(at, BLK), :])

        lowest = start_of(jnp.int32(i * BLK), ends) >> 8
        att[i * BLK : (i + 1) * BLK, :] = lax.fori_loop(
            lowest, i + 1, block, jnp.zeros((BLK, HD), F32)
        ).astype(BF16)

    for c in range(NCTX):
        att_ref[c] = jnp.concatenate(
            [att[c * HALF : (c + 1) * HALF, :], att[(15 - c) * HALF : (16 - c) * HALF, :]], axis=1
        )


def backward_kernel(
    len_ref, qk_ref, v_ref, ga_ref, g_ref, q, qt, k, kt, v, ga, gat, gqt, gk, gv
):
    ends = timeline_ends(len_ref)
    qk = qk_ref[...].reshape(EVENTS, 128)
    q[...] = qk[:, :HD]
    k[...] = qk[:, HD:]
    qkt = jnp.transpose(qk)
    qt[...] = qkt[:HD]
    kt[...] = qkt[HD:]
    in_position_order(v_ref, v)
    in_position_order(ga_ref, ga)
    gat[...] = jnp.transpose(ga[...])
    gqt[...] = jnp.zeros_like(gqt)

    for j in range(NB):
        t = j * BLK + lax.broadcasted_iota(jnp.int32, (BLK, 1), 0)
        keys = slice(j * BLK, (j + 1) * BLK)
        k_j, kt_j, v_j = k[keys, :], kt[:, keys], v[keys, :]

        def block(i, carry):
            gk_j, gv_j = carry
            at = pl.multiple_of(i * BLK, BLK)
            rows = pl.ds(at, BLK)
            h = dot(k_j, qt[:, rows])
            u = 1.0 + jnp.tanh(h)
            w = h * u
            e = dot(v_j, gat[:, rows]) * (u + w * (2.0 - u))
            p = at + lax.broadcasted_iota(jnp.int32, (1, BLK), 1)
            ok = (t >= start_of(p, ends)) & (t <= p)
            w = jnp.where(ok, w, 0.0).astype(BF16)
            e = jnp.where(ok, e, 0.0).astype(BF16)
            gqt[:, rows] += dot(kt_j, e)
            return gk_j + dot(e, q[rows, :]), gv_j + dot(w, ga[rows, :])

        zero = jnp.zeros((BLK, HD), F32)
        highest = (end_of(jnp.int32(j * BLK + BLK - 1), ends) - 1) >> 8
        gk_j, gv_j = lax.fori_loop(j, highest + 1, block, (zero, zero))
        gk[keys, :] = gk_j.astype(BF16)
        gv[keys, :] = gv_j.astype(BF16)

    gq = jnp.transpose(gqt[...] * 0.0625).astype(BF16)
    for c in range(NCTX):
        a = slice(c * HALF, (c + 1) * HALF)
        b = slice((15 - c) * HALF, (16 - c) * HALF)
        g_ref[c, 0] = jnp.concatenate([gv[a, :], gv[b, :]], axis=1)
        g_ref[c, 1] = jnp.concatenate([gq[a, :], gq[b, :]], axis=1)
        g_ref[c, 2] = jnp.concatenate([gk[a, :], gk[b, :]], axis=1)


def exchange(src, dst, sems, base=0):
    dp, cx = lax.axis_index("dp"), lax.axis_index("ctx")
    copies = []
    for rel in range(NCTX):
        peer = lax.rem(cx + rel, NCTX)
        if rel == 0:
            copy = pltpu.make_async_copy(src.at[peer], dst.at[cx], sems.at[base])
        else:
            copy = pltpu.make_async_remote_copy(
                src_ref=src.at[peer],
                dst_ref=dst.at[cx],
                send_sem=sems.at[base + rel],
                recv_sem=sems.at[base + NCTX + rel],
                device_id=(dp, peer),
                device_id_type=MESH,
            )
        copy.start()
        copies.append(copy)
    return copies


def gather_heads(parts):
    first = [low(parts[2 * a], parts[2 * a + 1]) for a in range(4)]
    second = [high(parts[2 * a], parts[2 * a + 1]) for a in range(4)]
    return jnp.concatenate(
        [jnp.concatenate(first, axis=1), jnp.concatenate(second, axis=1)], axis=0
    )


def middle_kernel(
    att_ref, own_ref, upd_ref, cot_hbm, wo_hbm,
    layer_ref, gu_ref, outterm_ref, ga_ref,
    cot_ref, wo_ref, att_in, ga_msg, sems, in_sems,
):
    loads = [
        pltpu.make_async_copy(cot_hbm, cot_ref, in_sems.at[0]),
        pltpu.make_async_copy(wo_hbm, wo_ref, in_sems.at[1]),
    ]
    for load in loads:
        load.start()
    barrier = greet_ctx()
    pl.semaphore_wait(barrier, NCTX - 1)
    copies = exchange(att_ref, att_in, sems)
    for load in loads:
        load.wait()
    cot = cot_ref[...]
    wo = wo_ref[...]
    grad_gated = dot_nt(cot, wo)
    update = upd_ref[...].astype(F32)
    for copy in copies:
        copy.wait()
    attended = gather_heads([att_in[h].astype(F32) for h in range(NCTX)])
    att_normed, inverse = normalize(attended)
    grad_att = normalize_back(grad_gated * update, att_normed, inverse).astype(BF16)
    for a in range(4):
        x = grad_att[:HALF, a * 128 : a * 128 + 128]
        y = grad_att[HALF:, a * 128 : a * 128 + 128]
        ga_msg[2 * a] = low(x, y)
        ga_msg[2 * a + 1] = high(x, y)
    copies = exchange(ga_msg, ga_ref, sems, 2 * NCTX)
    gated = (att_normed * update).astype(BF16)
    layer_ref[...] = (own_ref[...].astype(F32) + dot(gated, wo)).astype(BF16)
    outterm_ref[...] = dot(jnp.transpose(gated), cot)
    gu_ref[...] = grad_gated * att_normed
    for copy in copies:
        copy.wait()


def final_kernel(
    g_ref, own_ref, normed_ref, w_ref, cot_ref, gu_ref, outterm_ref,
    rowgrad_ref, sum_ref,
    g_in, slope, acc, mine, core_in, out1, in1, out2, in2, out3, in3, sems, core_sems, axis_sems,
):
    dp, cx = lax.axis_index("dp"), lax.axis_index("ctx")
    core, xlo, z = lax.rem(dp, 2), lax.rem(dp // 2, 2), dp // 4
    xhi, y = lax.rem(cx, 2), cx // 2
    place = {"x": xhi * 2 + xlo, "y": y, "z": z}
    sibling = (dp + 1 - 2 * core, cx)

    def along(axis, r):
        c = lax.rem(place[axis] + r, 4)
        if axis == "x":
            return c, (z * 4 + lax.rem(c, 2) * 2 + core, y * 2 + c // 2)
        if axis == "y":
            return c, (dp, c * 2 + xhi)
        return c, (c * 4 + xlo * 2 + core, cx)

    barrier = greet_ctx()
    for device in [sibling] + [along(axis, r)[1] for axis in "xyz" for r in (1, 2, 3)]:
        pl.semaphore_signal(barrier, inc=1, device_id=device, device_id_type=MESH)

    own, cot = own_ref[...].astype(F32), cot_ref[...]
    normed, inverse = normalize(own)
    normed_bf = normed_ref[...]
    normed_t = jnp.transpose(normed_bf)

    def put(u, term):
        for n in range(4):
            part = term[:, n * 128 : n * 128 + 128].reshape(32, 16, 128)
            at = pl.ds(u * 64 + (n % 2) * 32, 32)
            acc[n // 2, at] = part
            mine[n // 2, at] = part.astype(BF16)

    def columns(block):
        return w_ref[:, block * WIDTH : (block + 1) * WIDTH]

    def unit_grads(u, block, grad, slope):
        grad_pre = (grad * slope).astype(BF16)
        put(u, dot(normed_t, grad_pre))
        return dot_nt(grad_pre, columns(block))

    def remote(src, dst, send_sem, recv_sem, device):
        copy = pltpu.make_async_remote_copy(
            src_ref=src, dst_ref=dst, send_sem=send_sem, recv_sem=recv_sem,
            device_id=device, device_id_type=MESH,
        )
        copy.start()
        return copy

    running = {}
    lead = (out1, out2, out3)
    landing = (in1, in2, in3)
    sizes = (16, 4, 1)
    base = [u * 64 for u in range(UNITS)]

    def core_start(u):
        at = pl.ds(u * 64, 64)
        running[u] = [
            remote(
                mine.at[1 - core, at], core_in.at[at], core_sems.at[0, u], core_sems.at[1, u], sibling
            )
        ]

    def finish(u):
        for copy in running.pop(u):
            copy.wait()

    def core_finish(u):
        finish(u)
        at = pl.ds(u * 64, 64)
        total = acc[core, at] + core_in[at].astype(F32)
        acc[core, at] = total
        out1[at] = total.astype(BF16)

    def axis_start(u, step):
        size = sizes[step]
        running[u] = []
        for r in (1, 2, 3):
            c, device = along(ORDERS[u][step], r)
            running[u].append(
                remote(
                    lead[step].at[pl.ds((u * 4 + c) * size, size)],
                    landing[step].at[r - 1, pl.ds(u * size, size)],
                    axis_sems.at[0, step, u, r], axis_sems.at[1, step, u, r], device,
                )
            )

    def axis_finish(u, step):
        finish(u)
        size = sizes[step]
        base[u] = base[u] + place[ORDERS[u][step]] * size
        total = acc[core, pl.ds(base[u], size)]
        for r in range(3):
            total = total + landing[step][r, pl.ds(u * size, size)].astype(F32)
        if step == 2:
            sum_ref[pl.ds(core * (UNITS * 64) + base[u], size)] = total.astype(BF16)
        else:
            acc[core, pl.ds(base[u], size)] = total
            lead[step + 1][pl.ds(u * size, size)] = total.astype(BF16)

    def back_start(u, step):
        size = sizes[step]
        held = sum_ref.at[pl.ds(core * (UNITS * 64) + base[u], size)]
        axis = ORDERS[u][step]
        running[u] = [
            remote(
                held, held, axis_sems.at[2, step, u, r], axis_sems.at[3, step, u, r], along(axis, r)[1]
            )
            for r in (1, 2, 3)
        ]
        base[u] = base[u] - place[axis] * size

    def core_back(u):
        held = sum_ref.at[pl.ds((core * UNITS + u) * 64, 64)]
        running[u] = [remote(held, held, core_sems.at[2, u], core_sems.at[3, u], sibling)]

    put(1, outterm_ref[...])
    grad_normed = unit_grads(0, 0, gu_ref[...], silu_grad(dot(normed_bf, columns(0))))
    pl.semaphore_wait(barrier, NCTX - 1 + 10)
    g_copies = exchange(g_ref, g_in, sems)
    early, late = (0, 1), (2, 3, 4)
    for u in early:
        core_start(u)
    for n in range(3):
        slope[n] = silu_grad(dot(normed_bf, columns(n + 1)))
    for u in early:
        core_finish(u)
        axis_start(u, 0)
    for copy in g_copies:
        copy.wait()
    for n, u in enumerate(late):
        grad = gather_heads([g_in[h, n].astype(F32) for h in range(NCTX)])
        grad_normed = grad_normed + unit_grads(u, n + 1, grad, slope[n])
        core_start(u)
    rowgrad_ref[...] = (
        cot.astype(F32) + normalize_back(grad_normed, normed, inverse)
    ).astype(BF16)
    for u in early:
        axis_finish(u, 0)
        axis_start(u, 1)
    for u in late:
        core_finish(u)
        axis_start(u, 0)
    for u in early:
        axis_finish(u, 1)
        axis_start(u, 2)
    for u in late:
        axis_finish(u, 0)
        axis_start(u, 1)
    for u in early:
        axis_finish(u, 2)
        back_start(u, 2)
    for u in late:
        axis_finish(u, 1)
        axis_start(u, 2)
    for u in early:
        finish(u)
        back_start(u, 1)
    for u in late:
        axis_finish(u, 2)
        back_start(u, 2)
    for u in early:
        finish(u)
        back_start(u, 0)
    for u in late:
        finish(u)
        back_start(u, 1)
    for u in early:
        finish(u)
        core_back(u)
    for u in late:
        finish(u)
        back_start(u, 0)
    for u in late:
        finish(u)
        core_back(u)
    for u in early + late:
        finish(u)


def spread_kernel(scale, sum_ref, layer_ref, rowgrad_ref, proj_hbm, out_hbm, layer_hbm, rowgrad_hbm, wide, sems):
    copies = [
        pltpu.make_async_copy(layer_ref, layer_hbm, sems.at[5]),
        pltpu.make_async_copy(rowgrad_ref, rowgrad_hbm, sems.at[6]),
    ]
    for copy in copies:
        copy.start()
    for u in range(UNITS):
        for n in range(4):
            at = (n // 2) * UNITS * 64 + u * 64 + (n % 2) * 32
            wide[u, :, n * 128 : n * 128 + 128] = (
                sum_ref[at : at + 32].reshape(WIDTH, 128).astype(F32) * scale
            )
        block = (0, None, 1, 2, 3)[u]
        dst = out_hbm if block is None else proj_hbm.at[:, pl.ds(block * WIDTH, WIDTH)]
        copies.append(pltpu.make_async_copy(wide.at[u], dst, sems.at[u]))
        copies[-1].start()
    for copy in copies:
        copy.wait()


HBM = pl.BlockSpec(memory_space=pltpu.HBM)
VM = pl.BlockSpec(memory_space=pltpu.VMEM)
SM = pl.BlockSpec(memory_space=pltpu.SMEM)


def shape(*dims, dtype=BF16):
    return jax.ShapeDtypeStruct(dims, dtype)


def params(**kw):
    return pltpu.CompilerParams(vmem_limit_bytes=VMEM_LIMIT, **kw)


def local(loader_rows, send_slot, arrive_slot, user_lengths, proj_weight, out_weight, cotangent):
    own, normed, update, qk, v = pl.pallas_call(
        arrive_kernel,
        name="arrive",
        out_shape=(
            shape(BLK, WIDTH), shape(BLK, WIDTH), shape(BLK, WIDTH),
            shape(16, HALF, 128), shape(NCTX, HALF, 128),
        ),
        in_specs=[HBM] * 4,
        out_specs=(VM,) * 5,
        scratch_shapes=[
            pltpu.VMEM((BLK, WIDTH), BF16),
            pltpu.VMEM((1, BLK), jnp.int32),
            pltpu.VMEM((1, BLK), jnp.int32),
            pltpu.VMEM((WIDTH, 4 * WIDTH), BF16),
            pltpu.VMEM((128, 16, 128), BF16),
            pltpu.VMEM((128, 16, 128), BF16),
            pltpu.VMEM((4, BLK, EVENTS), BF16),
            pltpu.VMEM((NCTX, 2, HALF, 128), BF16),
            pltpu.VMEM((NCTX, HALF, 128), BF16),
            pltpu.SemaphoreType.DMA((2,)),
            pltpu.SemaphoreType.DMA((NCTX, 3)),
            pltpu.SemaphoreType.DMA((NCTX, 3)),
            pltpu.SemaphoreType.DMA((3,)),
            pltpu.SemaphoreType.DMA((4,)),
        ],
        compiler_params=params(collective_id=0, has_side_effects=True),
    )(loader_rows, send_slot.reshape(1, BLK), arrive_slot.reshape(1, BLK), proj_weight)

    att = pl.pallas_call(
        forward_kernel,
        name="attend",
        out_shape=shape(NCTX, HALF, 128),
        in_specs=[SM, VM, VM],
        out_specs=VM,
        scratch_shapes=[
            pltpu.VMEM((EVENTS, HD), BF16),
            pltpu.VMEM((HD, EVENTS), BF16),
            pltpu.VMEM((EVENTS, HD), BF16),
            pltpu.VMEM((EVENTS, HD), BF16),
        ],
        compiler_params=params(),
    )(user_lengths, qk, v)

    layer_out, grad_update, out_term, grad_att = pl.pallas_call(
        middle_kernel,
        name="middle",
        out_shape=(
            shape(BLK, WIDTH), shape(BLK, WIDTH, dtype=F32), shape(WIDTH, WIDTH, dtype=F32),
            shape(NCTX, HALF, 128),
        ),
        in_specs=[VM, VM, VM, HBM, HBM],
        out_specs=(VM,) * 4,
        scratch_shapes=[
            pltpu.VMEM((BLK, WIDTH), BF16),
            pltpu.VMEM((WIDTH, WIDTH), BF16),
            pltpu.VMEM((NCTX, HALF, 128), BF16),
            pltpu.VMEM((NCTX, HALF, 128), BF16),
            pltpu.SemaphoreType.DMA((4 * NCTX,)),
            pltpu.SemaphoreType.DMA((2,)),
        ],
        compiler_params=params(collective_id=1, has_side_effects=True),
    )(att, own, update, cotangent, out_weight)

    grads = pl.pallas_call(
        backward_kernel,
        name="attend_back",
        out_shape=shape(NCTX, 3, HALF, 128),
        in_specs=[SM, VM, VM, VM],
        out_specs=VM,
        scratch_shapes=[
            pltpu.VMEM((EVENTS, HD), BF16),
            pltpu.VMEM((HD, EVENTS), BF16),
            pltpu.VMEM((EVENTS, HD), BF16),
            pltpu.VMEM((HD, EVENTS), BF16),
            pltpu.VMEM((EVENTS, HD), BF16),
            pltpu.VMEM((EVENTS, HD), BF16),
            pltpu.VMEM((HD, EVENTS), BF16),
            pltpu.VMEM((HD, EVENTS), F32),
            pltpu.VMEM((EVENTS, HD), BF16),
            pltpu.VMEM((EVENTS, HD), BF16),
        ],
        compiler_params=params(),
    )(user_lengths, qk, v, grad_att)

    row_grads, sums = pl.pallas_call(
        final_kernel,
        name="final",
        out_shape=(shape(BLK, WIDTH), shape(TILES, 16, 128)),
        in_specs=[VM] * 7,
        out_specs=(VM,) * 2,
        scratch_shapes=[
            pltpu.VMEM((NCTX, 3, HALF, 128), BF16),
            pltpu.VMEM((3, BLK, WIDTH), F32),
            pltpu.VMEM((2, UNITS * 64, 16, 128), F32),
            pltpu.VMEM((2, UNITS * 64, 16, 128), BF16),
            pltpu.VMEM((UNITS * 64, 16, 128), BF16),
            pltpu.VMEM((UNITS * 64, 16, 128), BF16),
            pltpu.VMEM((3, UNITS * 16, 16, 128), BF16),
            pltpu.VMEM((UNITS * 16, 16, 128), BF16),
            pltpu.VMEM((3, UNITS * 4, 16, 128), BF16),
            pltpu.VMEM((UNITS * 4, 16, 128), BF16),
            pltpu.VMEM((3, UNITS, 16, 128), BF16),
            pltpu.SemaphoreType.DMA((2 * NCTX,)),
            pltpu.SemaphoreType.DMA((4, UNITS)),
            pltpu.SemaphoreType.DMA((4, 3, UNITS, 4)),
        ],
        compiler_params=params(collective_id=2, has_side_effects=True),
    )(grads, own, normed, proj_weight, cotangent, grad_update, out_term)

    proj_grad, out_grad, layer_out, row_grads = pl.pallas_call(
        functools.partial(spread_kernel, (BLK * 128) ** (-0.5)),
        name="spread",
        out_shape=(
            shape(WIDTH, 4 * WIDTH, dtype=F32), shape(WIDTH, WIDTH, dtype=F32),
            shape(BLK, WIDTH), shape(BLK, WIDTH),
        ),
        in_specs=[VM] * 3,
        out_specs=(HBM,) * 4,
        scratch_shapes=[
            pltpu.VMEM((UNITS, WIDTH, WIDTH), F32),
            pltpu.SemaphoreType.DMA((7,)),
        ],
        compiler_params=params(),
    )(sums, layer_out, row_grads)
    return (layer_out, row_grads, proj_grad, out_grad)


def solution(mesh):
    placed = (
        P(("dp", "ctx"), None),
        P(("dp", "ctx")),
        P(("dp", "ctx")),
        P("dp", None),
        P(),
        P(),
        P(("dp", "ctx"), None),
    )
    return jax.shard_map(
        local,
        mesh=mesh,
        in_specs=placed,
        out_specs=(P(("dp", "ctx"), None), P(("dp", "ctx"), None), P(), P()),
        check_vma=False,
    )
```

```python
import functools

import jax
import jax.numpy as jnp
from jax import lax
from jax.experimental import pallas as pl
from jax.experimental.pallas import tpu as pltpu
from jax.sharding import PartitionSpec as P

MESH = pl.DeviceIdType.MESH
F32 = jnp.float32
BF16 = jnp.bfloat16
norm_eps = 1e-05
VMEM_LIMIT = 32 * 2**20

NCTX = 8
HALF = 128
BLK = 256
NB = 8
WIDTH = 512
HD = 64
EVENTS = 2048
UNITS = 5
ORDERS = ("zxy", "zyx", "xyz", "yzx", "zxy")
BACK = ("zxy", "zyx", "zyx", "xzy", "yxz")


def normalize(values):
    centre = values - jnp.mean(values, axis=-1, keepdims=True)
    inverse = lax.rsqrt(jnp.mean(centre * centre, axis=-1, keepdims=True) + norm_eps)
    return (centre * inverse, inverse)


def normalize_back(grad_in, normed, inverse):
    mean_grad = jnp.mean(grad_in, axis=-1, keepdims=True)
    mean_cross = jnp.mean(grad_in * normed, axis=-1, keepdims=True)
    return (grad_in - mean_grad - normed * mean_cross) * inverse


def silu(z):
    h = 0.5 * z
    return h + h * jnp.tanh(h)


def silu_grad(z):
    h = 0.5 * z
    u = 1.0 + jnp.tanh(h)
    return 0.5 * (u + h * u * (2.0 - u))


def dot(a, b):
    return lax.dot_general(a, b, (((1,), (0,)), ((), ())), preferred_element_type=F32)


def dot_nt(a, b):
    return lax.dot_general(a, b, (((1,), (1,)), ((), ())), preferred_element_type=F32)


def low(a, b):
    return jnp.concatenate([a[:, :HD], b[:, :HD]], axis=1)


def high(a, b):
    return jnp.concatenate([a[:, HD:], b[:, HD:]], axis=1)


def mod(a, n):
    return lax.rem(a + n, n)


def third(a):
    return (a * 21846) >> 16


def greet_ctx():
    cx = lax.axis_index("ctx")
    dp = lax.axis_index("dp")
    sem = pltpu.get_barrier_semaphore()
    for rel in range(1, NCTX):
        pl.semaphore_signal(
            sem, inc=1, device_id=(dp, lax.rem(cx + rel, NCTX)), device_id_type=MESH
        )
    return sem


def arrive_kernel(
    rows_hbm, sslot_hbm, aslot_hbm, w_hbm,
    own_ref, normed_ref, upd_ref, qk_ref, v_ref,
    rows_ref, sslot_ref, aslot_ref, w_ref,
    out, recv, hot_ref, qk_msg, v_msg, row_sems, send_sems, recv_sems, local_sems, in_sems,
):
    dp, cx = lax.axis_index("dp"), lax.axis_index("ctx")
    me = dp * NCTX + cx
    ndev = 128
    loads = [
        pltpu.make_async_copy(src, dst, in_sems.at[n])
        for n, (src, dst) in enumerate(
            ((rows_hbm, rows_ref), (sslot_hbm, sslot_ref), (aslot_hbm, aslot_ref), (w_hbm, w_ref))
        )
    ]
    for load in loads:
        load.start()

    def device(rel):
        d = (me + rel) & (ndev - 1)
        return (d >> 3, d & (NCTX - 1))

    barrier = pltpu.get_barrier_semaphore()

    def greet(rel, carry):
        pl.semaphore_signal(barrier, inc=1, device_id=device(rel), device_id_type=MESH)
        return carry

    lax.fori_loop(1, ndev, greet, 0, unroll=6)

    for load in loads[:3]:
        load.wait()
    rows = rows_ref[...]
    rows4 = jnp.concatenate([rows[:, q * 128 : q * 128 + 128] for q in range(4)], axis=0)
    slot = sslot_ref[...]
    to = third(slot)
    place = ((to - me) & (ndev - 1)) * 16 + (slot - 3 * to)
    target = jnp.concatenate([place + 4 * q for q in range(4)], axis=1)
    seen = lax.broadcasted_iota(jnp.int32, (BLK, 1024), 0)

    def pack(n, carry):
        hot = jnp.where(seen == target - n * BLK, 1.0, 0.0).astype(BF16)
        part = dot(hot, rows4).astype(BF16)
        out[pl.ds(n * 16, 16)] = part.reshape(16, 16, 128)
        return carry

    lax.fori_loop(0, 8, pack, 0)

    pl.semaphore_wait(barrier, ndev - 1)

    def send(rel, carry):
        pltpu.make_async_remote_copy(
            src_ref=out.at[rel],
            dst_ref=recv.at[rel],
            send_sem=row_sems.at[0],
            recv_sem=row_sems.at[1],
            device_id=device(rel),
            device_id_type=MESH,
        ).start()
        return carry

    lax.fori_loop(1, ndev, send, 0, unroll=6)
    recv[0] = out[0]
    all_rows = pltpu.make_async_remote_copy(
        src_ref=out.at[pl.ds(1, ndev - 1)],
        dst_ref=recv.at[pl.ds(1, ndev - 1)],
        send_sem=row_sems.at[0],
        recv_sem=row_sems.at[1],
        device_id=(dp, cx),
        device_id_type=MESH,
    )
    aslot = jnp.transpose(jnp.broadcast_to(aslot_ref[...], (128, BLK)))[:, :1]
    come = third(aslot)
    picked = ((me - come) & (ndev - 1)) * 16 + (aslot - 3 * come)
    lanes = lax.broadcasted_iota(jnp.int32, (BLK, EVENTS), 1)
    for q in range(4):
        hot_ref[q] = jnp.where(lanes == picked + 4 * q, 1.0, 0.0).astype(BF16)
    loads[3].wait()
    all_rows.wait()

    got = recv[...].reshape(EVENTS, 128)
    own = jnp.concatenate([dot(hot_ref[q], got) for q in range(4)], axis=1)
    own_ref[...] = own.astype(BF16)
    normed = normalize(own)[0].astype(BF16)
    normed_ref[...] = normed

    query = (silu(dot(normed, w_ref[:, 1024:1536])).astype(BF16).astype(F32) * 0.0625).astype(BF16)
    key = silu(dot(normed, w_ref[:, 1536:2048])).astype(BF16)
    for a in range(4):
        x, y = query[:, a * 128 : a * 128 + 128], key[:, a * 128 : a * 128 + 128]
        qk_msg[2 * a] = low(x, y).reshape(2, HALF, 128)
        qk_msg[2 * a + 1] = high(x, y).reshape(2, HALF, 128)

    def to_head(peer, rel, n):
        if n < 2:
            src, dst = qk_msg.at[peer, n], qk_ref.at[cx if n == 0 else 15 - cx]
        else:
            src, dst = v_msg.at[peer], v_ref.at[cx]
        if rel == 0:
            return pltpu.make_async_copy(src, dst, local_sems.at[n])
        return pltpu.make_async_remote_copy(
            src_ref=src,
            dst_ref=dst,
            send_sem=send_sems.at[rel, n],
            recv_sem=recv_sems.at[rel, n],
            device_id=(dp, peer),
            device_id_type=MESH,
        )

    copies = []
    for rel in range(NCTX):
        peer = lax.rem(cx + rel, NCTX)
        for n in range(2):
            copies.append(to_head(peer, rel, n))
            copies[-1].start()

    value = silu(dot(normed, w_ref[:, 512:1024])).astype(BF16)
    for a in range(4):
        x = value[:HALF, a * 128 : a * 128 + 128]
        y = value[HALF:, a * 128 : a * 128 + 128]
        v_msg[2 * a] = low(x, y)
        v_msg[2 * a + 1] = high(x, y)
    for rel in range(NCTX):
        copies.append(to_head(lax.rem(cx + rel, NCTX), rel, 2))
        copies[-1].start()

    upd_ref[...] = silu(dot(normed, w_ref[:, :512])).astype(BF16)
    for copy in copies:
        copy.wait()


def timeline_ends(len_ref):
    ends, total = [], 0
    for n in range(4):
        total = total + len_ref[0, n]
        ends.append(total)
    return ends


def start_of(positions, ends):
    first = jnp.zeros_like(positions)
    for n in range(3):
        first = jnp.where(positions >= ends[n], ends[n], first)
    return first


def end_of(position, ends):
    last = ends[3]
    for n in (2, 1, 0):
        last = jnp.where(position < ends[n], ends[n], last)
    return last


def in_position_order(packed, dst):
    for c in range(NCTX):
        block = packed[c]
        dst[c * HALF : (c + 1) * HALF, :] = block[:, :HD]
        dst[(15 - c) * HALF : (16 - c) * HALF, :] = block[:, HD:]


def list_pairs(ends, table):
    count = jnp.int32(0)
    for i in range(NB):
        lowest = start_of(jnp.int32(i * BLK), ends) >> 8
        for j in range(i + 1):
            table[count] = i * NB + j
            count = count + jnp.where(j >= lowest, 1, 0).astype(jnp.int32)
    return count


def for_pairs(unroll, table, count, ends, pair_fn):
    t = lax.broadcasted_iota(jnp.int32, (BLK, BLK), 0)
    p = lax.broadcasted_iota(jnp.int32, (1, BLK), 1)

    def step(n, carry):
        for m in range(unroll):
            at = n * unroll + m
            live = at < count
            pair = jnp.where(live, table[jnp.minimum(at, NB * NB - 1)], 0)
            i, j = pair >> 3, pair & 7
            first = jnp.where(live, start_of(p + i * BLK, ends) - j * BLK, BLK)
            allowed = (t >= first) & (t <= p + (i - j) * BLK)
            pair_fn(
                pl.ds(pl.multiple_of(i * BLK, BLK), BLK),
                pl.ds(pl.multiple_of(j * BLK, BLK), BLK),
                allowed,
            )
        return carry

    lax.fori_loop(0, (count + unroll - 1) // unroll, step, 0)


def by_owner(blocks, c):
    return jnp.concatenate(
        [blocks[c * HALF : (c + 1) * HALF, :], blocks[(15 - c) * HALF : (16 - c) * HALF, :]], axis=1
    )


def backward_kernel(
    len_ref, qk_ref, v_ref, ga_ref, g_ref, q, qt, k, kt, v, ga, gat, gqt, gk, gv, table
):
    ends = timeline_ends(len_ref)
    count = list_pairs(ends, table)
    qk = qk_ref[...].reshape(EVENTS, 128)
    q[...] = qk[:, :HD]
    k[...] = qk[:, HD:]
    qkt = jnp.transpose(qk)
    qt[...] = qkt[:HD]
    kt[...] = qkt[HD:]
    in_position_order(v_ref, v)
    in_position_order(ga_ref, ga)
    gat[...] = jnp.transpose(ga[...])
    gqt[...] = jnp.zeros_like(gqt)
    gk[...] = jnp.zeros_like(gk)
    gv[...] = jnp.zeros_like(gv)

    def pair(rows, keys, allowed):
        h = dot(k[keys, :], qt[:, rows])
        u = 1.0 + jnp.tanh(h)
        w = h * u
        e = dot(v[keys, :], gat[:, rows]) * (u + w * (2.0 - u))
        w = jnp.where(allowed, w, 0.0).astype(BF16)
        e = jnp.where(allowed, e, 0.0).astype(BF16)
        gqt[:, rows] += dot(kt[:, keys], e)
        gk[keys, :] += dot(e, q[rows, :])
        gv[keys, :] += dot(w, ga[rows, :])

    for_pairs(3, table, count, ends, pair)
    gq = jnp.transpose(gqt[...] * 0.0625).astype(BF16)
    gk_done, gv_done = gk[...].astype(BF16), gv[...].astype(BF16)
    for c in range(NCTX):
        g_ref[c, 0] = by_owner(gv_done, c)
        g_ref[c, 1] = by_owner(gq, c)
        g_ref[c, 2] = by_owner(gk_done, c)


def exchange(src, dst, sems, base=0):
    dp, cx = lax.axis_index("dp"), lax.axis_index("ctx")
    copies = []
    for rel in range(NCTX):
        peer = lax.rem(cx + rel, NCTX)
        if rel == 0:
            copy = pltpu.make_async_copy(src.at[peer], dst.at[cx], sems.at[base])
        else:
            copy = pltpu.make_async_remote_copy(
                src_ref=src.at[peer],
                dst_ref=dst.at[cx],
                send_sem=sems.at[base + rel],
                recv_sem=sems.at[base + NCTX + rel],
                device_id=(dp, peer),
                device_id_type=MESH,
            )
        copy.start()
        copies.append(copy)
    return copies


def gather_heads(parts):
    first = [low(parts[2 * a], parts[2 * a + 1]) for a in range(4)]
    second = [high(parts[2 * a], parts[2 * a + 1]) for a in range(4)]
    return jnp.concatenate(
        [jnp.concatenate(first, axis=1), jnp.concatenate(second, axis=1)], axis=0
    )


def forward_kernel(
    len_ref, qk_ref, v_ref, own_ref, upd_ref, cot_hbm, wo_hbm,
    layer_ref, gu_ref, outterm_ref, ga_ref,
    qt, k, v, vt, att, att_msg, cot_ref, wo_ref, att_in, ga_msg, sems, in_sems,
):
    dp, cx = lax.axis_index("dp"), lax.axis_index("ctx")
    loads = [
        pltpu.make_async_copy(cot_hbm, cot_ref, in_sems.at[0]),
        pltpu.make_async_copy(wo_hbm, wo_ref, in_sems.at[1]),
    ]
    for load in loads:
        load.start()
    barrier = greet_ctx()
    ends = timeline_ends(len_ref)
    qk = qk_ref[...].reshape(EVENTS, 128)
    k[...] = qk[:, HD:]
    qt[...] = jnp.transpose(qk)[:HD, :]
    in_position_order(v_ref, v)
    vt[...] = jnp.transpose(v[...])
    t = lax.broadcasted_iota(jnp.int32, (BLK, BLK), 0)
    p = lax.broadcasted_iota(jnp.int32, (1, BLK), 1)

    def to_owner(c):
        far = pltpu.make_async_remote_copy(
            src_ref=att_msg.at[c],
            dst_ref=att_in.at[cx],
            send_sem=sems.at[c],
            recv_sem=sems.at[NCTX + cx],
            device_id=(dp, c),
            device_id_type=MESH,
        )
        return far, pltpu.make_async_copy(att_msg.at[c], att_in.at[cx], sems.at[c])

    pl.semaphore_wait(barrier, NCTX - 1)

    def step(n, carry):
        block = (n + (cx >> 1)) & 3
        att[...] = jnp.zeros_like(att)
        for m in range(9):
            second = m > block
            i = jnp.where(second, 7 - block, block)
            j = jnp.where(second, m - block - 1, m)
            rows = pl.ds(pl.multiple_of(i * BLK, BLK), BLK)
            keys = pl.ds(pl.multiple_of(j * BLK, BLK), BLK)
            h = dot(k[keys, :], qt[:, rows])
            w = h + h * jnp.tanh(h)
            first = start_of(p + i * BLK, ends) - j * BLK
            w = jnp.where((t >= first) & (t <= p + (i - j) * BLK), w, 0.0).astype(BF16)
            att[jnp.where(second, 1, 0)] += dot(vt[:, keys], w)
        near_rows = jnp.transpose(att[0]).astype(BF16)
        far_rows = jnp.transpose(att[1]).astype(BF16)
        for e in range(2):
            c = 2 * block + e
            att_msg[c] = jnp.concatenate(
                [near_rows[e * HALF : e * HALF + HALF], far_rows[HALF - e * HALF : BLK - e * HALF]], axis=1
            )
            far, near = to_owner(c)

            @pl.when(c != cx)
            def _():
                far.start()

            @pl.when(c == cx)
            def _():
                near.start()

        return carry

    lax.fori_loop(0, 4, step, 0)
    for load in loads:
        load.wait()
    cot = cot_ref[...]
    wo = wo_ref[...]
    grad_gated = dot_nt(cot, wo)
    to_owner(cx)[1].wait()
    for rel in range(1, NCTX):
        h = (cx + rel) & (NCTX - 1)
        to_owner(h)[0].wait_send()
        pltpu.make_async_remote_copy(
            src_ref=att_msg.at[h],
            dst_ref=att_in.at[h],
            send_sem=sems.at[h],
            recv_sem=sems.at[NCTX + h],
            device_id=(dp, h),
            device_id_type=MESH,
        ).wait_recv()
    update = upd_ref[...].astype(F32)
    attended = gather_heads([att_in[h].astype(F32) for h in range(NCTX)])
    att_normed, inverse = normalize(attended)
    grad_att = normalize_back(grad_gated * update, att_normed, inverse).astype(BF16)
    for a in range(4):
        x = grad_att[:HALF, a * 128 : a * 128 + 128]
        y = grad_att[HALF:, a * 128 : a * 128 + 128]
        ga_msg[2 * a] = low(x, y)
        ga_msg[2 * a + 1] = high(x, y)
    copies = exchange(ga_msg, ga_ref, sems, 2 * NCTX)
    gated = (att_normed * update).astype(BF16)
    layer_ref[...] = (own_ref[...].astype(F32) + dot(gated, wo)).astype(BF16)
    outterm_ref[...] = dot(jnp.transpose(gated), cot)
    gu_ref[...] = grad_gated * att_normed
    for copy in copies:
        copy.wait()


def final_kernel(
    g_ref, own_ref, normed_ref, w_ref, cot_ref, gu_ref, outterm_ref,
    rowgrad_ref, sum_ref,
    g_in, slope, acc, mine, core_in, out1, in1, out2, in2, out3, in3, sems, core_sems, axis_sems,
):
    dp, cx = lax.axis_index("dp"), lax.axis_index("ctx")
    core, xlo, z = lax.rem(dp, 2), lax.rem(dp // 2, 2), dp // 4
    xhi, y = lax.rem(cx, 2), cx // 2
    place = {"x": xhi * 2 + xlo, "y": y, "z": z}
    sibling = (dp + 1 - 2 * core, cx)

    def along(axis, r):
        c = lax.rem(place[axis] + r, 4)
        if axis == "x":
            return c, (z * 4 + lax.rem(c, 2) * 2 + core, y * 2 + c // 2)
        if axis == "y":
            return c, (dp, c * 2 + xhi)
        return c, (c * 4 + xlo * 2 + core, cx)

    barrier = greet_ctx()
    for device in [sibling] + [along(axis, r)[1] for axis in "xyz" for r in (1, 2, 3)]:
        pl.semaphore_signal(barrier, inc=1, device_id=device, device_id_type=MESH)

    def put(u, term):
        for n in range(4):
            part = term[:, n * 128 : n * 128 + 128].reshape(32, 16, 128)
            at = pl.ds(u * 64 + (n % 2) * 32, 32)
            acc[n // 2, at] = part
            mine[n // 2, at] = part.astype(BF16)

    def columns(block):
        return w_ref[:, block * WIDTH : (block + 1) * WIDTH]

    def unit_grads(u, block, grad, slope):
        grad_pre = (grad * slope).astype(BF16)
        put(u, dot(normed_t, grad_pre))
        return dot_nt(grad_pre, columns(block))

    def remote(src, dst, send_sem, recv_sem, device):
        copy = pltpu.make_async_remote_copy(
            src_ref=src, dst_ref=dst, send_sem=send_sem, recv_sem=recv_sem,
            device_id=device, device_id_type=MESH,
        )
        copy.start()
        return copy

    running = {}
    lead = (out1, out2, out3)
    landing = (in1, in2, in3)
    sizes = (16, 4, 1)
    base = [u * 64 for u in range(UNITS)]

    def core_start(u):
        at = pl.ds(u * 64, 64)
        running[u] = [
            remote(
                mine.at[1 - core, at], core_in.at[at], core_sems.at[0, u], core_sems.at[1, u], sibling
            )
        ]

    def finish(u):
        for copy in running.pop(u):
            copy.wait()

    def core_finish(u):
        finish(u)
        at = pl.ds(u * 64, 64)
        total = acc[core, at] + core_in[at].astype(F32)
        acc[core, at] = total
        out1[at] = total.astype(BF16)

    def axis_start(u, step):
        size = sizes[step]
        running[u] = []
        for r in (1, 2, 3):
            c, device = along(ORDERS[u][step], r)
            running[u].append(
                remote(
                    lead[step].at[pl.ds((u * 4 + c) * size, size)],
                    landing[step].at[r - 1, pl.ds(u * size, size)],
                    axis_sems.at[0, step, u, r], axis_sems.at[1, step, u, r], device,
                )
            )

    def axis_finish(u, step):
        finish(u)
        size = sizes[step]
        base[u] = base[u] + place[ORDERS[u][step]] * size
        total = acc[core, pl.ds(base[u], size)]
        for r in range(3):
            total = total + landing[step][r, pl.ds(u * size, size)].astype(F32)
        if step == 2:
            held[u] = [place[axis] for axis in ORDERS[u]]
            sum_ref[(core, u, *held[u])] = total.astype(BF16)[0]
        else:
            acc[core, pl.ds(base[u], size)] = total
            lead[step + 1][pl.ds(u * size, size)] = total.astype(BF16)

    held = {}

    def back_start(u, step):
        axis = BACK[u][step]
        part = sum_ref.at[(core, u, *held[u])]
        running[u] = [
            remote(
                part, part, axis_sems.at[2, step, u, r], axis_sems.at[3, step, u, r], along(axis, r)[1]
            )
            for r in (1, 2, 3)
        ]
        held[u][ORDERS[u].index(axis)] = slice(None)

    def core_back(u):
        part = sum_ref.at[core, u]
        running[u] = [remote(part, part, core_sems.at[2, u], core_sems.at[3, u], sibling)]

    def after_core(u):
        core_finish(u)
        axis_start(u, 0)

    def after_axis(u, step):
        axis_finish(u, step)
        if step < 2:
            axis_start(u, step + 1)
        else:
            back_start(u, 0)

    def after_back(u, step):
        finish(u)
        if step < 2:
            back_start(u, step + 1)
        else:
            core_back(u)

    pl.semaphore_wait(barrier, NCTX - 1 + 10)
    g_copies = []
    for n in range(3):
        for rel in range(NCTX):
            peer = (cx + rel) & (NCTX - 1)
            src, dst = g_ref.at[peer, n], g_in.at[cx, n]
            if rel == 0:
                g_copies.append(pltpu.make_async_copy(src, dst, sems.at[n, 0]))
                g_copies[-1].start()
            else:
                g_copies.append(
                    remote(src, dst, sems.at[n, rel], sems.at[n, NCTX + rel], (dp, peer))
                )

    own, cot = own_ref[...].astype(F32), cot_ref[...]
    normed, inverse = normalize(own)
    normed_bf = normed_ref[...]
    normed_t = jnp.transpose(normed_bf)
    put(1, outterm_ref[...])
    core_start(1)
    grad_normed = unit_grads(0, 0, gu_ref[...], silu_grad(dot(normed_bf, columns(0))))
    core_start(0)
    for n in range(3):
        slope[n] = silu_grad(dot(normed_bf, columns(n + 1)))

    def late(n, total):
        for copy in g_copies[n * NCTX : (n + 1) * NCTX]:
            copy.wait()
        grad = gather_heads([g_in[h, n].astype(F32) for h in range(NCTX)])
        total = total + unit_grads(n + 2, n + 1, grad, slope[n])
        core_start(n + 2)
        return total

    grad_normed = late(0, grad_normed)
    grad_normed = late(1, grad_normed)
    after_core(1)
    after_core(0)
    grad_normed = late(2, grad_normed)
    after_core(2)
    after_core(3)
    rowgrad_ref[...] = (
        cot.astype(F32) + normalize_back(grad_normed, normed, inverse)
    ).astype(BF16)
    after_core(4)
    after_axis(1, 0)
    after_axis(0, 0)
    after_axis(2, 0)
    after_axis(3, 0)
    after_axis(4, 0)
    after_axis(1, 1)
    after_axis(0, 1)
    after_axis(2, 1)
    after_axis(3, 1)
    after_axis(4, 1)
    after_axis(1, 2)
    after_axis(0, 2)
    after_axis(2, 2)
    after_axis(3, 2)
    after_axis(4, 2)
    after_back(1, 0)
    after_back(0, 0)
    after_back(2, 0)
    after_back(3, 0)
    after_back(4, 0)
    after_back(1, 1)
    after_back(0, 1)
    after_back(2, 1)
    after_back(3, 1)
    after_back(4, 1)
    after_back(1, 2)
    after_back(0, 2)
    after_back(2, 2)
    after_back(3, 2)
    after_back(4, 2)
    for u in range(UNITS):
        finish(u)


def spread_kernel(scale, sum_ref, layer_ref, rowgrad_ref, proj_hbm, out_hbm, layer_hbm, rowgrad_hbm, wide, sems):
    copies = [
        pltpu.make_async_copy(layer_ref, layer_hbm, sems.at[5]),
        pltpu.make_async_copy(rowgrad_ref, rowgrad_hbm, sems.at[6]),
    ]
    for copy in copies:
        copy.start()
    for u in range(UNITS):
        for n in range(4):
            at = (n % 2) * 2
            wide[u, :, n * 128 : n * 128 + 128] = (
                sum_ref[n // 2, u, at : at + 2].reshape(WIDTH, 128).astype(F32) * scale
            )
        block = (0, None, 1, 2, 3)[u]
        dst = out_hbm if block is None else proj_hbm.at[:, pl.ds(block * WIDTH, WIDTH)]
        copies.append(pltpu.make_async_copy(wide.at[u], dst, sems.at[u]))
        copies[-1].start()
    for copy in copies:
        copy.wait()


HBM = pl.BlockSpec(memory_space=pltpu.HBM)
VM = pl.BlockSpec(memory_space=pltpu.VMEM)
SM = pl.BlockSpec(memory_space=pltpu.SMEM)


def shape(*dims, dtype=BF16):
    return jax.ShapeDtypeStruct(dims, dtype)


def params(vmem_limit_bytes=VMEM_LIMIT, **kw):
    return pltpu.CompilerParams(vmem_limit_bytes=vmem_limit_bytes, **kw)


def in_hbm(array):
    return pltpu.with_memory_space_constraint(array, pltpu.HBM)


def local(loader_rows, send_slot, arrive_slot, user_lengths, proj_weight, out_weight, cotangent):
    own, normed, update, qk, v = pl.pallas_call(
        arrive_kernel,
        name="arrive",
        out_shape=(
            shape(BLK, WIDTH), shape(BLK, WIDTH), shape(BLK, WIDTH),
            shape(16, HALF, 128), shape(NCTX, HALF, 128),
        ),
        in_specs=[HBM] * 4,
        out_specs=(VM,) * 5,
        scratch_shapes=[
            pltpu.VMEM((BLK, WIDTH), BF16),
            pltpu.VMEM((1, BLK), jnp.int32),
            pltpu.VMEM((1, BLK), jnp.int32),
            pltpu.VMEM((WIDTH, 4 * WIDTH), BF16),
            pltpu.VMEM((128, 16, 128), BF16),
            pltpu.VMEM((128, 16, 128), BF16),
            pltpu.VMEM((4, BLK, EVENTS), BF16),
            pltpu.VMEM((NCTX, 2, HALF, 128), BF16),
            pltpu.VMEM((NCTX, HALF, 128), BF16),
            pltpu.SemaphoreType.DMA((2,)),
            pltpu.SemaphoreType.DMA((NCTX, 3)),
            pltpu.SemaphoreType.DMA((NCTX, 3)),
            pltpu.SemaphoreType.DMA((3,)),
            pltpu.SemaphoreType.DMA((4,)),
        ],
        compiler_params=params(collective_id=0, has_side_effects=True),
    )(
        *map(in_hbm, (loader_rows, send_slot.reshape(1, BLK), arrive_slot.reshape(1, BLK), proj_weight))
    )

    layer_out, grad_update, out_term, grad_att = pl.pallas_call(
        forward_kernel,
        name="forward",
        out_shape=(
            shape(BLK, WIDTH), shape(BLK, WIDTH, dtype=F32), shape(WIDTH, WIDTH, dtype=F32),
            shape(NCTX, HALF, 128),
        ),
        in_specs=[SM, VM, VM, VM, VM, HBM, HBM],
        out_specs=(VM,) * 4,
        scratch_shapes=[
            pltpu.VMEM((HD, EVENTS), BF16),
            pltpu.VMEM((EVENTS, HD), BF16),
            pltpu.VMEM((EVENTS, HD), BF16),
            pltpu.VMEM((HD, EVENTS), BF16),
            pltpu.VMEM((2, HD, BLK), F32),
            pltpu.VMEM((NCTX, HALF, 128), BF16),
            pltpu.VMEM((BLK, WIDTH), BF16),
            pltpu.VMEM((WIDTH, WIDTH), BF16),
            pltpu.VMEM((NCTX, HALF, 128), BF16),
            pltpu.VMEM((NCTX, HALF, 128), BF16),
            pltpu.SemaphoreType.DMA((4 * NCTX,)),
            pltpu.SemaphoreType.DMA((2,)),
        ],
        compiler_params=params(collective_id=1, has_side_effects=True),
    )(in_hbm(user_lengths), qk, v, own, update, in_hbm(cotangent), in_hbm(out_weight))

    grads = pl.pallas_call(
        backward_kernel,
        name="attend_back",
        out_shape=shape(NCTX, 3, HALF, 128),
        in_specs=[SM, VM, VM, VM],
        out_specs=VM,
        scratch_shapes=[
            pltpu.VMEM((EVENTS, HD), BF16),
            pltpu.VMEM((HD, EVENTS), BF16),
            pltpu.VMEM((EVENTS, HD), BF16),
            pltpu.VMEM((HD, EVENTS), BF16),
            pltpu.VMEM((EVENTS, HD), BF16),
            pltpu.VMEM((EVENTS, HD), BF16),
            pltpu.VMEM((HD, EVENTS), BF16),
            pltpu.VMEM((HD, EVENTS), F32),
            pltpu.VMEM((EVENTS, HD), F32),
            pltpu.VMEM((EVENTS, HD), F32),
            pltpu.SMEM((NB * NB,), jnp.int32),
        ],
        compiler_params=params(),
    )(in_hbm(user_lengths), qk, v, grad_att)

    row_grads, sums = pl.pallas_call(
        final_kernel,
        name="final",
        out_shape=(shape(BLK, WIDTH), shape(2, UNITS, 4, 4, 4, 16, 128)),
        in_specs=[VM] * 7,
        out_specs=(VM,) * 2,
        scratch_shapes=[
            pltpu.VMEM((NCTX, 3, HALF, 128), BF16),
            pltpu.VMEM((3, BLK, WIDTH), F32),
            pltpu.VMEM((2, UNITS * 64, 16, 128), F32),
            pltpu.VMEM((2, UNITS * 64, 16, 128), BF16),
            pltpu.VMEM((UNITS * 64, 16, 128), BF16),
            pltpu.VMEM((UNITS * 64, 16, 128), BF16),
            pltpu.VMEM((3, UNITS * 16, 16, 128), BF16),
            pltpu.VMEM((UNITS * 16, 16, 128), BF16),
            pltpu.VMEM((3, UNITS * 4, 16, 128), BF16),
            pltpu.VMEM((UNITS * 4, 16, 128), BF16),
            pltpu.VMEM((3, UNITS, 16, 128), BF16),
            pltpu.SemaphoreType.DMA((3, 2 * NCTX)),
            pltpu.SemaphoreType.DMA((4, UNITS)),
            pltpu.SemaphoreType.DMA((4, 3, UNITS, 4)),
        ],
        compiler_params=params(collective_id=2, has_side_effects=True),
    )(grads, own, normed, proj_weight, cotangent, grad_update, out_term)

    proj_grad, out_grad, layer_out, row_grads = pl.pallas_call(
        functools.partial(spread_kernel, (BLK * 128) ** (-0.5)),
        name="spread",
        out_shape=(
            shape(WIDTH, 4 * WIDTH, dtype=F32), shape(WIDTH, WIDTH, dtype=F32),
            shape(BLK, WIDTH), shape(BLK, WIDTH),
        ),
        in_specs=[VM] * 3,
        out_specs=(HBM,) * 4,
        scratch_shapes=[
            pltpu.VMEM((UNITS, WIDTH, WIDTH), F32),
            pltpu.SemaphoreType.DMA((7,)),
        ],
        compiler_params=params(),
    )(sums, layer_out, row_grads)
    return (layer_out, row_grads, proj_grad, out_grad)


def solution(mesh):
    placed = (
        P(("dp", "ctx"), None),
        P(("dp", "ctx")),
        P(("dp", "ctx")),
        P("dp", None),
        P(),
        P(),
        P(("dp", "ctx"), None),
    )
    return jax.shard_map(
        local,
        mesh=mesh,
        in_specs=placed,
        out_specs=(P(("dp", "ctx"), None), P(("dp", "ctx"), None), P(), P()),
        check_vma=False,
    )
```

```python
import functools

import jax
import jax.numpy as jnp
from jax import lax
from jax.experimental import pallas as pl
from jax.experimental.pallas import tpu as pltpu
from jax.sharding import PartitionSpec as P

MESH = pl.DeviceIdType.MESH
F32 = jnp.float32
BF16 = jnp.bfloat16
norm_eps = 1e-05
VMEM_LIMIT = 32 * 2**20

NCTX = 8
HALF = 128
BLK = 256
NB = 8
WIDTH = 512
HD = 64
EVENTS = 2048
UNITS = 5
ORDERS = ("zxy", "zyx", "xyz", "yzx", "zxy")
BACK = ("zxy", "zyx", "zyx", "xzy", "yxz")


def normalize(values):
    centre = values - jnp.mean(values, axis=-1, keepdims=True)
    inverse = lax.rsqrt(jnp.mean(centre * centre, axis=-1, keepdims=True) + norm_eps)
    return (centre * inverse, inverse)


def normalize_back(grad_in, normed, inverse):
    mean_grad = jnp.mean(grad_in, axis=-1, keepdims=True)
    mean_cross = jnp.mean(grad_in * normed, axis=-1, keepdims=True)
    return (grad_in - mean_grad - normed * mean_cross) * inverse


def silu(z):
    h = 0.5 * z
    return h + h * jnp.tanh(h)


def silu_grad(z):
    h = 0.5 * z
    u = 1.0 + jnp.tanh(h)
    return 0.5 * (u + h * u * (2.0 - u))


def dot(a, b):
    return lax.dot_general(a, b, (((1,), (0,)), ((), ())), preferred_element_type=F32)


def dot_nt(a, b):
    return lax.dot_general(a, b, (((1,), (1,)), ((), ())), preferred_element_type=F32)


def low(a, b):
    return jnp.concatenate([a[:, :HD], b[:, :HD]], axis=1)


def high(a, b):
    return jnp.concatenate([a[:, HD:], b[:, HD:]], axis=1)


def mod(a, n):
    return lax.rem(a + n, n)


def third(a):
    return (a * 21846) >> 16


def greet_ctx():
    cx = lax.axis_index("ctx")
    dp = lax.axis_index("dp")
    sem = pltpu.get_barrier_semaphore()
    for rel in range(1, NCTX):
        pl.semaphore_signal(
            sem, inc=1, device_id=(dp, lax.rem(cx + rel, NCTX)), device_id_type=MESH
        )
    return sem


def arrive_kernel(
    rows_hbm, sslot_hbm, aslot_hbm, w_hbm,
    own_ref, normed_ref, upd_ref, qk_ref, v_ref,
    rows_ref, sslot_ref, aslot_ref, w_ref,
    out, recv, hot_ref, qk_msg, v_msg, row_sems, send_sems, recv_sems, local_sems, in_sems,
):
    dp, cx = lax.axis_index("dp"), lax.axis_index("ctx")
    me = dp * NCTX + cx
    ndev = 128
    loads = [
        pltpu.make_async_copy(src, dst, in_sems.at[n])
        for n, (src, dst) in enumerate(
            ((rows_hbm, rows_ref), (sslot_hbm, sslot_ref), (aslot_hbm, aslot_ref), (w_hbm, w_ref))
        )
    ]
    for load in loads:
        load.start()

    def device(rel):
        d = (me + rel) & (ndev - 1)
        return (d >> 3, d & (NCTX - 1))

    barrier = pltpu.get_barrier_semaphore()

    def greet(rel, carry):
        pl.semaphore_signal(barrier, inc=1, device_id=device(rel), device_id_type=MESH)
        return carry

    lax.fori_loop(1, ndev, greet, 0, unroll=6)

    for load in loads[:3]:
        load.wait()
    rows = rows_ref[...]
    rows4 = jnp.concatenate([rows[:, q * 128 : q * 128 + 128] for q in range(4)], axis=0)
    slot = sslot_ref[...]
    to = third(slot)
    place = ((to - me) & (ndev - 1)) * 16 + (slot - 3 * to)
    target = jnp.concatenate([place + 4 * q for q in range(4)], axis=1)
    seen = lax.broadcasted_iota(jnp.int32, (BLK, 1024), 0)

    def pack(n, carry):
        hot = jnp.where(seen == target - n * BLK, 1.0, 0.0).astype(BF16)
        part = dot(hot, rows4).astype(BF16)
        out[pl.ds(n * 16, 16)] = part.reshape(16, 16, 128)
        return carry

    lax.fori_loop(0, 8, pack, 0)

    pl.semaphore_wait(barrier, ndev - 1)

    def send(rel, carry):
        pltpu.make_async_remote_copy(
            src_ref=out.at[rel],
            dst_ref=recv.at[rel],
            send_sem=row_sems.at[0],
            recv_sem=row_sems.at[1],
            device_id=device(rel),
            device_id_type=MESH,
        ).start()
        return carry

    lax.fori_loop(1, ndev, send, 0, unroll=6)
    recv[0] = out[0]
    all_rows = pltpu.make_async_remote_copy(
        src_ref=out.at[pl.ds(1, ndev - 1)],
        dst_ref=recv.at[pl.ds(1, ndev - 1)],
        send_sem=row_sems.at[0],
        recv_sem=row_sems.at[1],
        device_id=(dp, cx),
        device_id_type=MESH,
    )
    aslot = jnp.transpose(jnp.broadcast_to(aslot_ref[...], (128, BLK)))[:, :1]
    come = third(aslot)
    picked = ((me - come) & (ndev - 1)) * 16 + (aslot - 3 * come)
    lanes = lax.broadcasted_iota(jnp.int32, (BLK, EVENTS), 1)
    for q in range(4):
        hot_ref[q] = jnp.where(lanes == picked + 4 * q, 1.0, 0.0).astype(BF16)
    loads[3].wait()
    all_rows.wait()

    got = recv[...].reshape(EVENTS, 128)
    own = jnp.concatenate([dot(hot_ref[q], got) for q in range(4)], axis=1)
    own_ref[...] = own.astype(BF16)
    normed = normalize(own)[0].astype(BF16)
    normed_ref[...] = normed

    query = (silu(dot(normed, w_ref[:, 1024:1536])).astype(BF16).astype(F32) * 0.0625).astype(BF16)
    key = silu(dot(normed, w_ref[:, 1536:2048])).astype(BF16)
    for a in range(4):
        x, y = query[:, a * 128 : a * 128 + 128], key[:, a * 128 : a * 128 + 128]
        qk_msg[2 * a] = low(x, y).reshape(2, HALF, 128)
        qk_msg[2 * a + 1] = high(x, y).reshape(2, HALF, 128)

    def to_head(peer, rel, n):
        if n < 2:
            src, dst = qk_msg.at[peer, n], qk_ref.at[cx if n == 0 else 15 - cx]
        else:
            src, dst = v_msg.at[peer], v_ref.at[cx]
        if rel == 0:
            return pltpu.make_async_copy(src, dst, local_sems.at[n])
        return pltpu.make_async_remote_copy(
            src_ref=src,
            dst_ref=dst,
            send_sem=send_sems.at[rel, n],
            recv_sem=recv_sems.at[rel, n],
            device_id=(dp, peer),
            device_id_type=MESH,
        )

    copies = []
    for rel in range(NCTX):
        peer = lax.rem(cx + rel, NCTX)
        for n in range(2):
            copies.append(to_head(peer, rel, n))
            copies[-1].start()

    value = silu(dot(normed, w_ref[:, 512:1024])).astype(BF16)
    for a in range(4):
        x = value[:HALF, a * 128 : a * 128 + 128]
        y = value[HALF:, a * 128 : a * 128 + 128]
        v_msg[2 * a] = low(x, y)
        v_msg[2 * a + 1] = high(x, y)
    for rel in range(NCTX):
        copies.append(to_head(lax.rem(cx + rel, NCTX), rel, 2))
        copies[-1].start()

    upd_ref[...] = silu(dot(normed, w_ref[:, :512])).astype(BF16)
    for copy in copies:
        copy.wait()


def timeline_ends(len_ref):
    ends, total = [], 0
    for n in range(4):
        total = total + len_ref[0, n]
        ends.append(total)
    return ends


def start_of(positions, ends):
    first = jnp.zeros_like(positions)
    for n in range(3):
        first = jnp.where(positions >= ends[n], ends[n], first)
    return first


def end_of(position, ends):
    last = ends[3]
    for n in (2, 1, 0):
        last = jnp.where(position < ends[n], ends[n], last)
    return last


def in_position_order(packed, dst):
    for c in range(NCTX):
        block = packed[c]
        dst[c * HALF : (c + 1) * HALF, :] = block[:, :HD]
        dst[(15 - c) * HALF : (16 - c) * HALF, :] = block[:, HD:]


def by_owner(blocks, c):
    return jnp.concatenate(
        [blocks[c * HALF : (c + 1) * HALF, :], blocks[(15 - c) * HALF : (16 - c) * HALF, :]], axis=1
    )


def backward_kernel(
    len_ref, qk_ref, v_ref, ga_ref, g_ref, q, qt, k, kt, v, ga, gat, gqt, gk, gv
):
    ends = timeline_ends(len_ref)
    qk = qk_ref[...].reshape(EVENTS, 128)
    q[...] = qk[:, :HD]
    k[...] = qk[:, HD:]
    qkt = jnp.transpose(qk)
    qt[...] = qkt[:HD]
    kt[...] = qkt[HD:]
    in_position_order(v_ref, v)
    in_position_order(ga_ref, ga)
    gat[...] = jnp.transpose(ga[...])
    gqt[...] = jnp.zeros_like(gqt)
    gk[...] = jnp.zeros_like(gk)
    gv[...] = jnp.zeros_like(gv)

    t = lax.broadcasted_iota(jnp.int32, (BLK, BLK), 0)
    p = lax.broadcasted_iota(jnp.int32, (1, BLK), 1)

    def blocks(i, keys_of):
        rows = slice(i * BLK, (i + 1) * BLK)
        first = start_of(p + i * BLK, ends)
        query, parts = 0.0, []
        for j in keys_of:
            keys = slice(j * BLK, (j + 1) * BLK)
            allowed = t >= first - j * BLK
            if j == i:
                allowed = allowed & (t <= p)
            h = dot(k[keys, :], qt[:, rows])
            u = 1.0 + jnp.tanh(h)
            w = h * u
            e = dot(v[keys, :], gat[:, rows]) * (u + w * (2.0 - u))
            w = jnp.where(allowed, w, 0.0).astype(BF16)
            e = jnp.where(allowed, e, 0.0).astype(BF16)
            query = query + dot(kt[:, keys], e)
            parts.append((keys, dot(e, q[rows, :]), dot(w, ga[rows, :])))
        gqt[:, rows] += query
        for keys, key, value in parts:
            gk[keys, :] += key
            gv[keys, :] += value

    for i in range(NB):
        lowest = start_of(jnp.int32(i * BLK), ends) >> 8
        blocks(i, range(i, max(i - 3, -1), -1))
        for top in range(i - 3, -1, -3):
            pl.when(lowest <= top)(
                functools.partial(blocks, i, range(top, max(top - 3, -1), -1))
            )

    gq = jnp.transpose(gqt[...] * 0.0625).astype(BF16)
    gk_done, gv_done = gk[...].astype(BF16), gv[...].astype(BF16)
    for c in range(NCTX):
        g_ref[c, 0] = by_owner(gv_done, c)
        g_ref[c, 1] = by_owner(gq, c)
        g_ref[c, 2] = by_owner(gk_done, c)


def exchange(src, dst, sems, base=0):
    dp, cx = lax.axis_index("dp"), lax.axis_index("ctx")
    copies = []
    for rel in range(NCTX):
        peer = lax.rem(cx + rel, NCTX)
        if rel == 0:
            copy = pltpu.make_async_copy(src.at[peer], dst.at[cx], sems.at[base])
        else:
            copy = pltpu.make_async_remote_copy(
                src_ref=src.at[peer],
                dst_ref=dst.at[cx],
                send_sem=sems.at[base + rel],
                recv_sem=sems.at[base + NCTX + rel],
                device_id=(dp, peer),
                device_id_type=MESH,
            )
        copy.start()
        copies.append(copy)
    return copies


def gather_heads(parts):
    first = [low(parts[2 * a], parts[2 * a + 1]) for a in range(4)]
    second = [high(parts[2 * a], parts[2 * a + 1]) for a in range(4)]
    return jnp.concatenate(
        [jnp.concatenate(first, axis=1), jnp.concatenate(second, axis=1)], axis=0
    )


def forward_kernel(
    len_ref, qk_ref, v_ref, own_ref, upd_ref, cot_hbm, wo_hbm,
    layer_ref, gu_ref, outterm_ref, ga_ref,
    qt, k, v, vt, att_msg, cot_ref, wo_ref, att_in, ga_msg, sems, in_sems,
):
    dp, cx = lax.axis_index("dp"), lax.axis_index("ctx")
    loads = [
        pltpu.make_async_copy(cot_hbm, cot_ref, in_sems.at[0]),
        pltpu.make_async_copy(wo_hbm, wo_ref, in_sems.at[1]),
    ]
    for load in loads:
        load.start()
    barrier = greet_ctx()
    ends = timeline_ends(len_ref)
    qk = qk_ref[...].reshape(EVENTS, 128)
    k[...] = qk[:, HD:]
    qt[...] = jnp.transpose(qk)[:HD, :]
    in_position_order(v_ref, v)
    vt[...] = jnp.transpose(v[...])
    t = lax.broadcasted_iota(jnp.int32, (BLK, BLK), 0)
    p = lax.broadcasted_iota(jnp.int32, (1, BLK), 1)

    def to_owner(c):
        far = pltpu.make_async_remote_copy(
            src_ref=att_msg.at[c],
            dst_ref=att_in.at[cx],
            send_sem=sems.at[c],
            recv_sem=sems.at[NCTX + cx],
            device_id=(dp, c),
            device_id_type=MESH,
        )
        return far, pltpu.make_async_copy(att_msg.at[c], att_in.at[cx], sems.at[c])

    pl.semaphore_wait(barrier, NCTX - 1)

    def step(n, carry):
        block = (n + (cx >> 1)) & 3
        near_sum = jnp.zeros((HD, BLK), F32)
        far_sum = jnp.zeros((HD, BLK), F32)
        for m in range(9):
            second = m > block
            i = jnp.where(second, 7 - block, block)
            j = jnp.where(second, m - block - 1, m)
            rows = pl.ds(pl.multiple_of(i * BLK, BLK), BLK)
            keys = pl.ds(pl.multiple_of(j * BLK, BLK), BLK)
            h = dot(k[keys, :], qt[:, rows])
            w = h + h * jnp.tanh(h)
            first = start_of(p + i * BLK, ends) - j * BLK
            w = jnp.where((t >= first) & (t <= p + (i - j) * BLK), w, 0.0).astype(BF16)
            part = dot(vt[:, keys], w)
            if m == 0:
                near_sum = part
            elif m > 3:
                far_sum = far_sum + part
            else:
                near_sum = near_sum + jnp.where(second, 0.0, part)
                far_sum = far_sum + jnp.where(second, part, 0.0)
        near_rows = jnp.transpose(near_sum).astype(BF16)
        far_rows = jnp.transpose(far_sum).astype(BF16)
        for e in range(2):
            c = 2 * block + e
            att_msg[c] = jnp.concatenate(
                [near_rows[e * HALF : e * HALF + HALF], far_rows[HALF - e * HALF : BLK - e * HALF]], axis=1
            )
            far, near = to_owner(c)

            @pl.when(c != cx)
            def _():
                far.start()

            @pl.when(c == cx)
            def _():
                near.start()

        return carry

    lax.fori_loop(0, 4, step, 0)
    for load in loads:
        load.wait()
    cot = cot_ref[...]
    wo = wo_ref[...]
    grad_gated = dot_nt(cot, wo)
    to_owner(cx)[1].wait()
    for rel in range(1, NCTX):
        h = (cx + rel) & (NCTX - 1)
        to_owner(h)[0].wait_send()
        pltpu.make_async_remote_copy(
            src_ref=att_msg.at[h],
            dst_ref=att_in.at[h],
            send_sem=sems.at[h],
            recv_sem=sems.at[NCTX + h],
            device_id=(dp, h),
            device_id_type=MESH,
        ).wait_recv()
    update = upd_ref[...].astype(F32)
    attended = gather_heads([att_in[h].astype(F32) for h in range(NCTX)])
    att_normed, inverse = normalize(attended)
    grad_att = normalize_back(grad_gated * update, att_normed, inverse).astype(BF16)
    for a in range(4):
        x = grad_att[:HALF, a * 128 : a * 128 + 128]
        y = grad_att[HALF:, a * 128 : a * 128 + 128]
        ga_msg[2 * a] = low(x, y)
        ga_msg[2 * a + 1] = high(x, y)
    copies = exchange(ga_msg, ga_ref, sems, 2 * NCTX)
    gated = (att_normed * update).astype(BF16)
    layer_ref[...] = (own_ref[...].astype(F32) + dot(gated, wo)).astype(BF16)
    outterm_ref[...] = dot(jnp.transpose(gated), cot)
    gu_ref[...] = grad_gated * att_normed
    for copy in copies:
        copy.wait()


def final_kernel(
    g_ref, own_ref, normed_ref, w_ref, cot_ref, gu_ref, outterm_ref,
    rowgrad_ref, sum_ref,
    g_in, slope, acc, mine, core_in, out1, in1, out2, in2, out3, in3, sems, core_sems, axis_sems,
):
    dp, cx = lax.axis_index("dp"), lax.axis_index("ctx")
    core, xlo, z = lax.rem(dp, 2), lax.rem(dp // 2, 2), dp // 4
    xhi, y = lax.rem(cx, 2), cx // 2
    place = {"x": xhi * 2 + xlo, "y": y, "z": z}
    sibling = (dp + 1 - 2 * core, cx)

    def along(axis, r):
        c = lax.rem(place[axis] + r, 4)
        if axis == "x":
            return c, (z * 4 + lax.rem(c, 2) * 2 + core, y * 2 + c // 2)
        if axis == "y":
            return c, (dp, c * 2 + xhi)
        return c, (c * 4 + xlo * 2 + core, cx)

    barrier = greet_ctx()
    for device in [sibling] + [along(axis, r)[1] for axis in "xyz" for r in (1, 2, 3)]:
        pl.semaphore_signal(barrier, inc=1, device_id=device, device_id_type=MESH)

    def put(u, term):
        for n in range(4):
            part = term[:, n * 128 : n * 128 + 128].reshape(32, 16, 128)
            at = pl.ds(u * 64 + (n % 2) * 32, 32)
            acc[n // 2, at] = part
            mine[n // 2, at] = part.astype(BF16)

    def columns(block):
        return w_ref[:, block * WIDTH : (block + 1) * WIDTH]

    def unit_grads(u, block, grad, slope):
        grad_pre = (grad * slope).astype(BF16)
        put(u, dot(normed_t, grad_pre))
        return dot_nt(grad_pre, columns(block))

    def remote(src, dst, send_sem, recv_sem, device):
        copy = pltpu.make_async_remote_copy(
            src_ref=src, dst_ref=dst, send_sem=send_sem, recv_sem=recv_sem,
            device_id=device, device_id_type=MESH,
        )
        copy.start()
        return copy

    running = {}
    lead = (out1, out2, out3)
    landing = (in1, in2, in3)
    sizes = (16, 4, 1)
    base = [u * 64 for u in range(UNITS)]

    def core_start(u):
        at = pl.ds(u * 64, 64)
        running[u] = [
            remote(
                mine.at[1 - core, at], core_in.at[at], core_sems.at[0, u], core_sems.at[1, u], sibling
            )
        ]

    def finish(u):
        for copy in running.pop(u):
            copy.wait()

    def core_finish(u):
        finish(u)
        at = pl.ds(u * 64, 64)
        total = acc[core, at] + core_in[at].astype(F32)
        acc[core, at] = total
        out1[at] = total.astype(BF16)

    def axis_start(u, step):
        size = sizes[step]
        running[u] = []
        for r in (1, 2, 3):
            c, device = along(ORDERS[u][step], r)
            running[u].append(
                remote(
                    lead[step].at[pl.ds((u * 4 + c) * size, size)],
                    landing[step].at[r - 1, pl.ds(u * size, size)],
                    axis_sems.at[0, step, u, r], axis_sems.at[1, step, u, r], device,
                )
            )

    def axis_finish(u, step):
        finish(u)
        size = sizes[step]
        base[u] = base[u] + place[ORDERS[u][step]] * size
        total = acc[core, pl.ds(base[u], size)]
        for r in range(3):
            total = total + landing[step][r, pl.ds(u * size, size)].astype(F32)
        if step == 2:
            held[u] = [place[axis] for axis in ORDERS[u]]
            sum_ref[(core, u, *held[u])] = total.astype(BF16)[0]
        else:
            acc[core, pl.ds(base[u], size)] = total
            lead[step + 1][pl.ds(u * size, size)] = total.astype(BF16)

    held = {}

    def back_start(u, step):
        axis = BACK[u][step]
        part = sum_ref.at[(core, u, *held[u])]
        running[u] = [
            remote(
                part, part, axis_sems.at[2, step, u, r], axis_sems.at[3, step, u, r], along(axis, r)[1]
            )
            for r in (1, 2, 3)
        ]
        held[u][ORDERS[u].index(axis)] = slice(None)

    def core_back(u):
        part = sum_ref.at[core, u]
        running[u] = [remote(part, part, core_sems.at[2, u], core_sems.at[3, u], sibling)]

    def after_core(u):
        core_finish(u)
        axis_start(u, 0)

    def after_axis(u, step):
        axis_finish(u, step)
        if step < 2:
            axis_start(u, step + 1)
        else:
            back_start(u, 0)

    def after_back(u, step):
        finish(u)
        if step < 2:
            back_start(u, step + 1)
        else:
            core_back(u)

    pl.semaphore_wait(barrier, NCTX - 1 + 10)
    g_copies = []
    for n in range(3):
        for rel in range(NCTX):
            peer = (cx + rel) & (NCTX - 1)
            src, dst = g_ref.at[peer, n], g_in.at[cx, n]
            if rel == 0:
                g_copies.append(pltpu.make_async_copy(src, dst, sems.at[n, 0]))
                g_copies[-1].start()
            else:
                g_copies.append(
                    remote(src, dst, sems.at[n, rel], sems.at[n, NCTX + rel], (dp, peer))
                )

    own, cot = own_ref[...].astype(F32), cot_ref[...]
    normed, inverse = normalize(own)
    normed_bf = normed_ref[...]
    normed_t = jnp.transpose(normed_bf)
    put(1, outterm_ref[...])
    core_start(1)
    grad_normed = unit_grads(0, 0, gu_ref[...], silu_grad(dot(normed_bf, columns(0))))
    core_start(0)
    for n in range(3):
        slope[n] = silu_grad(dot(normed_bf, columns(n + 1)))

    def late(n, total):
        for copy in g_copies[n * NCTX : (n + 1) * NCTX]:
            copy.wait()
        grad = gather_heads([g_in[h, n].astype(F32) for h in range(NCTX)])
        total = total + unit_grads(n + 2, n + 1, grad, slope[n])
        core_start(n + 2)
        return total

    grad_normed = late(0, grad_normed)
    grad_normed = late(1, grad_normed)
    after_core(1)
    after_core(0)
    grad_normed = late(2, grad_normed)
    after_core(2)
    after_core(3)
    rowgrad_ref[...] = (
        cot.astype(F32) + normalize_back(grad_normed, normed, inverse)
    ).astype(BF16)
    after_core(4)
    after_axis(1, 0)
    after_axis(0, 0)
    after_axis(2, 0)
    after_axis(3, 0)
    after_axis(4, 0)
    after_axis(1, 1)
    after_axis(0, 1)
    after_axis(2, 1)
    after_axis(3, 1)
    after_axis(4, 1)
    after_axis(1, 2)
    after_axis(0, 2)
    after_axis(2, 2)
    after_axis(3, 2)
    after_axis(4, 2)
    after_back(1, 0)
    after_back(0, 0)
    after_back(2, 0)
    after_back(3, 0)
    after_back(4, 0)
    after_back(1, 1)
    after_back(0, 1)
    after_back(2, 1)
    after_back(3, 1)
    after_back(4, 1)
    after_back(1, 2)
    after_back(0, 2)
    after_back(2, 2)
    after_back(3, 2)
    after_back(4, 2)
    for u in range(UNITS):
        finish(u)


def spread_kernel(scale, sum_ref, layer_ref, rowgrad_ref, proj_hbm, out_hbm, layer_hbm, rowgrad_hbm, wide, sems):
    copies = [
        pltpu.make_async_copy(layer_ref, layer_hbm, sems.at[5]),
        pltpu.make_async_copy(rowgrad_ref, rowgrad_hbm, sems.at[6]),
    ]
    for copy in copies:
        copy.start()
    for u in range(UNITS):
        for n in range(4):
            at = (n % 2) * 2
            wide[u, :, n * 128 : n * 128 + 128] = (
                sum_ref[n // 2, u, at : at + 2].reshape(WIDTH, 128).astype(F32) * scale
            )
        block = (0, None, 1, 2, 3)[u]
        dst = out_hbm if block is None else proj_hbm.at[:, pl.ds(block * WIDTH, WIDTH)]
        copies.append(pltpu.make_async_copy(wide.at[u], dst, sems.at[u]))
        copies[-1].start()
    for copy in copies:
        copy.wait()


HBM = pl.BlockSpec(memory_space=pltpu.HBM)
VM = pl.BlockSpec(memory_space=pltpu.VMEM)
SM = pl.BlockSpec(memory_space=pltpu.SMEM)


def shape(*dims, dtype=BF16):
    return jax.ShapeDtypeStruct(dims, dtype)


def params(vmem_limit_bytes=VMEM_LIMIT, **kw):
    return pltpu.CompilerParams(vmem_limit_bytes=vmem_limit_bytes, **kw)


def in_hbm(array):
    return pltpu.with_memory_space_constraint(array, pltpu.HBM)


def local(loader_rows, send_slot, arrive_slot, user_lengths, proj_weight, out_weight, cotangent):
    own, normed, update, qk, v = pl.pallas_call(
        arrive_kernel,
        name="arrive",
        out_shape=(
            shape(BLK, WIDTH), shape(BLK, WIDTH), shape(BLK, WIDTH),
            shape(16, HALF, 128), shape(NCTX, HALF, 128),
        ),
        in_specs=[HBM] * 4,
        out_specs=(VM,) * 5,
        scratch_shapes=[
            pltpu.VMEM((BLK, WIDTH), BF16),
            pltpu.VMEM((1, BLK), jnp.int32),
            pltpu.VMEM((1, BLK), jnp.int32),
            pltpu.VMEM((WIDTH, 4 * WIDTH), BF16),
            pltpu.VMEM((128, 16, 128), BF16),
            pltpu.VMEM((128, 16, 128), BF16),
            pltpu.VMEM((4, BLK, EVENTS), BF16),
            pltpu.VMEM((NCTX, 2, HALF, 128), BF16),
            pltpu.VMEM((NCTX, HALF, 128), BF16),
            pltpu.SemaphoreType.DMA((2,)),
            pltpu.SemaphoreType.DMA((NCTX, 3)),
            pltpu.SemaphoreType.DMA((NCTX, 3)),
            pltpu.SemaphoreType.DMA((3,)),
            pltpu.SemaphoreType.DMA((4,)),
        ],
        compiler_params=params(collective_id=0, has_side_effects=True),
    )(
        *map(in_hbm, (loader_rows, send_slot.reshape(1, BLK), arrive_slot.reshape(1, BLK), proj_weight))
    )

    layer_out, grad_update, out_term, grad_att = pl.pallas_call(
        forward_kernel,
        name="forward",
        out_shape=(
            shape(BLK, WIDTH), shape(BLK, WIDTH, dtype=F32), shape(WIDTH, WIDTH, dtype=F32),
            shape(NCTX, HALF, 128),
        ),
        in_specs=[SM, VM, VM, VM, VM, HBM, HBM],
        out_specs=(VM,) * 4,
        scratch_shapes=[
            pltpu.VMEM((HD, EVENTS), BF16),
            pltpu.VMEM((EVENTS, HD), BF16),
            pltpu.VMEM((EVENTS, HD), BF16),
            pltpu.VMEM((HD, EVENTS), BF16),
            pltpu.VMEM((NCTX, HALF, 128), BF16),
            pltpu.VMEM((BLK, WIDTH), BF16),
            pltpu.VMEM((WIDTH, WIDTH), BF16),
            pltpu.VMEM((NCTX, HALF, 128), BF16),
            pltpu.VMEM((NCTX, HALF, 128), BF16),
            pltpu.SemaphoreType.DMA((4 * NCTX,)),
            pltpu.SemaphoreType.DMA((2,)),
        ],
        compiler_params=params(collective_id=1, has_side_effects=True),
    )(in_hbm(user_lengths), qk, v, own, update, in_hbm(cotangent), in_hbm(out_weight))

    grads = pl.pallas_call(
        backward_kernel,
        name="attend_back",
        out_shape=shape(NCTX, 3, HALF, 128),
        in_specs=[SM, VM, VM, VM],
        out_specs=VM,
        scratch_shapes=[
            pltpu.VMEM((EVENTS, HD), BF16),
            pltpu.VMEM((HD, EVENTS), BF16),
            pltpu.VMEM((EVENTS, HD), BF16),
            pltpu.VMEM((HD, EVENTS), BF16),
            pltpu.VMEM((EVENTS, HD), BF16),
            pltpu.VMEM((EVENTS, HD), BF16),
            pltpu.VMEM((HD, EVENTS), BF16),
            pltpu.VMEM((HD, EVENTS), F32),
            pltpu.VMEM((EVENTS, HD), F32),
            pltpu.VMEM((EVENTS, HD), F32),
        ],
        compiler_params=params(),
    )(in_hbm(user_lengths), qk, v, grad_att)

    row_grads, sums = pl.pallas_call(
        final_kernel,
        name="final",
        out_shape=(shape(BLK, WIDTH), shape(2, UNITS, 4, 4, 4, 16, 128)),
        in_specs=[VM] * 7,
        out_specs=(VM,) * 2,
        scratch_shapes=[
            pltpu.VMEM((NCTX, 3, HALF, 128), BF16),
            pltpu.VMEM((3, BLK, WIDTH), F32),
            pltpu.VMEM((2, UNITS * 64, 16, 128), F32),
            pltpu.VMEM((2, UNITS * 64, 16, 128), BF16),
            pltpu.VMEM((UNITS * 64, 16, 128), BF16),
            pltpu.VMEM((UNITS * 64, 16, 128), BF16),
            pltpu.VMEM((3, UNITS * 16, 16, 128), BF16),
            pltpu.VMEM((UNITS * 16, 16, 128), BF16),
            pltpu.VMEM((3, UNITS * 4, 16, 128), BF16),
            pltpu.VMEM((UNITS * 4, 16, 128), BF16),
            pltpu.VMEM((3, UNITS, 16, 128), BF16),
            pltpu.SemaphoreType.DMA((3, 2 * NCTX)),
            pltpu.SemaphoreType.DMA((4, UNITS)),
            pltpu.SemaphoreType.DMA((4, 3, UNITS, 4)),
        ],
        compiler_params=params(collective_id=2, has_side_effects=True),
    )(grads, own, normed, proj_weight, cotangent, grad_update, out_term)

    proj_grad, out_grad, layer_out, row_grads = pl.pallas_call(
        functools.partial(spread_kernel, (BLK * 128) ** (-0.5)),
        name="spread",
        out_shape=(
            shape(WIDTH, 4 * WIDTH, dtype=F32), shape(WIDTH, WIDTH, dtype=F32),
            shape(BLK, WIDTH), shape(BLK, WIDTH),
        ),
        in_specs=[VM] * 3,
        out_specs=(HBM,) * 4,
        scratch_shapes=[
            pltpu.VMEM((UNITS, WIDTH, WIDTH), F32),
            pltpu.SemaphoreType.DMA((7,)),
        ],
        compiler_params=params(),
    )(sums, layer_out, row_grads)
    return (layer_out, row_grads, proj_grad, out_grad)


def solution(mesh):
    placed = (
        P(("dp", "ctx"), None),
        P(("dp", "ctx")),
        P(("dp", "ctx")),
        P("dp", None),
        P(),
        P(),
        P(("dp", "ctx"), None),
    )
    return jax.shard_map(
        local,
        mesh=mesh,
        in_specs=placed,
        out_specs=(P(("dp", "ctx"), None), P(("dp", "ctx"), None), P(), P()),
        check_vma=False,
    )
```

```python
import functools

import jax
import jax.numpy as jnp
from jax import lax
from jax.experimental import pallas as pl
from jax.experimental.pallas import tpu as pltpu
from jax.sharding import PartitionSpec as P

MESH = pl.DeviceIdType.MESH
F32 = jnp.float32
BF16 = jnp.bfloat16
norm_eps = 1e-05
VMEM_LIMIT = 32 * 2**20

NCTX = 8
HALF = 128
BLK = 256
NB = 8
WIDTH = 512
HD = 64
EVENTS = 2048
UNITS = 5
ORDERS = ("zxy", "zyx", "xyz", "yzx", "zxy")
BACK = ("zxy", "zyx", "zyx", "xzy", "yxz")


def normalize(values):
    centre = values - jnp.mean(values, axis=-1, keepdims=True)
    inverse = lax.rsqrt(jnp.mean(centre * centre, axis=-1, keepdims=True) + norm_eps)
    return (centre * inverse, inverse)


def normalize_back(grad_in, normed, inverse):
    mean_grad = jnp.mean(grad_in, axis=-1, keepdims=True)
    mean_cross = jnp.mean(grad_in * normed, axis=-1, keepdims=True)
    return (grad_in - mean_grad - normed * mean_cross) * inverse


def silu(z):
    h = 0.5 * z
    return h + h * jnp.tanh(h)


def silu_grad(z):
    h = 0.5 * z
    u = 1.0 + jnp.tanh(h)
    return 0.5 * (u + h * u * (2.0 - u))


def dot(a, b):
    return lax.dot_general(a, b, (((1,), (0,)), ((), ())), preferred_element_type=F32)


def dot_nt(a, b):
    return lax.dot_general(a, b, (((1,), (1,)), ((), ())), preferred_element_type=F32)


def low(a, b):
    return jnp.concatenate([a[:, :HD], b[:, :HD]], axis=1)


def high(a, b):
    return jnp.concatenate([a[:, HD:], b[:, HD:]], axis=1)


def mod(a, n):
    return lax.rem(a + n, n)


def third(a):
    return (a * 21846) >> 16


def greet_ctx():
    cx = lax.axis_index("ctx")
    dp = lax.axis_index("dp")
    sem = pltpu.get_barrier_semaphore()
    for rel in range(1, NCTX):
        pl.semaphore_signal(
            sem, inc=1, device_id=(dp, lax.rem(cx + rel, NCTX)), device_id_type=MESH
        )
    return sem


def arrive_kernel(
    rows_hbm, sslot_hbm, aslot_hbm, w_hbm,
    own_ref, normed_ref, upd_ref, qk_ref, v_ref,
    rows_ref, sslot_ref, aslot_ref, w_ref,
    out, recv, hot_ref, qk_msg, v_msg, row_sems, send_sems, recv_sems, local_sems, in_sems,
):
    dp, cx = lax.axis_index("dp"), lax.axis_index("ctx")
    me = dp * NCTX + cx
    ndev = 128
    loads = [
        pltpu.make_async_copy(src, dst, in_sems.at[n])
        for n, (src, dst) in enumerate(
            ((rows_hbm, rows_ref), (sslot_hbm, sslot_ref), (aslot_hbm, aslot_ref), (w_hbm, w_ref))
        )
    ]
    for load in loads:
        load.start()

    def device(rel):
        d = (me + rel) & (ndev - 1)
        return (d >> 3, d & (NCTX - 1))

    barrier = pltpu.get_barrier_semaphore()

    def greet(rel, carry):
        pl.semaphore_signal(barrier, inc=1, device_id=device(rel), device_id_type=MESH)
        return carry

    lax.fori_loop(1, ndev, greet, 0, unroll=6)

    for load in loads[:3]:
        load.wait()
    rows = rows_ref[...]
    rows4 = jnp.concatenate([rows[:, q * 128 : q * 128 + 128] for q in range(4)], axis=0)
    slot = sslot_ref[...]
    to = third(slot)
    place = ((to - me) & (ndev - 1)) * 16 + (slot - 3 * to)
    target = jnp.concatenate([place + 4 * q for q in range(4)], axis=1)
    seen = lax.broadcasted_iota(jnp.int32, (BLK, 1024), 0)

    def pack(n, carry):
        hot = jnp.where(seen == target - n * BLK, 1.0, 0.0).astype(BF16)
        part = dot(hot, rows4).astype(BF16)
        out[pl.ds(n * 16, 16)] = part.reshape(16, 16, 128)
        return carry

    lax.fori_loop(0, 8, pack, 0)

    pl.semaphore_wait(barrier, ndev - 1)

    def send(rel, carry):
        pltpu.make_async_remote_copy(
            src_ref=out.at[rel],
            dst_ref=recv.at[rel],
            send_sem=row_sems.at[0],
            recv_sem=row_sems.at[1],
            device_id=device(rel),
            device_id_type=MESH,
        ).start()
        return carry

    lax.fori_loop(1, ndev, send, 0, unroll=6)
    recv[0] = out[0]
    all_rows = pltpu.make_async_remote_copy(
        src_ref=out.at[pl.ds(1, ndev - 1)],
        dst_ref=recv.at[pl.ds(1, ndev - 1)],
        send_sem=row_sems.at[0],
        recv_sem=row_sems.at[1],
        device_id=(dp, cx),
        device_id_type=MESH,
    )
    aslot = jnp.transpose(jnp.broadcast_to(aslot_ref[...], (128, BLK)))[:, :1]
    come = third(aslot)
    picked = ((me - come) & (ndev - 1)) * 16 + (aslot - 3 * come)
    lanes = lax.broadcasted_iota(jnp.int32, (BLK, EVENTS), 1)
    for q in range(4):
        hot_ref[q] = jnp.where(lanes == picked + 4 * q, 1.0, 0.0).astype(BF16)
    loads[3].wait()
    all_rows.wait()

    got = recv[...].reshape(EVENTS, 128)
    own = jnp.concatenate([dot(hot_ref[q], got) for q in range(4)], axis=1)
    own_ref[...] = own.astype(BF16)
    normed = normalize(own)[0].astype(BF16)
    normed_ref[...] = normed

    query = (silu(dot(normed, w_ref[:, 1024:1536])).astype(BF16).astype(F32) * 0.0625).astype(BF16)
    key = silu(dot(normed, w_ref[:, 1536:2048])).astype(BF16)
    for a in range(4):
        x, y = query[:, a * 128 : a * 128 + 128], key[:, a * 128 : a * 128 + 128]
        qk_msg[2 * a] = low(x, y).reshape(2, HALF, 128)
        qk_msg[2 * a + 1] = high(x, y).reshape(2, HALF, 128)

    def to_head(peer, rel, n):
        if n < 2:
            src, dst = qk_msg.at[peer, n], qk_ref.at[cx if n == 0 else 15 - cx]
        else:
            src, dst = v_msg.at[peer], v_ref.at[cx]
        if rel == 0:
            return pltpu.make_async_copy(src, dst, local_sems.at[n])
        return pltpu.make_async_remote_copy(
            src_ref=src,
            dst_ref=dst,
            send_sem=send_sems.at[rel, n],
            recv_sem=recv_sems.at[rel, n],
            device_id=(dp, peer),
            device_id_type=MESH,
        )

    copies = []
    for rel in range(NCTX):
        peer = lax.rem(cx + rel, NCTX)
        for n in range(2):
            copies.append(to_head(peer, rel, n))
            copies[-1].start()

    value = silu(dot(normed, w_ref[:, 512:1024])).astype(BF16)
    for a in range(4):
        x = value[:HALF, a * 128 : a * 128 + 128]
        y = value[HALF:, a * 128 : a * 128 + 128]
        v_msg[2 * a] = low(x, y)
        v_msg[2 * a + 1] = high(x, y)
    for rel in range(NCTX):
        copies.append(to_head(lax.rem(cx + rel, NCTX), rel, 2))
        copies[-1].start()

    upd_ref[...] = silu(dot(normed, w_ref[:, :512])).astype(BF16)
    for copy in copies:
        copy.wait()


def timeline_ends(len_ref):
    ends, total = [], 0
    for n in range(4):
        total = total + len_ref[0, n]
        ends.append(total)
    return ends


def start_of(positions, ends):
    first = jnp.zeros_like(positions)
    for n in range(3):
        first = jnp.where(positions >= ends[n], ends[n], first)
    return first


def end_of(position, ends):
    last = ends[3]
    for n in (2, 1, 0):
        last = jnp.where(position < ends[n], ends[n], last)
    return last


def in_position_order(packed, dst):
    for c in range(NCTX):
        block = packed[c]
        dst[c * HALF : (c + 1) * HALF, :] = block[:, :HD]
        dst[(15 - c) * HALF : (16 - c) * HALF, :] = block[:, HD:]


def by_owner(blocks, c):
    return jnp.concatenate(
        [blocks[c * HALF : (c + 1) * HALF, :], blocks[(15 - c) * HALF : (16 - c) * HALF, :]], axis=1
    )


def backward_kernel(
    len_ref, qk_ref, v_ref, ga_ref, g_ref, q, qt, k, kt, v, ga, gat, gqt, gk, gv
):
    ends = timeline_ends(len_ref)
    qk = qk_ref[...].reshape(EVENTS, 128)
    q[...] = qk[:, :HD]
    k[...] = qk[:, HD:]
    qkt = jnp.transpose(qk)
    qt[...] = qkt[:HD]
    kt[...] = qkt[HD:]
    in_position_order(v_ref, v)
    in_position_order(ga_ref, ga)
    gat[...] = jnp.transpose(ga[...])
    gqt[...] = jnp.zeros_like(gqt)
    gk[...] = jnp.zeros_like(gk)
    gv[...] = jnp.zeros_like(gv)

    t = lax.broadcasted_iota(jnp.int32, (BLK, BLK), 0)
    p = lax.broadcasted_iota(jnp.int32, (1, BLK), 1)

    def blocks(i, keys_of):
        rows = slice(i * BLK, (i + 1) * BLK)
        first = start_of(p + i * BLK, ends)
        query, parts = 0.0, []
        for j in keys_of:
            keys = slice(j * BLK, (j + 1) * BLK)
            allowed = t >= first - j * BLK
            if j == i:
                allowed = allowed & (t <= p)
            h = dot(k[keys, :], qt[:, rows])
            u = 1.0 + jnp.tanh(h)
            w = h * u
            e = dot(v[keys, :], gat[:, rows]) * (u + w * (2.0 - u))
            w = jnp.where(allowed, w, 0.0).astype(BF16)
            e = jnp.where(allowed, e, 0.0).astype(BF16)
            query = query + dot(kt[:, keys], e)
            parts.append((keys, dot(e, q[rows, :]), dot(w, ga[rows, :])))
        gqt[:, rows] += query
        for keys, key, value in parts:
            gk[keys, :] += key
            gv[keys, :] += value

    for i in range(NB):
        lowest = start_of(jnp.int32(i * BLK), ends) >> 8
        blocks(i, range(i, max(i - 3, -1), -1))
        for top in range(i - 3, -1, -3):
            pl.when(lowest <= top)(
                functools.partial(blocks, i, range(top, max(top - 3, -1), -1))
            )

    gq = jnp.transpose(gqt[...] * 0.0625).astype(BF16)
    gk_done, gv_done = gk[...].astype(BF16), gv[...].astype(BF16)
    for c in range(NCTX):
        g_ref[c, 0] = by_owner(gv_done, c)
        g_ref[c, 1] = by_owner(gq, c)
        g_ref[c, 2] = by_owner(gk_done, c)


def exchange(src, dst, sems, base=0):
    dp, cx = lax.axis_index("dp"), lax.axis_index("ctx")
    copies = []
    for rel in range(NCTX):
        peer = lax.rem(cx + rel, NCTX)
        if rel == 0:
            copy = pltpu.make_async_copy(src.at[peer], dst.at[cx], sems.at[base])
        else:
            copy = pltpu.make_async_remote_copy(
                src_ref=src.at[peer],
                dst_ref=dst.at[cx],
                send_sem=sems.at[base + rel],
                recv_sem=sems.at[base + NCTX + rel],
                device_id=(dp, peer),
                device_id_type=MESH,
            )
        copy.start()
        copies.append(copy)
    return copies


def gather_heads(parts):
    first = [low(parts[2 * a], parts[2 * a + 1]) for a in range(4)]
    second = [high(parts[2 * a], parts[2 * a + 1]) for a in range(4)]
    return jnp.concatenate(
        [jnp.concatenate(first, axis=1), jnp.concatenate(second, axis=1)], axis=0
    )


def forward_kernel(
    len_ref, qk_ref, v_ref, own_ref, upd_ref, cot_hbm, wo_hbm,
    layer_ref, gu_ref, outterm_ref, ga_ref,
    qt, k, v, vt, att_msg, cot_ref, wo_ref, att_in, ga_msg, sems, in_sems,
):
    dp, cx = lax.axis_index("dp"), lax.axis_index("ctx")
    loads = [
        pltpu.make_async_copy(cot_hbm, cot_ref, in_sems.at[0]),
        pltpu.make_async_copy(wo_hbm, wo_ref, in_sems.at[1]),
    ]
    for load in loads:
        load.start()
    barrier = greet_ctx()
    ends = timeline_ends(len_ref)
    qk = qk_ref[...].reshape(EVENTS, 128)
    k[...] = qk[:, HD:]
    qt[...] = jnp.transpose(qk)[:HD, :]
    in_position_order(v_ref, v)
    vt[...] = jnp.transpose(v[...])
    t = lax.broadcasted_iota(jnp.int32, (BLK, BLK), 0)
    p = lax.broadcasted_iota(jnp.int32, (1, BLK), 1)

    def to_owner(c):
        far = pltpu.make_async_remote_copy(
            src_ref=att_msg.at[c],
            dst_ref=att_in.at[cx],
            send_sem=sems.at[c],
            recv_sem=sems.at[NCTX + cx],
            device_id=(dp, c),
            device_id_type=MESH,
        )
        return far, pltpu.make_async_copy(att_msg.at[c], att_in.at[cx], sems.at[c])

    def step(n, carry):
        block = (n + (cx >> 1)) & 3
        near_sum = jnp.zeros((HD, BLK), F32)
        far_sum = jnp.zeros((HD, BLK), F32)
        for m in range(9):
            second = m > block
            i = jnp.where(second, 7 - block, block)
            j = jnp.where(second, m - block - 1, m)
            rows = pl.ds(pl.multiple_of(i * BLK, BLK), BLK)
            keys = pl.ds(pl.multiple_of(j * BLK, BLK), BLK)
            h = dot(k[keys, :], qt[:, rows])
            w = h + h * jnp.tanh(h)
            first = start_of(p + i * BLK, ends) - j * BLK
            w = jnp.where((t >= first) & (t <= p + (i - j) * BLK), w, 0.0).astype(BF16)
            part = dot(vt[:, keys], w)
            if m == 0:
                near_sum = part
            elif m > 3:
                far_sum = far_sum + part
            else:
                near_sum = near_sum + jnp.where(second, 0.0, part)
                far_sum = far_sum + jnp.where(second, part, 0.0)
        near_rows = jnp.transpose(near_sum).astype(BF16)
        far_rows = jnp.transpose(far_sum).astype(BF16)

        @pl.when(n == 0)
        def _():
            pl.semaphore_wait(barrier, NCTX - 1)

        for e in range(2):
            c = 2 * block + e
            att_msg[c] = jnp.concatenate(
                [near_rows[e * HALF : e * HALF + HALF], far_rows[HALF - e * HALF : BLK - e * HALF]], axis=1
            )
            far, near = to_owner(c)

            @pl.when(c != cx)
            def _():
                far.start()

            @pl.when(c == cx)
            def _():
                near.start()

        return carry

    lax.fori_loop(0, 4, step, 0)
    for load in loads:
        load.wait()
    cot = cot_ref[...]
    wo = wo_ref[...]
    grad_gated = dot_nt(cot, wo)
    to_owner(cx)[1].wait()
    for rel in range(1, NCTX):
        h = (cx + rel) & (NCTX - 1)
        to_owner(h)[0].wait_send()
        pltpu.make_async_remote_copy(
            src_ref=att_msg.at[h],
            dst_ref=att_in.at[h],
            send_sem=sems.at[h],
            recv_sem=sems.at[NCTX + h],
            device_id=(dp, h),
            device_id_type=MESH,
        ).wait_recv()
    update = upd_ref[...].astype(F32)
    attended = gather_heads([att_in[h].astype(F32) for h in range(NCTX)])
    att_normed, inverse = normalize(attended)
    grad_att = normalize_back(grad_gated * update, att_normed, inverse).astype(BF16)
    for a in range(4):
        x = grad_att[:HALF, a * 128 : a * 128 + 128]
        y = grad_att[HALF:, a * 128 : a * 128 + 128]
        ga_msg[2 * a] = low(x, y)
        ga_msg[2 * a + 1] = high(x, y)
    copies = exchange(ga_msg, ga_ref, sems, 2 * NCTX)
    gated = (att_normed * update).astype(BF16)
    layer_ref[...] = (own_ref[...].astype(F32) + dot(gated, wo)).astype(BF16)
    outterm_ref[...] = dot(jnp.transpose(gated), cot)
    gu_ref[...] = grad_gated * att_normed
    for copy in copies:
        copy.wait()


def final_kernel(
    g_ref, own_ref, normed_ref, w_ref, cot_ref, gu_ref, outterm_ref,
    rowgrad_ref, sum_ref,
    g_in, slope, acc, mine, core_in, out1, in1, out2, in2, out3, in3, sems, core_sems, axis_sems,
):
    dp, cx = lax.axis_index("dp"), lax.axis_index("ctx")
    core, xlo, z = lax.rem(dp, 2), lax.rem(dp // 2, 2), dp // 4
    xhi, y = lax.rem(cx, 2), cx // 2
    place = {"x": xhi * 2 + xlo, "y": y, "z": z}
    sibling = (dp + 1 - 2 * core, cx)

    def along(axis, r):
        c = lax.rem(place[axis] + r, 4)
        if axis == "x":
            return c, (z * 4 + lax.rem(c, 2) * 2 + core, y * 2 + c // 2)
        if axis == "y":
            return c, (dp, c * 2 + xhi)
        return c, (c * 4 + xlo * 2 + core, cx)

    barrier = greet_ctx()
    for device in [sibling] + [along(axis, r)[1] for axis in "xyz" for r in (1, 2, 3)]:
        pl.semaphore_signal(barrier, inc=1, device_id=device, device_id_type=MESH)

    def put(u, term):
        for n in range(4):
            part = term[:, n * 128 : n * 128 + 128].reshape(32, 16, 128)
            at = pl.ds(u * 64 + (n % 2) * 32, 32)
            acc[n // 2, at] = part
            mine[n // 2, at] = part.astype(BF16)

    def columns(block):
        return w_ref[:, block * WIDTH : (block + 1) * WIDTH]

    def unit_grads(u, block, grad, slope):
        grad_pre = (grad * slope).astype(BF16)
        put(u, dot(normed_t, grad_pre))
        return dot_nt(grad_pre, columns(block))

    def remote(src, dst, send_sem, recv_sem, device):
        copy = pltpu.make_async_remote_copy(
            src_ref=src, dst_ref=dst, send_sem=send_sem, recv_sem=recv_sem,
            device_id=device, device_id_type=MESH,
        )
        copy.start()
        return copy

    running = {}
    lead = (out1, out2, out3)
    landing = (in1, in2, in3)
    sizes = (16, 4, 1)
    base = [u * 64 for u in range(UNITS)]

    def core_start(u):
        at = pl.ds(u * 64, 64)
        running[u] = [
            remote(
                mine.at[1 - core, at], core_in.at[at], core_sems.at[0, u], core_sems.at[1, u], sibling
            )
        ]

    def finish(u):
        for copy in running.pop(u):
            copy.wait()

    def core_finish(u):
        finish(u)
        at = pl.ds(u * 64, 64)
        total = acc[core, at] + core_in[at].astype(F32)
        acc[core, at] = total
        out1[at] = total.astype(BF16)

    def axis_start(u, step):
        size = sizes[step]
        running[u] = []
        for r in (1, 2, 3):
            c, device = along(ORDERS[u][step], r)
            running[u].append(
                remote(
                    lead[step].at[pl.ds((u * 4 + c) * size, size)],
                    landing[step].at[r - 1, pl.ds(u * size, size)],
                    axis_sems.at[0, step, u, r], axis_sems.at[1, step, u, r], device,
                )
            )

    def axis_finish(u, step):
        finish(u)
        size = sizes[step]
        base[u] = base[u] + place[ORDERS[u][step]] * size
        total = acc[core, pl.ds(base[u], size)]
        for r in range(3):
            total = total + landing[step][r, pl.ds(u * size, size)].astype(F32)
        if step == 2:
            held[u] = [place[axis] for axis in ORDERS[u]]
            sum_ref[(core, u, *held[u])] = total.astype(BF16)[0]
        else:
            acc[core, pl.ds(base[u], size)] = total
            lead[step + 1][pl.ds(u * size, size)] = total.astype(BF16)

    held = {}

    def back_start(u, step):
        axis = BACK[u][step]
        part = sum_ref.at[(core, u, *held[u])]
        running[u] = [
            remote(
                part, part, axis_sems.at[2, step, u, r], axis_sems.at[3, step, u, r], along(axis, r)[1]
            )
            for r in (1, 2, 3)
        ]
        held[u][ORDERS[u].index(axis)] = slice(None)

    def core_back(u):
        part = sum_ref.at[core, u]
        running[u] = [remote(part, part, core_sems.at[2, u], core_sems.at[3, u], sibling)]

    def after_core(u):
        core_finish(u)
        axis_start(u, 0)

    def after_axis(u, step):
        axis_finish(u, step)
        if step < 2:
            axis_start(u, step + 1)
        else:
            back_start(u, 0)

    def after_back(u, step):
        finish(u)
        if step < 2:
            back_start(u, step + 1)
        else:
            core_back(u)

    pl.semaphore_wait(barrier, NCTX - 1 + 10)
    g_copies = []
    for n in range(3):
        for rel in range(NCTX):
            peer = (cx + rel) & (NCTX - 1)
            src, dst = g_ref.at[peer, n], g_in.at[cx, n]
            if rel == 0:
                g_copies.append(pltpu.make_async_copy(src, dst, sems.at[n, 0]))
                g_copies[-1].start()
            else:
                g_copies.append(
                    remote(src, dst, sems.at[n, rel], sems.at[n, NCTX + rel], (dp, peer))
                )

    own, cot = own_ref[...].astype(F32), cot_ref[...]
    normed, inverse = normalize(own)
    normed_bf = normed_ref[...]
    normed_t = jnp.transpose(normed_bf)
    put(1, outterm_ref[...])
    core_start(1)
    grad_normed = unit_grads(0, 0, gu_ref[...], silu_grad(dot(normed_bf, columns(0))))
    core_start(0)
    for n in range(3):
        slope[n] = silu_grad(dot(normed_bf, columns(n + 1)))

    def late(n, total):
        for copy in g_copies[n * NCTX : (n + 1) * NCTX]:
            copy.wait()
        grad = gather_heads([g_in[h, n].astype(F32) for h in range(NCTX)])
        total = total + unit_grads(n + 2, n + 1, grad, slope[n])
        core_start(n + 2)
        return total

    grad_normed = late(0, grad_normed)
    grad_normed = late(1, grad_normed)
    after_core(1)
    after_core(0)
    grad_normed = late(2, grad_normed)
    after_core(2)
    after_core(3)
    rowgrad_ref[...] = (
        cot.astype(F32) + normalize_back(grad_normed, normed, inverse)
    ).astype(BF16)
    after_core(4)
    after_axis(1, 0)
    after_axis(0, 0)
    after_axis(2, 0)
    after_axis(3, 0)
    after_axis(4, 0)
    after_axis(1, 1)
    after_axis(0, 1)
    after_axis(2, 1)
    after_axis(3, 1)
    after_axis(4, 1)
    after_axis(1, 2)
    after_axis(0, 2)
    after_axis(2, 2)
    after_axis(3, 2)
    after_axis(4, 2)
    after_back(1, 0)
    after_back(0, 0)
    after_back(2, 0)
    after_back(3, 0)
    after_back(4, 0)
    after_back(1, 1)
    after_back(0, 1)
    after_back(2, 1)
    after_back(3, 1)
    after_back(4, 1)
    after_back(1, 2)
    after_back(0, 2)
    after_back(2, 2)
    after_back(3, 2)
    after_back(4, 2)
    for u in range(UNITS):
        finish(u)


def spread_kernel(scale, sum_ref, layer_ref, rowgrad_ref, proj_hbm, out_hbm, layer_hbm, rowgrad_hbm, wide, sems):
    copies = [
        pltpu.make_async_copy(layer_ref, layer_hbm, sems.at[5]),
        pltpu.make_async_copy(rowgrad_ref, rowgrad_hbm, sems.at[6]),
    ]
    for copy in copies:
        copy.start()
    for u in range(UNITS):
        for n in range(4):
            at = (n % 2) * 2
            wide[u, :, n * 128 : n * 128 + 128] = (
                sum_ref[n // 2, u, at : at + 2].reshape(WIDTH, 128).astype(F32) * scale
            )
        block = (0, None, 1, 2, 3)[u]
        dst = out_hbm if block is None else proj_hbm.at[:, pl.ds(block * WIDTH, WIDTH)]
        copies.append(pltpu.make_async_copy(wide.at[u], dst, sems.at[u]))
        copies[-1].start()
    for copy in copies:
        copy.wait()


HBM = pl.BlockSpec(memory_space=pltpu.HBM)
VM = pl.BlockSpec(memory_space=pltpu.VMEM)
SM = pl.BlockSpec(memory_space=pltpu.SMEM)


def shape(*dims, dtype=BF16):
    return jax.ShapeDtypeStruct(dims, dtype)


def params(vmem_limit_bytes=VMEM_LIMIT, **kw):
    return pltpu.CompilerParams(vmem_limit_bytes=vmem_limit_bytes, **kw)


def in_hbm(array):
    return pltpu.with_memory_space_constraint(array, pltpu.HBM)


def local(loader_rows, send_slot, arrive_slot, user_lengths, proj_weight, out_weight, cotangent):
    own, normed, update, qk, v = pl.pallas_call(
        arrive_kernel,
        name="arrive",
        out_shape=(
            shape(BLK, WIDTH), shape(BLK, WIDTH), shape(BLK, WIDTH),
            shape(16, HALF, 128), shape(NCTX, HALF, 128),
        ),
        in_specs=[HBM] * 4,
        out_specs=(VM,) * 5,
        scratch_shapes=[
            pltpu.VMEM((BLK, WIDTH), BF16),
            pltpu.VMEM((1, BLK), jnp.int32),
            pltpu.VMEM((1, BLK), jnp.int32),
            pltpu.VMEM((WIDTH, 4 * WIDTH), BF16),
            pltpu.VMEM((128, 16, 128), BF16),
            pltpu.VMEM((128, 16, 128), BF16),
            pltpu.VMEM((4, BLK, EVENTS), BF16),
            pltpu.VMEM((NCTX, 2, HALF, 128), BF16),
            pltpu.VMEM((NCTX, HALF, 128), BF16),
            pltpu.SemaphoreType.DMA((2,)),
            pltpu.SemaphoreType.DMA((NCTX, 3)),
            pltpu.SemaphoreType.DMA((NCTX, 3)),
            pltpu.SemaphoreType.DMA((3,)),
            pltpu.SemaphoreType.DMA((4,)),
        ],
        compiler_params=params(collective_id=0, has_side_effects=True),
    )(
        *map(in_hbm, (loader_rows, send_slot.reshape(1, BLK), arrive_slot.reshape(1, BLK), proj_weight))
    )

    layer_out, grad_update, out_term, grad_att = pl.pallas_call(
        forward_kernel,
        name="forward",
        out_shape=(
            shape(BLK, WIDTH), shape(BLK, WIDTH, dtype=F32), shape(WIDTH, WIDTH, dtype=F32),
            shape(NCTX, HALF, 128),
        ),
        in_specs=[SM, VM, VM, VM, VM, HBM, HBM],
        out_specs=(VM,) * 4,
        scratch_shapes=[
            pltpu.VMEM((HD, EVENTS), BF16),
            pltpu.VMEM((EVENTS, HD), BF16),
            pltpu.VMEM((EVENTS, HD), BF16),
            pltpu.VMEM((HD, EVENTS), BF16),
            pltpu.VMEM((NCTX, HALF, 128), BF16),
            pltpu.VMEM((BLK, WIDTH), BF16),
            pltpu.VMEM((WIDTH, WIDTH), BF16),
            pltpu.VMEM((NCTX, HALF, 128), BF16),
            pltpu.VMEM((NCTX, HALF, 128), BF16),
            pltpu.SemaphoreType.DMA((4 * NCTX,)),
            pltpu.SemaphoreType.DMA((2,)),
        ],
        compiler_params=params(collective_id=1, has_side_effects=True),
    )(in_hbm(user_lengths), qk, v, own, update, in_hbm(cotangent), in_hbm(out_weight))

    grads = pl.pallas_call(
        backward_kernel,
        name="attend_back",
        out_shape=shape(NCTX, 3, HALF, 128),
        in_specs=[SM, VM, VM, VM],
        out_specs=VM,
        scratch_shapes=[
            pltpu.VMEM((EVENTS, HD), BF16),
            pltpu.VMEM((HD, EVENTS), BF16),
            pltpu.VMEM((EVENTS, HD), BF16),
            pltpu.VMEM((HD, EVENTS), BF16),
            pltpu.VMEM((EVENTS, HD), BF16),
            pltpu.VMEM((EVENTS, HD), BF16),
            pltpu.VMEM((HD, EVENTS), BF16),
            pltpu.VMEM((HD, EVENTS), F32),
            pltpu.VMEM((EVENTS, HD), F32),
            pltpu.VMEM((EVENTS, HD), F32),
        ],
        compiler_params=params(),
    )(in_hbm(user_lengths), qk, v, grad_att)

    row_grads, sums = pl.pallas_call(
        final_kernel,
        name="final",
        out_shape=(shape(BLK, WIDTH), shape(2, UNITS, 4, 4, 4, 16, 128)),
        in_specs=[VM] * 7,
        out_specs=(VM,) * 2,
        scratch_shapes=[
            pltpu.VMEM((NCTX, 3, HALF, 128), BF16),
            pltpu.VMEM((3, BLK, WIDTH), F32),
            pltpu.VMEM((2, UNITS * 64, 16, 128), F32),
            pltpu.VMEM((2, UNITS * 64, 16, 128), BF16),
            pltpu.VMEM((UNITS * 64, 16, 128), BF16),
            pltpu.VMEM((UNITS * 64, 16, 128), BF16),
            pltpu.VMEM((3, UNITS * 16, 16, 128), BF16),
            pltpu.VMEM((UNITS * 16, 16, 128), BF16),
            pltpu.VMEM((3, UNITS * 4, 16, 128), BF16),
            pltpu.VMEM((UNITS * 4, 16, 128), BF16),
            pltpu.VMEM((3, UNITS, 16, 128), BF16),
            pltpu.SemaphoreType.DMA((3, 2 * NCTX)),
            pltpu.SemaphoreType.DMA((4, UNITS)),
            pltpu.SemaphoreType.DMA((4, 3, UNITS, 4)),
        ],
        compiler_params=params(collective_id=2, has_side_effects=True),
    )(grads, own, normed, proj_weight, cotangent, grad_update, out_term)

    proj_grad, out_grad, layer_out, row_grads = pl.pallas_call(
        functools.partial(spread_kernel, (BLK * 128) ** (-0.5)),
        name="spread",
        out_shape=(
            shape(WIDTH, 4 * WIDTH, dtype=F32), shape(WIDTH, WIDTH, dtype=F32),
            shape(BLK, WIDTH), shape(BLK, WIDTH),
        ),
        in_specs=[VM] * 3,
        out_specs=(HBM,) * 4,
        scratch_shapes=[
            pltpu.VMEM((UNITS, WIDTH, WIDTH), F32),
            pltpu.SemaphoreType.DMA((7,)),
        ],
        compiler_params=params(),
    )(sums, layer_out, row_grads)
    return (layer_out, row_grads, proj_grad, out_grad)


def solution(mesh):
    placed = (
        P(("dp", "ctx"), None),
        P(("dp", "ctx")),
        P(("dp", "ctx")),
        P("dp", None),
        P(),
        P(),
        P(("dp", "ctx"), None),
    )
    return jax.shard_map(
        local,
        mesh=mesh,
        in_specs=placed,
        out_specs=(P(("dp", "ctx"), None), P(("dp", "ctx"), None), P(), P()),
        check_vma=False,
    )
```

```python
import functools

import jax
import jax.numpy as jnp
from jax import lax
from jax.experimental import pallas as pl
from jax.experimental.pallas import tpu as pltpu
from jax.sharding import PartitionSpec as P

MESH = pl.DeviceIdType.MESH
F32 = jnp.float32
BF16 = jnp.bfloat16
norm_eps = 1e-05
VMEM_LIMIT = 32 * 2**20

NCTX = 8
HALF = 128
BLK = 256
NB = 8
WIDTH = 512
HD = 64
EVENTS = 2048
UNITS = 5
ORDERS = ("zxy", "zyx", "xyz", "yzx", "zxy")
BACK = ("zxy", "zyx", "zyx", "xzy", "yxz")


def normalize(values):
    centre = values - jnp.mean(values, axis=-1, keepdims=True)
    inverse = lax.rsqrt(jnp.mean(centre * centre, axis=-1, keepdims=True) + norm_eps)
    return (centre * inverse, inverse)


def normalize_back(grad_in, normed, inverse):
    mean_grad = jnp.mean(grad_in, axis=-1, keepdims=True)
    mean_cross = jnp.mean(grad_in * normed, axis=-1, keepdims=True)
    return (grad_in - mean_grad - normed * mean_cross) * inverse


def silu(z):
    h = 0.5 * z
    return h + h * jnp.tanh(h)


def silu_grad(z):
    h = 0.5 * z
    u = 1.0 + jnp.tanh(h)
    return 0.5 * (u + h * u * (2.0 - u))


def dot(a, b):
    return lax.dot_general(a, b, (((1,), (0,)), ((), ())), preferred_element_type=F32)


def dot_nt(a, b):
    return lax.dot_general(a, b, (((1,), (1,)), ((), ())), preferred_element_type=F32)


def low(a, b):
    return jnp.concatenate([a[:, :HD], b[:, :HD]], axis=1)


def high(a, b):
    return jnp.concatenate([a[:, HD:], b[:, HD:]], axis=1)


def mod(a, n):
    return lax.rem(a + n, n)


def third(a):
    return (a * 21846) >> 16


def greet_ctx():
    cx = lax.axis_index("ctx")
    dp = lax.axis_index("dp")
    sem = pltpu.get_barrier_semaphore()
    for rel in range(1, NCTX):
        pl.semaphore_signal(
            sem, inc=1, device_id=(dp, lax.rem(cx + rel, NCTX)), device_id_type=MESH
        )
    return sem


def arrive_kernel(
    rows_hbm, sslot_hbm, aslot_hbm, w_hbm,
    own_ref, normed_ref, upd_ref, qk_ref, v_ref,
    rows_ref, sslot_ref, aslot_ref, w_ref,
    out, recv, hot_ref, qk_msg, v_msg, row_sems, send_sems, recv_sems, local_sems, in_sems,
):
    dp, cx = lax.axis_index("dp"), lax.axis_index("ctx")
    me = dp * NCTX + cx
    ndev = 128
    loads = [
        pltpu.make_async_copy(src, dst, in_sems.at[n])
        for n, (src, dst) in enumerate(
            ((rows_hbm, rows_ref), (sslot_hbm, sslot_ref), (aslot_hbm, aslot_ref), (w_hbm, w_ref))
        )
    ]
    for load in loads:
        load.start()

    def device(rel):
        d = (me + rel) & (ndev - 1)
        return (d >> 3, d & (NCTX - 1))

    barrier = pltpu.get_barrier_semaphore()

    def greet(rel, carry):
        pl.semaphore_signal(barrier, inc=1, device_id=device(rel), device_id_type=MESH)
        return carry

    lax.fori_loop(1, ndev, greet, 0, unroll=6)

    for load in loads[:3]:
        load.wait()
    rows = rows_ref[...]
    rows4 = jnp.concatenate([rows[:, q * 128 : q * 128 + 128] for q in range(4)], axis=0)
    slot = sslot_ref[...]
    to = third(slot)
    place = ((to - me) & (ndev - 1)) * 16 + (slot - 3 * to)
    target = jnp.concatenate([place + 4 * q for q in range(4)], axis=1)
    seen = lax.broadcasted_iota(jnp.int32, (BLK, 1024), 0)

    def pack(n, carry):
        hot = jnp.where(seen == target - n * BLK, 1.0, 0.0).astype(BF16)
        part = dot(hot, rows4).astype(BF16)
        out[pl.ds(n * 16, 16)] = part.reshape(16, 16, 128)
        return carry

    lax.fori_loop(0, 8, pack, 0)

    pl.semaphore_wait(barrier, ndev - 1)

    def send(rel, carry):
        pltpu.make_async_remote_copy(
            src_ref=out.at[rel],
            dst_ref=recv.at[rel],
            send_sem=row_sems.at[0],
            recv_sem=row_sems.at[1],
            device_id=device(rel),
            device_id_type=MESH,
        ).start()
        return carry

    lax.fori_loop(1, ndev, send, 0, unroll=6)
    recv[0] = out[0]
    all_rows = pltpu.make_async_remote_copy(
        src_ref=out.at[pl.ds(1, ndev - 1)],
        dst_ref=recv.at[pl.ds(1, ndev - 1)],
        send_sem=row_sems.at[0],
        recv_sem=row_sems.at[1],
        device_id=(dp, cx),
        device_id_type=MESH,
    )
    aslot = jnp.transpose(jnp.broadcast_to(aslot_ref[...], (128, BLK)))[:, :1]
    come = third(aslot)
    picked = ((me - come) & (ndev - 1)) * 16 + (aslot - 3 * come)
    lanes = lax.broadcasted_iota(jnp.int32, (BLK, EVENTS), 1)
    for q in range(4):
        hot_ref[q] = jnp.where(lanes == picked + 4 * q, 1.0, 0.0).astype(BF16)
    loads[3].wait()
    all_rows.wait()

    got = recv[...].reshape(EVENTS, 128)
    own = jnp.concatenate([dot(hot_ref[q], got) for q in range(4)], axis=1)
    own_ref[...] = own.astype(BF16)
    normed = normalize(own)[0].astype(BF16)
    normed_ref[...] = normed

    query = (silu(dot(normed, w_ref[:, 1024:1536])).astype(BF16).astype(F32) * 0.0625).astype(BF16)
    key = silu(dot(normed, w_ref[:, 1536:2048])).astype(BF16)
    for a in range(4):
        x, y = query[:, a * 128 : a * 128 + 128], key[:, a * 128 : a * 128 + 128]
        qk_msg[2 * a] = low(x, y).reshape(2, HALF, 128)
        qk_msg[2 * a + 1] = high(x, y).reshape(2, HALF, 128)

    def to_head(peer, rel, n):
        if n < 2:
            src, dst = qk_msg.at[peer, n], qk_ref.at[cx if n == 0 else 15 - cx]
        else:
            src, dst = v_msg.at[peer], v_ref.at[cx]
        if rel == 0:
            return pltpu.make_async_copy(src, dst, local_sems.at[n])
        return pltpu.make_async_remote_copy(
            src_ref=src,
            dst_ref=dst,
            send_sem=send_sems.at[rel, n],
            recv_sem=recv_sems.at[rel, n],
            device_id=(dp, peer),
            device_id_type=MESH,
        )

    copies = []
    for rel in range(NCTX):
        peer = lax.rem(cx + rel, NCTX)
        for n in range(2):
            copies.append(to_head(peer, rel, n))
            copies[-1].start()

    value = silu(dot(normed, w_ref[:, 512:1024])).astype(BF16)
    for a in range(4):
        x = value[:HALF, a * 128 : a * 128 + 128]
        y = value[HALF:, a * 128 : a * 128 + 128]
        v_msg[2 * a] = low(x, y)
        v_msg[2 * a + 1] = high(x, y)
    for rel in range(NCTX):
        copies.append(to_head(lax.rem(cx + rel, NCTX), rel, 2))
        copies[-1].start()

    upd_ref[...] = silu(dot(normed, w_ref[:, :512])).astype(BF16)
    for copy in copies:
        copy.wait()


def timeline_ends(len_ref):
    ends, total = [], 0
    for n in range(4):
        total = total + len_ref[0, n]
        ends.append(total)
    return ends


def start_of(positions, ends):
    first = jnp.zeros_like(positions)
    for n in range(3):
        first = jnp.where(positions >= ends[n], ends[n], first)
    return first


def end_of(position, ends):
    last = ends[3]
    for n in (2, 1, 0):
        last = jnp.where(position < ends[n], ends[n], last)
    return last


def in_position_order(packed, dst):
    for c in range(NCTX):
        block = packed[c]
        dst[c * HALF : (c + 1) * HALF, :] = block[:, :HD]
        dst[(15 - c) * HALF : (16 - c) * HALF, :] = block[:, HD:]


def by_owner(blocks, c):
    return jnp.concatenate(
        [blocks[c * HALF : (c + 1) * HALF, :], blocks[(15 - c) * HALF : (16 - c) * HALF, :]], axis=1
    )


def backward_kernel(
    len_ref, qk_ref, v_ref, ga_ref, g_ref, q, qt, k, kt, v, ga, gat, gqt, gk, gv
):
    ends = timeline_ends(len_ref)
    qk = qk_ref[...].reshape(EVENTS, 128)
    q[...] = qk[:, :HD]
    k[...] = qk[:, HD:]
    qkt = jnp.transpose(qk)
    qt[...] = qkt[:HD]
    kt[...] = qkt[HD:]
    in_position_order(v_ref, v)
    in_position_order(ga_ref, ga)
    gat[...] = jnp.transpose(ga[...])
    gqt[...] = jnp.zeros_like(gqt)
    gk[...] = jnp.zeros_like(gk)
    gv[...] = jnp.zeros_like(gv)

    t = lax.broadcasted_iota(jnp.int32, (BLK, BLK), 0)
    p = lax.broadcasted_iota(jnp.int32, (1, BLK), 1)

    def blocks(i, keys_of):
        rows = slice(i * BLK, (i + 1) * BLK)
        first = start_of(p + i * BLK, ends)
        query, parts = 0.0, []
        for j in keys_of:
            keys = slice(j * BLK, (j + 1) * BLK)
            allowed = t >= first - j * BLK
            if j == i:
                allowed = allowed & (t <= p)
            h = dot(k[keys, :], qt[:, rows])
            u = 1.0 + jnp.tanh(h)
            w = h * u
            e = dot(v[keys, :], gat[:, rows]) * (u + w * (2.0 - u))
            w = jnp.where(allowed, w, 0.0).astype(BF16)
            e = jnp.where(allowed, e, 0.0).astype(BF16)
            query = query + dot(kt[:, keys], e)
            parts.append((keys, dot(e, q[rows, :]), dot(w, ga[rows, :])))
        gqt[:, rows] += query
        for keys, key, value in parts:
            gk[keys, :] += key
            gv[keys, :] += value

    for i in range(NB):
        lowest = start_of(jnp.int32(i * BLK), ends) >> 8
        blocks(i, range(i, max(i - 3, -1), -1))
        for top in range(i - 3, -1, -3):
            pl.when(lowest <= top)(
                functools.partial(blocks, i, range(top, max(top - 3, -1), -1))
            )

    gq = jnp.transpose(gqt[...] * 0.0625).astype(BF16)
    gk_done, gv_done = gk[...].astype(BF16), gv[...].astype(BF16)
    for c in range(NCTX):
        g_ref[c, 0] = by_owner(gv_done, c)
        g_ref[c, 1] = by_owner(gq, c)
        g_ref[c, 2] = by_owner(gk_done, c)


def exchange(src, dst, sems, base=0):
    dp, cx = lax.axis_index("dp"), lax.axis_index("ctx")
    copies = []
    for rel in range(NCTX):
        peer = lax.rem(cx + rel, NCTX)
        if rel == 0:
            copy = pltpu.make_async_copy(src.at[peer], dst.at[cx], sems.at[base])
        else:
            copy = pltpu.make_async_remote_copy(
                src_ref=src.at[peer],
                dst_ref=dst.at[cx],
                send_sem=sems.at[base + rel],
                recv_sem=sems.at[base + NCTX + rel],
                device_id=(dp, peer),
                device_id_type=MESH,
            )
        copy.start()
        copies.append(copy)
    return copies


def gather_heads(parts):
    first = [low(parts[2 * a], parts[2 * a + 1]) for a in range(4)]
    second = [high(parts[2 * a], parts[2 * a + 1]) for a in range(4)]
    return jnp.concatenate(
        [jnp.concatenate(first, axis=1), jnp.concatenate(second, axis=1)], axis=0
    )


def forward_kernel(
    len_ref, qk_ref, v_ref, own_ref, upd_ref, cot_hbm, wo_hbm,
    layer_ref, gu_ref, outterm_ref, ga_ref,
    qt, k, v, vt, att_msg, cot_ref, wo_ref, att_in, ga_msg, sems, in_sems,
):
    dp, cx = lax.axis_index("dp"), lax.axis_index("ctx")
    loads = [
        pltpu.make_async_copy(cot_hbm, cot_ref, in_sems.at[0]),
        pltpu.make_async_copy(wo_hbm, wo_ref, in_sems.at[1]),
    ]
    for load in loads:
        load.start()
    barrier = greet_ctx()
    ends = timeline_ends(len_ref)
    qk = qk_ref[...].reshape(EVENTS, 128)
    k[...] = qk[:, HD:]
    qt[...] = jnp.transpose(qk)[:HD, :]
    in_position_order(v_ref, v)
    vt[...] = jnp.transpose(v[...])
    t = lax.broadcasted_iota(jnp.int32, (BLK, BLK), 0)
    p = lax.broadcasted_iota(jnp.int32, (1, BLK), 1)

    def to_owner(c):
        far = pltpu.make_async_remote_copy(
            src_ref=att_msg.at[c],
            dst_ref=att_in.at[cx],
            send_sem=sems.at[c],
            recv_sem=sems.at[NCTX + cx],
            device_id=(dp, c),
            device_id_type=MESH,
        )
        return far, pltpu.make_async_copy(att_msg.at[c], att_in.at[cx], sems.at[c])

    def step(n, carry):
        block = (n + (cx >> 1)) & 3
        near_sum = jnp.zeros((HD, BLK), F32)
        far_sum = jnp.zeros((HD, BLK), F32)
        for m in range(9):
            second = m > block
            i = jnp.where(second, 7 - block, block)
            j = jnp.where(second, m - block - 1, m)
            rows = pl.ds(pl.multiple_of(i * BLK, BLK), BLK)
            keys = pl.ds(pl.multiple_of(j * BLK, BLK), BLK)
            h = dot(k[keys, :], qt[:, rows])
            w = h + h * jnp.tanh(h)
            first = start_of(p + i * BLK, ends) - j * BLK
            w = jnp.where((t >= first) & (t <= p + (i - j) * BLK), w, 0.0).astype(BF16)
            part = dot(vt[:, keys], w)
            if m == 0:
                near_sum = part
            elif m > 3:
                far_sum = far_sum + part
            else:
                near_sum = near_sum + jnp.where(second, 0.0, part)
                far_sum = far_sum + jnp.where(second, part, 0.0)
        near_rows = jnp.transpose(near_sum).astype(BF16)
        far_rows = jnp.transpose(far_sum).astype(BF16)

        @pl.when(n == 0)
        def _():
            pl.semaphore_wait(barrier, NCTX - 1)

        for e in range(2):
            c = 2 * block + e
            att_msg[c] = jnp.concatenate(
                [near_rows[e * HALF : e * HALF + HALF], far_rows[HALF - e * HALF : BLK - e * HALF]], axis=1
            )
            far, near = to_owner(c)

            @pl.when(c != cx)
            def _():
                far.start()

            @pl.when(c == cx)
            def _():
                near.start()

        return carry

    lax.fori_loop(0, 4, step, 0)
    for load in loads:
        load.wait()
    cot = cot_ref[...]
    wo = wo_ref[...]
    grad_gated = dot_nt(cot, wo)
    to_owner(cx)[1].wait()
    for rel in range(1, NCTX):
        h = (cx + rel) & (NCTX - 1)
        to_owner(h)[0].wait_send()
        pltpu.make_async_remote_copy(
            src_ref=att_msg.at[h],
            dst_ref=att_in.at[h],
            send_sem=sems.at[h],
            recv_sem=sems.at[NCTX + h],
            device_id=(dp, h),
            device_id_type=MESH,
        ).wait_recv()
    update = upd_ref[...].astype(F32)
    attended = gather_heads([att_in[h].astype(F32) for h in range(NCTX)])
    att_normed, inverse = normalize(attended)
    grad_att = normalize_back(grad_gated * update, att_normed, inverse).astype(BF16)
    for a in range(4):
        x = grad_att[:HALF, a * 128 : a * 128 + 128]
        y = grad_att[HALF:, a * 128 : a * 128 + 128]
        ga_msg[2 * a] = low(x, y)
        ga_msg[2 * a + 1] = high(x, y)
    copies = exchange(ga_msg, ga_ref, sems, 2 * NCTX)
    gated = (att_normed * update).astype(BF16)
    layer_ref[...] = (own_ref[...].astype(F32) + dot(gated, wo)).astype(BF16)
    outterm_ref[...] = dot(jnp.transpose(gated), cot)
    gu_ref[...] = grad_gated * att_normed
    for copy in copies:
        copy.wait()


def final_kernel(
    g_ref, own_ref, normed_ref, w_ref, cot_ref, gu_ref, outterm_ref,
    rowgrad_ref, sum_ref,
    g_in, slope, acc, mine, core_in, out1, in1, out2, in2, out3, in3, sems, core_sems, axis_sems,
):
    dp, cx = lax.axis_index("dp"), lax.axis_index("ctx")
    core, xlo, z = lax.rem(dp, 2), lax.rem(dp // 2, 2), dp // 4
    xhi, y = lax.rem(cx, 2), cx // 2
    place = {"x": xhi * 2 + xlo, "y": y, "z": z}
    sibling = (dp + 1 - 2 * core, cx)

    def along(axis, r):
        c = lax.rem(place[axis] + r, 4)
        if axis == "x":
            return c, (z * 4 + lax.rem(c, 2) * 2 + core, y * 2 + c // 2)
        if axis == "y":
            return c, (dp, c * 2 + xhi)
        return c, (c * 4 + xlo * 2 + core, cx)

    barrier = greet_ctx()
    for device in [sibling] + [along(axis, r)[1] for axis in "xyz" for r in (1, 2, 3)]:
        pl.semaphore_signal(barrier, inc=1, device_id=device, device_id_type=MESH)

    def put(u, term):
        for n in range(4):
            part = term[:, n * 128 : n * 128 + 128].reshape(32, 16, 128)
            at = pl.ds(u * 64 + (n % 2) * 32, 32)
            acc[n // 2, at] = part
            mine[n // 2, at] = part.astype(BF16)

    def columns(block):
        return w_ref[:, block * WIDTH : (block + 1) * WIDTH]

    def unit_grads(u, block, grad, slope):
        grad_pre = (grad * slope).astype(BF16)
        put(u, dot(normed_t, grad_pre))
        return dot_nt(grad_pre, columns(block))

    def remote(src, dst, send_sem, recv_sem, device):
        copy = pltpu.make_async_remote_copy(
            src_ref=src, dst_ref=dst, send_sem=send_sem, recv_sem=recv_sem,
            device_id=device, device_id_type=MESH,
        )
        copy.start()
        return copy

    running = {}
    lead = (out1, out2, out3)
    landing = (in1, in2, in3)
    sizes = (16, 4, 1)
    base = [u * 64 for u in range(UNITS)]

    def core_start(u):
        at = pl.ds(u * 64, 64)
        running[u] = [
            remote(
                mine.at[1 - core, at], core_in.at[at], core_sems.at[0, u], core_sems.at[1, u], sibling
            )
        ]

    def finish(u):
        for copy in running.pop(u):
            copy.wait()

    def core_finish(u):
        finish(u)
        at = pl.ds(u * 64, 64)
        total = acc[core, at] + core_in[at].astype(F32)
        acc[core, at] = total
        out1[at] = total.astype(BF16)

    def axis_start(u, step):
        size = sizes[step]
        running[u] = []
        for r in (1, 2, 3):
            c, device = along(ORDERS[u][step], r)
            running[u].append(
                remote(
                    lead[step].at[pl.ds((u * 4 + c) * size, size)],
                    landing[step].at[r - 1, pl.ds(u * size, size)],
                    axis_sems.at[0, step, u, r], axis_sems.at[1, step, u, r], device,
                )
            )

    def axis_finish(u, step):
        finish(u)
        size = sizes[step]
        base[u] = base[u] + place[ORDERS[u][step]] * size
        total = acc[core, pl.ds(base[u], size)]
        for r in range(3):
            total = total + landing[step][r, pl.ds(u * size, size)].astype(F32)
        if step == 2:
            held[u] = [place[axis] for axis in ORDERS[u]]
            sum_ref[(core, u, *held[u])] = total.astype(BF16)[0]
        else:
            acc[core, pl.ds(base[u], size)] = total
            lead[step + 1][pl.ds(u * size, size)] = total.astype(BF16)

    held = {}

    def back_start(u, step):
        axis = BACK[u][step]
        part = sum_ref.at[(core, u, *held[u])]
        running[u] = [
            remote(
                part, part, axis_sems.at[2, step, u, r], axis_sems.at[3, step, u, r], along(axis, r)[1]
            )
            for r in (1, 2, 3)
        ]
        held[u][ORDERS[u].index(axis)] = slice(None)

    def core_back(u):
        part = sum_ref.at[core, u]
        running[u] = [remote(part, part, core_sems.at[2, u], core_sems.at[3, u], sibling)]

    def after_core(u):
        core_finish(u)
        axis_start(u, 0)

    def after_axis(u, step):
        axis_finish(u, step)
        if step < 2:
            axis_start(u, step + 1)
        else:
            back_start(u, 0)

    def after_back(u, step):
        finish(u)
        if step < 2:
            back_start(u, step + 1)
        else:
            core_back(u)

    pl.semaphore_wait(barrier, NCTX - 1 + 10)
    g_copies = []
    for n in range(3):
        for rel in range(NCTX):
            peer = (cx + rel) & (NCTX - 1)
            src, dst = g_ref.at[peer, n], g_in.at[cx, n]
            if rel == 0:
                g_copies.append(pltpu.make_async_copy(src, dst, sems.at[n, 0]))
                g_copies[-1].start()
            else:
                g_copies.append(
                    remote(src, dst, sems.at[n, rel], sems.at[n, NCTX + rel], (dp, peer))
                )

    own, cot = own_ref[...].astype(F32), cot_ref[...]
    normed, inverse = normalize(own)
    normed_bf = normed_ref[...]
    normed_t = jnp.transpose(normed_bf)
    put(1, outterm_ref[...])
    core_start(1)
    grad_normed = unit_grads(0, 0, gu_ref[...], silu_grad(dot(normed_bf, columns(0))))
    core_start(0)
    for n in range(3):
        slope[n] = silu_grad(dot(normed_bf, columns(n + 1)))

    def late(n, total):
        for copy in g_copies[n * NCTX : (n + 1) * NCTX]:
            copy.wait()
        grad = gather_heads([g_in[h, n].astype(F32) for h in range(NCTX)])
        total = total + unit_grads(n + 2, n + 1, grad, slope[n])
        core_start(n + 2)
        return total

    grad_normed = late(0, grad_normed)
    after_core(1)
    after_core(0)
    grad_normed = late(1, grad_normed)
    grad_normed = late(2, grad_normed)
    after_core(2)
    after_core(3)
    rowgrad_ref[...] = (
        cot.astype(F32) + normalize_back(grad_normed, normed, inverse)
    ).astype(BF16)
    after_core(4)
    after_axis(1, 0)
    after_axis(0, 0)
    after_axis(2, 0)
    after_axis(3, 0)
    after_axis(4, 0)
    after_axis(1, 1)
    after_axis(0, 1)
    after_axis(2, 1)
    after_axis(3, 1)
    after_axis(4, 1)
    after_axis(1, 2)
    after_axis(0, 2)
    after_axis(2, 2)
    after_axis(3, 2)
    after_axis(4, 2)
    after_back(1, 0)
    after_back(0, 0)
    after_back(2, 0)
    after_back(3, 0)
    after_back(4, 0)
    after_back(1, 1)
    after_back(0, 1)
    after_back(2, 1)
    after_back(3, 1)
    after_back(4, 1)
    after_back(1, 2)
    after_back(0, 2)
    after_back(2, 2)
    after_back(3, 2)
    after_back(4, 2)
    for u in range(UNITS):
        finish(u)


def spread_kernel(scale, sum_ref, layer_ref, rowgrad_ref, proj_hbm, out_hbm, layer_hbm, rowgrad_hbm, wide, sems):
    copies = [
        pltpu.make_async_copy(layer_ref, layer_hbm, sems.at[5]),
        pltpu.make_async_copy(rowgrad_ref, rowgrad_hbm, sems.at[6]),
    ]
    for copy in copies:
        copy.start()
    for u in range(UNITS):
        for n in range(4):
            at = (n % 2) * 2
            wide[u, :, n * 128 : n * 128 + 128] = (
                sum_ref[n // 2, u, at : at + 2].reshape(WIDTH, 128).astype(F32) * scale
            )
        block = (0, None, 1, 2, 3)[u]
        dst = out_hbm if block is None else proj_hbm.at[:, pl.ds(block * WIDTH, WIDTH)]
        copies.append(pltpu.make_async_copy(wide.at[u], dst, sems.at[u]))
        copies[-1].start()
    for copy in copies:
        copy.wait()


HBM = pl.BlockSpec(memory_space=pltpu.HBM)
VM = pl.BlockSpec(memory_space=pltpu.VMEM)
SM = pl.BlockSpec(memory_space=pltpu.SMEM)


def shape(*dims, dtype=BF16):
    return jax.ShapeDtypeStruct(dims, dtype)


def params(vmem_limit_bytes=VMEM_LIMIT, **kw):
    return pltpu.CompilerParams(vmem_limit_bytes=vmem_limit_bytes, **kw)


def in_hbm(array):
    return pltpu.with_memory_space_constraint(array, pltpu.HBM)


def local(loader_rows, send_slot, arrive_slot, user_lengths, proj_weight, out_weight, cotangent):
    own, normed, update, qk, v = pl.pallas_call(
        arrive_kernel,
        name="arrive",
        out_shape=(
            shape(BLK, WIDTH), shape(BLK, WIDTH), shape(BLK, WIDTH),
            shape(16, HALF, 128), shape(NCTX, HALF, 128),
        ),
        in_specs=[HBM] * 4,
        out_specs=(VM,) * 5,
        scratch_shapes=[
            pltpu.VMEM((BLK, WIDTH), BF16),
            pltpu.VMEM((1, BLK), jnp.int32),
            pltpu.VMEM((1, BLK), jnp.int32),
            pltpu.VMEM((WIDTH, 4 * WIDTH), BF16),
            pltpu.VMEM((128, 16, 128), BF16),
            pltpu.VMEM((128, 16, 128), BF16),
            pltpu.VMEM((4, BLK, EVENTS), BF16),
            pltpu.VMEM((NCTX, 2, HALF, 128), BF16),
            pltpu.VMEM((NCTX, HALF, 128), BF16),
            pltpu.SemaphoreType.DMA((2,)),
            pltpu.SemaphoreType.DMA((NCTX, 3)),
            pltpu.SemaphoreType.DMA((NCTX, 3)),
            pltpu.SemaphoreType.DMA((3,)),
            pltpu.SemaphoreType.DMA((4,)),
        ],
        compiler_params=params(collective_id=0, has_side_effects=True),
    )(
        *map(in_hbm, (loader_rows, send_slot.reshape(1, BLK), arrive_slot.reshape(1, BLK), proj_weight))
    )

    layer_out, grad_update, out_term, grad_att = pl.pallas_call(
        forward_kernel,
        name="forward",
        out_shape=(
            shape(BLK, WIDTH), shape(BLK, WIDTH, dtype=F32), shape(WIDTH, WIDTH, dtype=F32),
            shape(NCTX, HALF, 128),
        ),
        in_specs=[SM, VM, VM, VM, VM, HBM, HBM],
        out_specs=(VM,) * 4,
        scratch_shapes=[
            pltpu.VMEM((HD, EVENTS), BF16),
            pltpu.VMEM((EVENTS, HD), BF16),
            pltpu.VMEM((EVENTS, HD), BF16),
            pltpu.VMEM((HD, EVENTS), BF16),
            pltpu.VMEM((NCTX, HALF, 128), BF16),
            pltpu.VMEM((BLK, WIDTH), BF16),
            pltpu.VMEM((WIDTH, WIDTH), BF16),
            pltpu.VMEM((NCTX, HALF, 128), BF16),
            pltpu.VMEM((NCTX, HALF, 128), BF16),
            pltpu.SemaphoreType.DMA((4 * NCTX,)),
            pltpu.SemaphoreType.DMA((2,)),
        ],
        compiler_params=params(collective_id=1, has_side_effects=True),
    )(in_hbm(user_lengths), qk, v, own, update, in_hbm(cotangent), in_hbm(out_weight))

    grads = pl.pallas_call(
        backward_kernel,
        name="attend_back",
        out_shape=shape(NCTX, 3, HALF, 128),
        in_specs=[SM, VM, VM, VM],
        out_specs=VM,
        scratch_shapes=[
            pltpu.VMEM((EVENTS, HD), BF16),
            pltpu.VMEM((HD, EVENTS), BF16),
            pltpu.VMEM((EVENTS, HD), BF16),
            pltpu.VMEM((HD, EVENTS), BF16),
            pltpu.VMEM((EVENTS, HD), BF16),
            pltpu.VMEM((EVENTS, HD), BF16),
            pltpu.VMEM((HD, EVENTS), BF16),
            pltpu.VMEM((HD, EVENTS), F32),
            pltpu.VMEM((EVENTS, HD), F32),
            pltpu.VMEM((EVENTS, HD), F32),
        ],
        compiler_params=params(),
    )(in_hbm(user_lengths), qk, v, grad_att)

    row_grads, sums = pl.pallas_call(
        final_kernel,
        name="final",
        out_shape=(shape(BLK, WIDTH), shape(2, UNITS, 4, 4, 4, 16, 128)),
        in_specs=[VM] * 7,
        out_specs=(VM,) * 2,
        scratch_shapes=[
            pltpu.VMEM((NCTX, 3, HALF, 128), BF16),
            pltpu.VMEM((3, BLK, WIDTH), F32),
            pltpu.VMEM((2, UNITS * 64, 16, 128), F32),
            pltpu.VMEM((2, UNITS * 64, 16, 128), BF16),
            pltpu.VMEM((UNITS * 64, 16, 128), BF16),
            pltpu.VMEM((UNITS * 64, 16, 128), BF16),
            pltpu.VMEM((3, UNITS * 16, 16, 128), BF16),
            pltpu.VMEM((UNITS * 16, 16, 128), BF16),
            pltpu.VMEM((3, UNITS * 4, 16, 128), BF16),
            pltpu.VMEM((UNITS * 4, 16, 128), BF16),
            pltpu.VMEM((3, UNITS, 16, 128), BF16),
            pltpu.SemaphoreType.DMA((3, 2 * NCTX)),
            pltpu.SemaphoreType.DMA((4, UNITS)),
            pltpu.SemaphoreType.DMA((4, 3, UNITS, 4)),
        ],
        compiler_params=params(collective_id=2, has_side_effects=True),
    )(grads, own, normed, proj_weight, cotangent, grad_update, out_term)

    proj_grad, out_grad, layer_out, row_grads = pl.pallas_call(
        functools.partial(spread_kernel, (BLK * 128) ** (-0.5)),
        name="spread",
        out_shape=(
            shape(WIDTH, 4 * WIDTH, dtype=F32), shape(WIDTH, WIDTH, dtype=F32),
            shape(BLK, WIDTH), shape(BLK, WIDTH),
        ),
        in_specs=[VM] * 3,
        out_specs=(HBM,) * 4,
        scratch_shapes=[
            pltpu.VMEM((UNITS, WIDTH, WIDTH), F32),
            pltpu.SemaphoreType.DMA((7,)),
        ],
        compiler_params=params(),
    )(sums, layer_out, row_grads)
    return (layer_out, row_grads, proj_grad, out_grad)


def solution(mesh):
    placed = (
        P(("dp", "ctx"), None),
        P(("dp", "ctx")),
        P(("dp", "ctx")),
        P("dp", None),
        P(),
        P(),
        P(("dp", "ctx"), None),
    )
    return jax.shard_map(
        local,
        mesh=mesh,
        in_specs=placed,
        out_specs=(P(("dp", "ctx"), None), P(("dp", "ctx"), None), P(), P()),
        check_vma=False,
    )
```

```python
import functools

import jax
import jax.numpy as jnp
from jax import lax
from jax.experimental import pallas as pl
from jax.experimental.pallas import tpu as pltpu
from jax.sharding import PartitionSpec as P

MESH = pl.DeviceIdType.MESH
F32 = jnp.float32
BF16 = jnp.bfloat16
norm_eps = 1e-05
VMEM_LIMIT = 32 * 2**20

NCTX = 8
HALF = 128
BLK = 256
NB = 8
WIDTH = 512
HD = 64
EVENTS = 2048
UNITS = 5
ORDERS = ("zxy", "zyx", "xyz", "yzx", "zxy")
BACK = ("zxy", "zyx", "zyx", "xzy", "yxz")


def normalize(values):
    centre = values - jnp.mean(values, axis=-1, keepdims=True)
    inverse = lax.rsqrt(jnp.mean(centre * centre, axis=-1, keepdims=True) + norm_eps)
    return (centre * inverse, inverse)


def normalize_back(grad_in, normed, inverse):
    mean_grad = jnp.mean(grad_in, axis=-1, keepdims=True)
    mean_cross = jnp.mean(grad_in * normed, axis=-1, keepdims=True)
    return (grad_in - mean_grad - normed * mean_cross) * inverse


def silu(z):
    h = 0.5 * z
    return h + h * jnp.tanh(h)


def silu_grad(z):
    h = 0.5 * z
    u = 1.0 + jnp.tanh(h)
    return 0.5 * (u + h * u * (2.0 - u))


def dot(a, b):
    return lax.dot_general(a, b, (((1,), (0,)), ((), ())), preferred_element_type=F32)


def dot_nt(a, b):
    return lax.dot_general(a, b, (((1,), (1,)), ((), ())), preferred_element_type=F32)


def low(a, b):
    return jnp.concatenate([a[:, :HD], b[:, :HD]], axis=1)


def high(a, b):
    return jnp.concatenate([a[:, HD:], b[:, HD:]], axis=1)


def mod(a, n):
    return lax.rem(a + n, n)


def third(a):
    return (a * 21846) >> 16


def greet_ctx():
    cx = lax.axis_index("ctx")
    dp = lax.axis_index("dp")
    sem = pltpu.get_barrier_semaphore()
    for rel in range(1, NCTX):
        pl.semaphore_signal(
            sem, inc=1, device_id=(dp, lax.rem(cx + rel, NCTX)), device_id_type=MESH
        )
    return sem


def arrive_kernel(
    rows_hbm, sslot_hbm, aslot_hbm, w_hbm,
    own_ref, normed_ref, upd_ref, qk_ref, v_ref,
    rows_ref, sslot_ref, aslot_ref, w_ref,
    out, recv, hot_ref, qk_msg, v_msg, row_sems, send_sems, recv_sems, local_sems, in_sems,
):
    dp, cx = lax.axis_index("dp"), lax.axis_index("ctx")
    me = dp * NCTX + cx
    ndev = 128
    loads = [
        pltpu.make_async_copy(src, dst, in_sems.at[n])
        for n, (src, dst) in enumerate(
            ((rows_hbm, rows_ref), (sslot_hbm, sslot_ref), (aslot_hbm, aslot_ref), (w_hbm, w_ref))
        )
    ]
    for load in loads:
        load.start()

    def device(rel):
        d = (me + rel) & (ndev - 1)
        return (d >> 3, d & (NCTX - 1))

    barrier = pltpu.get_barrier_semaphore()

    def greet(rel, carry):
        pl.semaphore_signal(barrier, inc=1, device_id=device(rel), device_id_type=MESH)
        return carry

    lax.fori_loop(1, ndev, greet, 0, unroll=6)

    for load in loads[:3]:
        load.wait()
    rows = rows_ref[...]
    rows4 = jnp.concatenate([rows[:, q * 128 : q * 128 + 128] for q in range(4)], axis=0)
    slot = sslot_ref[...]
    to = third(slot)
    place = ((to - me) & (ndev - 1)) * 16 + (slot - 3 * to)
    target = jnp.concatenate([place + 4 * q for q in range(4)], axis=1)
    seen = lax.broadcasted_iota(jnp.int32, (BLK, 1024), 0)

    def pack(n, carry):
        hot = jnp.where(seen == target - n * BLK, 1.0, 0.0).astype(BF16)
        part = dot(hot, rows4).astype(BF16)
        out[pl.ds(n * 16, 16)] = part.reshape(16, 16, 128)
        return carry

    lax.fori_loop(0, 8, pack, 0)

    pl.semaphore_wait(barrier, ndev - 1)

    def send(rel, carry):
        pltpu.make_async_remote_copy(
            src_ref=out.at[rel],
            dst_ref=recv.at[rel],
            send_sem=row_sems.at[0],
            recv_sem=row_sems.at[1],
            device_id=device(rel),
            device_id_type=MESH,
        ).start()
        return carry

    lax.fori_loop(1, ndev, send, 0, unroll=6)
    recv[0] = out[0]
    all_rows = pltpu.make_async_remote_copy(
        src_ref=out.at[pl.ds(1, ndev - 1)],
        dst_ref=recv.at[pl.ds(1, ndev - 1)],
        send_sem=row_sems.at[0],
        recv_sem=row_sems.at[1],
        device_id=(dp, cx),
        device_id_type=MESH,
    )
    aslot = jnp.transpose(jnp.broadcast_to(aslot_ref[...], (128, BLK)))[:, :1]
    come = third(aslot)
    picked = ((me - come) & (ndev - 1)) * 16 + (aslot - 3 * come)
    lanes = lax.broadcasted_iota(jnp.int32, (BLK, EVENTS), 1)
    for q in range(4):
        hot_ref[q] = jnp.where(lanes == picked + 4 * q, 1.0, 0.0).astype(BF16)
    loads[3].wait()
    all_rows.wait()

    got = recv[...].reshape(EVENTS, 128)
    own = jnp.concatenate([dot(hot_ref[q], got) for q in range(4)], axis=1)
    own_ref[...] = own.astype(BF16)
    normed = normalize(own)[0].astype(BF16)
    normed_ref[...] = normed

    query = (silu(dot(normed, w_ref[:, 1024:1536])).astype(BF16).astype(F32) * 0.0625).astype(BF16)
    key = silu(dot(normed, w_ref[:, 1536:2048])).astype(BF16)
    for a in range(4):
        x, y = query[:, a * 128 : a * 128 + 128], key[:, a * 128 : a * 128 + 128]
        qk_msg[2 * a] = low(x, y).reshape(2, HALF, 128)
        qk_msg[2 * a + 1] = high(x, y).reshape(2, HALF, 128)

    def to_head(peer, rel, n):
        if n < 2:
            src, dst = qk_msg.at[peer, n], qk_ref.at[cx if n == 0 else 15 - cx]
        else:
            src, dst = v_msg.at[peer], v_ref.at[cx]
        if rel == 0:
            return pltpu.make_async_copy(src, dst, local_sems.at[n])
        return pltpu.make_async_remote_copy(
            src_ref=src,
            dst_ref=dst,
            send_sem=send_sems.at[rel, n],
            recv_sem=recv_sems.at[rel, n],
            device_id=(dp, peer),
            device_id_type=MESH,
        )

    copies = []
    for rel in range(NCTX):
        peer = lax.rem(cx + rel, NCTX)
        for n in range(2):
            copies.append(to_head(peer, rel, n))
            copies[-1].start()

    value = silu(dot(normed, w_ref[:, 512:1024])).astype(BF16)
    for a in range(4):
        x = value[:HALF, a * 128 : a * 128 + 128]
        y = value[HALF:, a * 128 : a * 128 + 128]
        v_msg[2 * a] = low(x, y)
        v_msg[2 * a + 1] = high(x, y)
    for rel in range(NCTX):
        copies.append(to_head(lax.rem(cx + rel, NCTX), rel, 2))
        copies[-1].start()

    upd_ref[...] = silu(dot(normed, w_ref[:, :512])).astype(BF16)
    for copy in copies:
        copy.wait()


def timeline_ends(len_ref):
    ends, total = [], 0
    for n in range(4):
        total = total + len_ref[0, n]
        ends.append(total)
    return ends


def start_of(positions, ends):
    first = jnp.zeros_like(positions)
    for n in range(3):
        first = jnp.where(positions >= ends[n], ends[n], first)
    return first


def end_of(position, ends):
    last = ends[3]
    for n in (2, 1, 0):
        last = jnp.where(position < ends[n], ends[n], last)
    return last


def in_position_order(packed, dst):
    for c in range(NCTX):
        block = packed[c]
        dst[c * HALF : (c + 1) * HALF, :] = block[:, :HD]
        dst[(15 - c) * HALF : (16 - c) * HALF, :] = block[:, HD:]


def by_owner(blocks, c):
    return jnp.concatenate(
        [blocks[c * HALF : (c + 1) * HALF, :], blocks[(15 - c) * HALF : (16 - c) * HALF, :]], axis=1
    )


def backward_kernel(
    len_ref, qk_ref, v_ref, ga_ref, g_ref, q, qt, k, kt, v, ga, gat, gqt, gk, gv
):
    ends = timeline_ends(len_ref)
    qk = qk_ref[...].reshape(EVENTS, 128)
    q[...] = qk[:, :HD]
    k[...] = qk[:, HD:]
    qkt = jnp.transpose(qk)
    qt[...] = qkt[:HD]
    kt[...] = qkt[HD:]
    in_position_order(v_ref, v)
    in_position_order(ga_ref, ga)
    gat[...] = jnp.transpose(ga[...])
    gqt[...] = jnp.zeros_like(gqt)
    gk[...] = jnp.zeros_like(gk)
    gv[...] = jnp.zeros_like(gv)

    t = lax.broadcasted_iota(jnp.int32, (BLK, BLK), 0)
    p = lax.broadcasted_iota(jnp.int32, (1, BLK), 1)

    def blocks(i, keys_of):
        rows = slice(i * BLK, (i + 1) * BLK)
        first = start_of(p + i * BLK, ends)
        query, parts = 0.0, []
        for j in keys_of:
            keys = slice(j * BLK, (j + 1) * BLK)
            allowed = t >= first - j * BLK
            if j == i:
                allowed = allowed & (t <= p)
            h = dot(k[keys, :], qt[:, rows])
            u = 1.0 + jnp.tanh(h)
            w = h * u
            e = dot(v[keys, :], gat[:, rows]) * (u + w * (2.0 - u))
            w = jnp.where(allowed, w, 0.0).astype(BF16)
            e = jnp.where(allowed, e, 0.0).astype(BF16)
            query = query + dot(kt[:, keys], e)
            parts.append((keys, dot(e, q[rows, :]), dot(w, ga[rows, :])))
        gqt[:, rows] += query
        for keys, key, value in parts:
            gk[keys, :] += key
            gv[keys, :] += value

    for i in range(NB):
        lowest = start_of(jnp.int32(i * BLK), ends) >> 8
        blocks(i, range(i, max(i - 3, -1), -1))
        for top in range(i - 3, -1, -3):
            pl.when(lowest <= top)(
                functools.partial(blocks, i, range(top, max(top - 3, -1), -1))
            )

    gq = jnp.transpose(gqt[...] * 0.0625).astype(BF16)
    gk_done, gv_done = gk[...].astype(BF16), gv[...].astype(BF16)
    for c in range(NCTX):
        g_ref[c, 0] = by_owner(gv_done, c)
        g_ref[c, 1] = by_owner(gq, c)
        g_ref[c, 2] = by_owner(gk_done, c)


def exchange(src, dst, sems, base=0):
    dp, cx = lax.axis_index("dp"), lax.axis_index("ctx")
    copies = []
    for rel in range(NCTX):
        peer = lax.rem(cx + rel, NCTX)
        if rel == 0:
            copy = pltpu.make_async_copy(src.at[peer], dst.at[cx], sems.at[base])
        else:
            copy = pltpu.make_async_remote_copy(
                src_ref=src.at[peer],
                dst_ref=dst.at[cx],
                send_sem=sems.at[base + rel],
                recv_sem=sems.at[base + NCTX + rel],
                device_id=(dp, peer),
                device_id_type=MESH,
            )
        copy.start()
        copies.append(copy)
    return copies


def gather_heads(parts):
    first = [low(parts[2 * a], parts[2 * a + 1]) for a in range(4)]
    second = [high(parts[2 * a], parts[2 * a + 1]) for a in range(4)]
    return jnp.concatenate(
        [jnp.concatenate(first, axis=1), jnp.concatenate(second, axis=1)], axis=0
    )


def forward_kernel(
    len_ref, qk_ref, v_ref, own_ref, upd_ref, cot_hbm, wo_hbm,
    layer_ref, gu_ref, outterm_ref, ga_ref,
    qt, k, v, vt, att_msg, cot_ref, wo_ref, att_in, ga_msg, sems, in_sems,
):
    dp, cx = lax.axis_index("dp"), lax.axis_index("ctx")
    loads = [
        pltpu.make_async_copy(cot_hbm, cot_ref, in_sems.at[0]),
        pltpu.make_async_copy(wo_hbm, wo_ref, in_sems.at[1]),
    ]
    for load in loads:
        load.start()
    barrier = greet_ctx()
    ends = timeline_ends(len_ref)
    qk = qk_ref[...].reshape(EVENTS, 128)
    k[...] = qk[:, HD:]
    qt[...] = jnp.transpose(qk)[:HD, :]
    in_position_order(v_ref, v)
    vt[...] = jnp.transpose(v[...])
    t = lax.broadcasted_iota(jnp.int32, (BLK, BLK), 0)
    p = lax.broadcasted_iota(jnp.int32, (1, BLK), 1)

    def to_owner(c):
        far = pltpu.make_async_remote_copy(
            src_ref=att_msg.at[c],
            dst_ref=att_in.at[cx],
            send_sem=sems.at[c],
            recv_sem=sems.at[NCTX + cx],
            device_id=(dp, c),
            device_id_type=MESH,
        )
        return far, pltpu.make_async_copy(att_msg.at[c], att_in.at[cx], sems.at[c])

    def step(n, carry):
        block = (n + (cx >> 1)) & 3
        near_sum = jnp.zeros((HD, BLK), F32)
        far_sum = jnp.zeros((HD, BLK), F32)
        for m in range(9):
            second = m > block
            i = jnp.where(second, 7 - block, block)
            j = jnp.where(second, m - block - 1, m)
            rows = pl.ds(pl.multiple_of(i * BLK, BLK), BLK)
            keys = pl.ds(pl.multiple_of(j * BLK, BLK), BLK)
            h = dot(k[keys, :], qt[:, rows])
            w = h + h * jnp.tanh(h)
            first = start_of(p + i * BLK, ends) - j * BLK
            w = jnp.where((t >= first) & (t <= p + (i - j) * BLK), w, 0.0).astype(BF16)
            part = dot(vt[:, keys], w)
            if m == 0:
                near_sum = part
            elif m > 3:
                far_sum = far_sum + part
            else:
                near_sum = near_sum + jnp.where(second, 0.0, part)
                far_sum = far_sum + jnp.where(second, part, 0.0)
        near_rows = jnp.transpose(near_sum).astype(BF16)
        far_rows = jnp.transpose(far_sum).astype(BF16)

        @pl.when(n == 0)
        def _():
            pl.semaphore_wait(barrier, NCTX - 1)

        for e in range(2):
            c = 2 * block + e
            att_msg[c] = jnp.concatenate(
                [near_rows[e * HALF : e * HALF + HALF], far_rows[HALF - e * HALF : BLK - e * HALF]], axis=1
            )
            far, near = to_owner(c)

            @pl.when(c != cx)
            def _():
                far.start()

            @pl.when(c == cx)
            def _():
                near.start()

        return carry

    lax.fori_loop(0, 4, step, 0)
    for load in loads:
        load.wait()
    cot = cot_ref[...]
    wo = wo_ref[...]
    grad_gated = dot_nt(cot, wo)
    to_owner(cx)[1].wait()
    for rel in range(1, NCTX):
        h = (cx + rel) & (NCTX - 1)
        to_owner(h)[0].wait_send()
        pltpu.make_async_remote_copy(
            src_ref=att_msg.at[h],
            dst_ref=att_in.at[h],
            send_sem=sems.at[h],
            recv_sem=sems.at[NCTX + h],
            device_id=(dp, h),
            device_id_type=MESH,
        ).wait_recv()
    update = upd_ref[...].astype(F32)
    attended = gather_heads([att_in[h].astype(F32) for h in range(NCTX)])
    att_normed, inverse = normalize(attended)
    grad_att = normalize_back(grad_gated * update, att_normed, inverse).astype(BF16)
    for a in range(4):
        x = grad_att[:HALF, a * 128 : a * 128 + 128]
        y = grad_att[HALF:, a * 128 : a * 128 + 128]
        ga_msg[2 * a] = low(x, y)
        ga_msg[2 * a + 1] = high(x, y)
    copies = exchange(ga_msg, ga_ref, sems, 2 * NCTX)
    gated = (att_normed * update).astype(BF16)
    layer_ref[...] = (own_ref[...].astype(F32) + dot(gated, wo)).astype(BF16)
    outterm_ref[...] = dot(jnp.transpose(gated), cot)
    gu_ref[...] = grad_gated * att_normed
    for copy in copies:
        copy.wait()


def final_kernel(
    g_ref, own_ref, normed_ref, w_ref, cot_ref, gu_ref, outterm_ref,
    rowgrad_ref, sum_ref,
    g_in, slope, acc, mine, core_in, out1, in1, out2, in2, out3, in3, sems, core_sems, axis_sems,
):
    dp, cx = lax.axis_index("dp"), lax.axis_index("ctx")
    core, xlo, z = lax.rem(dp, 2), lax.rem(dp // 2, 2), dp // 4
    xhi, y = lax.rem(cx, 2), cx // 2
    place = {"x": xhi * 2 + xlo, "y": y, "z": z}
    sibling = (dp + 1 - 2 * core, cx)

    def along(axis, r):
        c = lax.rem(place[axis] + r, 4)
        if axis == "x":
            return c, (z * 4 + lax.rem(c, 2) * 2 + core, y * 2 + c // 2)
        if axis == "y":
            return c, (dp, c * 2 + xhi)
        return c, (c * 4 + xlo * 2 + core, cx)

    barrier = greet_ctx()
    for device in [sibling] + [along(axis, r)[1] for axis in "xyz" for r in (1, 2, 3)]:
        pl.semaphore_signal(barrier, inc=1, device_id=device, device_id_type=MESH)

    def put(u, term):
        for n in range(4):
            part = term[:, n * 128 : n * 128 + 128].reshape(32, 16, 128)
            at = pl.ds(u * 64 + (n % 2) * 32, 32)
            acc[n // 2, at] = part
            mine[n // 2, at] = part.astype(BF16)

    def columns(block):
        return w_ref[:, block * WIDTH : (block + 1) * WIDTH]

    def unit_grads(u, block, grad, slope):
        grad_pre = (grad * slope).astype(BF16)
        put(u, dot(normed_t, grad_pre))
        return dot_nt(grad_pre, columns(block))

    def remote(src, dst, send_sem, recv_sem, device):
        copy = pltpu.make_async_remote_copy(
            src_ref=src, dst_ref=dst, send_sem=send_sem, recv_sem=recv_sem,
            device_id=device, device_id_type=MESH,
        )
        copy.start()
        return copy

    running = {}
    lead = (out1, out2, out3)
    landing = (in1, in2, in3)
    sizes = (16, 4, 1)
    base = [u * 64 for u in range(UNITS)]

    def core_start(u):
        at = pl.ds(u * 64, 64)
        running[u] = [
            remote(
                mine.at[1 - core, at], core_in.at[at], core_sems.at[0, u], core_sems.at[1, u], sibling
            )
        ]

    def finish(u):
        for copy in running.pop(u):
            copy.wait()

    def core_finish(u):
        finish(u)
        at = pl.ds(u * 64, 64)
        total = acc[core, at] + core_in[at].astype(F32)
        acc[core, at] = total
        out1[at] = total.astype(BF16)

    def axis_start(u, step):
        size = sizes[step]
        running[u] = []
        for r in (1, 2, 3):
            c, device = along(ORDERS[u][step], r)
            running[u].append(
                remote(
                    lead[step].at[pl.ds((u * 4 + c) * size, size)],
                    landing[step].at[r - 1, pl.ds(u * size, size)],
                    axis_sems.at[0, step, u, r], axis_sems.at[1, step, u, r], device,
                )
            )

    def axis_finish(u, step):
        finish(u)
        size = sizes[step]
        base[u] = base[u] + place[ORDERS[u][step]] * size
        total = acc[core, pl.ds(base[u], size)]
        for r in range(3):
            total = total + landing[step][r, pl.ds(u * size, size)].astype(F32)
        if step == 2:
            held[u] = [place[axis] for axis in ORDERS[u]]
            sum_ref[(core, u, *held[u])] = total.astype(BF16)[0]
        else:
            acc[core, pl.ds(base[u], size)] = total
            lead[step + 1][pl.ds(u * size, size)] = total.astype(BF16)

    held = {}

    def back_start(u, step):
        axis = BACK[u][step]
        part = sum_ref.at[(core, u, *held[u])]
        running[u] = [
            remote(
                part, part, axis_sems.at[2, step, u, r], axis_sems.at[3, step, u, r], along(axis, r)[1]
            )
            for r in (1, 2, 3)
        ]
        held[u][ORDERS[u].index(axis)] = slice(None)

    def core_back(u):
        part = sum_ref.at[core, u]
        running[u] = [remote(part, part, core_sems.at[2, u], core_sems.at[3, u], sibling)]

    def after_core(u):
        core_finish(u)
        axis_start(u, 0)

    def after_axis(u, step):
        axis_finish(u, step)
        if step < 2:
            axis_start(u, step + 1)
        else:
            back_start(u, 0)

    def after_back(u, step):
        finish(u)
        if step < 2:
            back_start(u, step + 1)
        else:
            core_back(u)

    pl.semaphore_wait(barrier, NCTX - 1 + 10)
    g_copies = []
    for n in range(3):
        for rel in range(NCTX):
            peer = (cx + rel) & (NCTX - 1)
            src, dst = g_ref.at[peer, n], g_in.at[cx, n]
            if rel == 0:
                g_copies.append(pltpu.make_async_copy(src, dst, sems.at[n, 0]))
                g_copies[-1].start()
            else:
                g_copies.append(
                    remote(src, dst, sems.at[n, rel], sems.at[n, NCTX + rel], (dp, peer))
                )

    own, cot = own_ref[...].astype(F32), cot_ref[...]
    normed, inverse = normalize(own)
    normed_bf = normed_ref[...]
    normed_t = jnp.transpose(normed_bf)
    put(1, outterm_ref[...])
    core_start(1)
    grad_normed = unit_grads(0, 0, gu_ref[...], silu_grad(dot(normed_bf, columns(0))))
    core_start(0)
    for n in range(3):
        slope[n] = silu_grad(dot(normed_bf, columns(n + 1)))

    def late(n, total):
        for copy in g_copies[n * NCTX : (n + 1) * NCTX]:
            copy.wait()
        grad = gather_heads([g_in[h, n].astype(F32) for h in range(NCTX)])
        total = total + unit_grads(n + 2, n + 1, grad, slope[n])
        core_start(n + 2)
        return total

    after_core(1)
    after_core(0)
    grad_normed = late(0, grad_normed)
    grad_normed = late(1, grad_normed)
    grad_normed = late(2, grad_normed)
    after_core(2)
    after_core(3)
    rowgrad_ref[...] = (
        cot.astype(F32) + normalize_back(grad_normed, normed, inverse)
    ).astype(BF16)
    after_core(4)
    after_axis(1, 0)
    after_axis(0, 0)
    after_axis(2, 0)
    after_axis(3, 0)
    after_axis(4, 0)
    after_axis(1, 1)
    after_axis(0, 1)
    after_axis(2, 1)
    after_axis(3, 1)
    after_axis(4, 1)
    after_axis(1, 2)
    after_axis(0, 2)
    after_axis(2, 2)
    after_axis(3, 2)
    after_axis(4, 2)
    after_back(1, 0)
    after_back(0, 0)
    after_back(2, 0)
    after_back(3, 0)
    after_back(4, 0)
    after_back(1, 1)
    after_back(0, 1)
    after_back(2, 1)
    after_back(3, 1)
    after_back(4, 1)
    after_back(1, 2)
    after_back(0, 2)
    after_back(2, 2)
    after_back(3, 2)
    after_back(4, 2)
    for u in range(UNITS):
        finish(u)


def spread_kernel(scale, sum_ref, layer_ref, rowgrad_ref, proj_hbm, out_hbm, layer_hbm, rowgrad_hbm, wide, sems):
    copies = [
        pltpu.make_async_copy(layer_ref, layer_hbm, sems.at[5]),
        pltpu.make_async_copy(rowgrad_ref, rowgrad_hbm, sems.at[6]),
    ]
    for copy in copies:
        copy.start()
    for u in range(UNITS):
        for n in range(4):
            at = (n % 2) * 2
            wide[u, :, n * 128 : n * 128 + 128] = (
                sum_ref[n // 2, u, at : at + 2].reshape(WIDTH, 128).astype(F32) * scale
            )
        block = (0, None, 1, 2, 3)[u]
        dst = out_hbm if block is None else proj_hbm.at[:, pl.ds(block * WIDTH, WIDTH)]
        copies.append(pltpu.make_async_copy(wide.at[u], dst, sems.at[u]))
        copies[-1].start()
    for copy in copies:
        copy.wait()


HBM = pl.BlockSpec(memory_space=pltpu.HBM)
VM = pl.BlockSpec(memory_space=pltpu.VMEM)
SM = pl.BlockSpec(memory_space=pltpu.SMEM)


def shape(*dims, dtype=BF16):
    return jax.ShapeDtypeStruct(dims, dtype)


def params(vmem_limit_bytes=VMEM_LIMIT, **kw):
    return pltpu.CompilerParams(vmem_limit_bytes=vmem_limit_bytes, **kw)


def in_hbm(array):
    return pltpu.with_memory_space_constraint(array, pltpu.HBM)


def local(loader_rows, send_slot, arrive_slot, user_lengths, proj_weight, out_weight, cotangent):
    own, normed, update, qk, v = pl.pallas_call(
        arrive_kernel,
        name="arrive",
        out_shape=(
            shape(BLK, WIDTH), shape(BLK, WIDTH), shape(BLK, WIDTH),
            shape(16, HALF, 128), shape(NCTX, HALF, 128),
        ),
        in_specs=[HBM] * 4,
        out_specs=(VM,) * 5,
        scratch_shapes=[
            pltpu.VMEM((BLK, WIDTH), BF16),
            pltpu.VMEM((1, BLK), jnp.int32),
            pltpu.VMEM((1, BLK), jnp.int32),
            pltpu.VMEM((WIDTH, 4 * WIDTH), BF16),
            pltpu.VMEM((128, 16, 128), BF16),
            pltpu.VMEM((128, 16, 128), BF16),
            pltpu.VMEM((4, BLK, EVENTS), BF16),
            pltpu.VMEM((NCTX, 2, HALF, 128), BF16),
            pltpu.VMEM((NCTX, HALF, 128), BF16),
            pltpu.SemaphoreType.DMA((2,)),
            pltpu.SemaphoreType.DMA((NCTX, 3)),
            pltpu.SemaphoreType.DMA((NCTX, 3)),
            pltpu.SemaphoreType.DMA((3,)),
            pltpu.SemaphoreType.DMA((4,)),
        ],
        compiler_params=params(collective_id=0, has_side_effects=True),
    )(
        *map(in_hbm, (loader_rows, send_slot.reshape(1, BLK), arrive_slot.reshape(1, BLK), proj_weight))
    )

    layer_out, grad_update, out_term, grad_att = pl.pallas_call(
        forward_kernel,
        name="forward",
        out_shape=(
            shape(BLK, WIDTH), shape(BLK, WIDTH, dtype=F32), shape(WIDTH, WIDTH, dtype=F32),
            shape(NCTX, HALF, 128),
        ),
        in_specs=[SM, VM, VM, VM, VM, HBM, HBM],
        out_specs=(VM,) * 4,
        scratch_shapes=[
            pltpu.VMEM((HD, EVENTS), BF16),
            pltpu.VMEM((EVENTS, HD), BF16),
            pltpu.VMEM((EVENTS, HD), BF16),
            pltpu.VMEM((HD, EVENTS), BF16),
            pltpu.VMEM((NCTX, HALF, 128), BF16),
            pltpu.VMEM((BLK, WIDTH), BF16),
            pltpu.VMEM((WIDTH, WIDTH), BF16),
            pltpu.VMEM((NCTX, HALF, 128), BF16),
            pltpu.VMEM((NCTX, HALF, 128), BF16),
            pltpu.SemaphoreType.DMA((4 * NCTX,)),
            pltpu.SemaphoreType.DMA((2,)),
        ],
        compiler_params=params(collective_id=1, has_side_effects=True),
    )(in_hbm(user_lengths), qk, v, own, update, in_hbm(cotangent), in_hbm(out_weight))

    grads = pl.pallas_call(
        backward_kernel,
        name="attend_back",
        out_shape=shape(NCTX, 3, HALF, 128),
        in_specs=[SM, VM, VM, VM],
        out_specs=VM,
        scratch_shapes=[
            pltpu.VMEM((EVENTS, HD), BF16),
            pltpu.VMEM((HD, EVENTS), BF16),
            pltpu.VMEM((EVENTS, HD), BF16),
            pltpu.VMEM((HD, EVENTS), BF16),
            pltpu.VMEM((EVENTS, HD), BF16),
            pltpu.VMEM((EVENTS, HD), BF16),
            pltpu.VMEM((HD, EVENTS), BF16),
            pltpu.VMEM((HD, EVENTS), F32),
            pltpu.VMEM((EVENTS, HD), F32),
            pltpu.VMEM((EVENTS, HD), F32),
        ],
        compiler_params=params(),
    )(in_hbm(user_lengths), qk, v, grad_att)

    row_grads, sums = pl.pallas_call(
        final_kernel,
        name="final",
        out_shape=(shape(BLK, WIDTH), shape(2, UNITS, 4, 4, 4, 16, 128)),
        in_specs=[VM] * 7,
        out_specs=(VM,) * 2,
        scratch_shapes=[
            pltpu.VMEM((NCTX, 3, HALF, 128), BF16),
            pltpu.VMEM((3, BLK, WIDTH), F32),
            pltpu.VMEM((2, UNITS * 64, 16, 128), F32),
            pltpu.VMEM((2, UNITS * 64, 16, 128), BF16),
            pltpu.VMEM((UNITS * 64, 16, 128), BF16),
            pltpu.VMEM((UNITS * 64, 16, 128), BF16),
            pltpu.VMEM((3, UNITS * 16, 16, 128), BF16),
            pltpu.VMEM((UNITS * 16, 16, 128), BF16),
            pltpu.VMEM((3, UNITS * 4, 16, 128), BF16),
            pltpu.VMEM((UNITS * 4, 16, 128), BF16),
            pltpu.VMEM((3, UNITS, 16, 128), BF16),
            pltpu.SemaphoreType.DMA((3, 2 * NCTX)),
            pltpu.SemaphoreType.DMA((4, UNITS)),
            pltpu.SemaphoreType.DMA((4, 3, UNITS, 4)),
        ],
        compiler_params=params(collective_id=2, has_side_effects=True),
    )(grads, own, normed, proj_weight, cotangent, grad_update, out_term)

    proj_grad, out_grad, layer_out, row_grads = pl.pallas_call(
        functools.partial(spread_kernel, (BLK * 128) ** (-0.5)),
        name="spread",
        out_shape=(
            shape(WIDTH, 4 * WIDTH, dtype=F32), shape(WIDTH, WIDTH, dtype=F32),
            shape(BLK, WIDTH), shape(BLK, WIDTH),
        ),
        in_specs=[VM] * 3,
        out_specs=(HBM,) * 4,
        scratch_shapes=[
            pltpu.VMEM((UNITS, WIDTH, WIDTH), F32),
            pltpu.SemaphoreType.DMA((7,)),
        ],
        compiler_params=params(),
    )(sums, layer_out, row_grads)
    return (layer_out, row_grads, proj_grad, out_grad)


def solution(mesh):
    placed = (
        P(("dp", "ctx"), None),
        P(("dp", "ctx")),
        P(("dp", "ctx")),
        P("dp", None),
        P(),
        P(),
        P(("dp", "ctx"), None),
    )
    return jax.shard_map(
        local,
        mesh=mesh,
        in_specs=placed,
        out_specs=(P(("dp", "ctx"), None), P(("dp", "ctx"), None), P(), P()),
        check_vma=False,
    )
```
